128 devices in a mesh: gx: 4 (over z), gy: 4 (over y), gz: 8 (over x, core).
Axes of the slice: x: 4, y: 4, z: 4, core: 2. Of those that a mesh axis runs over, the one named last changes fastest.
Arguments:
- design: float32 [16, 256, 1024], P('gx', 'gy', 'gz'), may hold values from 0.05 to 1
- support_mask: int32 [16, 256, 1024], P('gx', 'gy', 'gz'), may hold values 0 or 1
- load_mask: int32 [16, 256, 1024], P('gx', 'gy', 'gz'), may hold values 0 or 1
- solid_mask: int32 [16, 256, 1024], P('gx', 'gy', 'gz'), may hold values 0 or 1
- void_mask: int32 [16, 256, 1024], P('gx', 'gy', 'gz'), may hold values 0 or 1
- loads: float32 [3, 16, 256, 1024], P(None, 'gx', 'gy', 'gz'), may hold values from -0.3 to 0.3
- start_displacement: float32 [3, 16, 256, 1024], P(None, 'gx', 'gy', 'gz'), may hold values from -6 to 6
Outputs:
- displacement: float32 [3, 16, 256, 1024], P(None, 'gx', 'gy', 'gz')
- design_sensitivity: float32 [16, 256, 1024], P('gx', 'gy', 'gz')
- compliance: float32 [], replicated
The draws below stay inside these ranges and needn't reach their ends.
Inputs may be any that keep to these rules, and one draw needn't show every extreme that they name: `void_mask`: 0 or 1; where both passive masks are 1 the voxel is solid.
All inputs are finite; a program needn't handle non-finite values. No bound on the sum of `support_mask` or of `load_mask` or of `solid_mask` or of `void_mask` on one device may be relied on, other than what follows from the above.
Results may differ from the reference program's by a relative error of at most 0.0003.
Values sent between devices are 32-bit elements; how exact they have to be, the bound alone decides.
A program may use at most 128 MiB of HBM per device.

```python
import math
import jax
import jax.numpy as jnp
import numpy as np
from jax import lax

ITERS = 3
NX = 16
NY = 256
NZ = 1024


def place_ends(result, own_key, low, high):
    longest = result.shape.index(max(result.shape))
    spots = []
    for shift in (0, 1):
        where = [jax.random.randint(jax.random.fold_in(own_key, axis), (), 0, length) for axis, length in enumerate(result.shape)]
        where[longest] = (where[longest] + shift) % result.shape[longest]
        spots.append(tuple(where))
    return result.at[spots[0]].set(low).at[spots[1]].set(high)


def shard_levels(stream_key, shape, split, low, high):
    def one(axis_at, blocks):
        steps = jax.random.uniform(jax.random.fold_in(jax.random.fold_in(stream_key, 6), axis_at), (blocks,), jnp.float32, low / len(split), high / len(split))
        return jnp.repeat(jnp.exp(steps), shape[axis_at] // blocks).reshape((-1,) + (1,) * (len(shape) - axis_at - 1))

    loudness = one(*split[0])
    for cut in split[1:]:
        loudness = loudness * one(*cut)
    return loudness


def gaussian(own_key, dims, width, bound, shards=(), kind=jnp.bfloat16):
    values = jax.random.normal(own_key, dims, jnp.float32) * width
    if len(shards) > 0:
        values = shard_levels(own_key, dims, shards, -0.22, 0.18) * values
    return jnp.clip(values, min=-bound, max=bound).astype(kind)


def setup_inputs(seed: int = 0) -> dict:
    splits = jax.random.split(jax.random.key(seed), 8)
    design = jnp.clip(0.05 + 0.95 * jax.random.uniform(splits[0], (NX, NY, NZ), jnp.float32) ** shard_levels(splits[0], (NX, NY, NZ), ((0, 4), (1, 4), (2, 8)), -0.2, 0.2), 0.05, 1.0)
    support_mask = place_ends((jax.random.randint(splits[1], (NX, NY, NZ), 0, 32) < 1).astype(jnp.int32), jax.random.fold_in(splits[1], 1), 0, 1)
    load_mask = place_ends((jax.random.randint(splits[2], (NX, NY, NZ), 0, 8) < 1).astype(jnp.int32), jax.random.fold_in(splits[2], 1), 0, 1)
    solid_mask = place_ends((jax.random.randint(splits[3], (NX, NY, NZ), 0, 32) < 1).astype(jnp.int32), jax.random.fold_in(splits[3], 1), 0, 1)
    void_mask = place_ends((jax.random.randint(splits[4], (NX, NY, NZ), 0, 32) < 1).astype(jnp.int32), jax.random.fold_in(splits[4], 1), 0, 1)
    loads = gaussian(splits[5], (3, NX, NY, NZ), 0.05, 0.3, ((1, 4), (2, 4), (3, 8)), jnp.float32)
    start_displacement = gaussian(splits[6], (3, NX, NY, NZ), 1.0, 6.0, ((1, 4), (2, 4), (3, 8)), jnp.float32)
    return dict(design=design, support_mask=support_mask, load_mask=load_mask, solid_mask=solid_mask, void_mask=void_mask, loads=loads, start_displacement=start_displacement)


EMIN = 0.001
PENALTY = 3.0

def corner_list():
    return [(corner // 4, corner // 2 % 2, corner % 2) for corner in range(8)]

def unit_stiffness():
    poisson = 0.3
    lame_first = poisson / ((1.0 + poisson) * (1.0 - 2.0 * poisson))
    shear_mod = 0.5 / (1.0 + poisson)
    elastic = np.zeros((6, 6))
    elastic[:3, :3] = lame_first
    for axis_num in range(3):
        elastic[axis_num, axis_num] += 2.0 * shear_mod
        elastic[axis_num + 3, axis_num + 3] = shear_mod
    gauss_points = [0.5 - 0.5 / math.sqrt(3.0), 0.5 + 0.5 / math.sqrt(3.0)]
    matrix = np.zeros((24, 24))
    for point_x in gauss_points:
        for point_y in gauss_points:
            for point_z in gauss_points:
                strain = np.zeros((6, 24))
                for corner, (side_x, side_y, side_z) in enumerate(corner_list()):
                    factor_x = point_x if side_x else 1.0 - point_x
                    factor_y = point_y if side_y else 1.0 - point_y
                    factor_z = point_z if side_z else 1.0 - point_z
                    slope_x = 1.0 if side_x else -1.0
                    slope_y = 1.0 if side_y else -1.0
                    slope_z = 1.0 if side_z else -1.0
                    grad_x = slope_x * factor_y * factor_z
                    grad_y = factor_x * slope_y * factor_z
                    grad_z = factor_x * factor_y * slope_z
                    column = 3 * corner
                    strain[0, column] = grad_x
                    strain[1, column + 1] = grad_y
                    strain[2, column + 2] = grad_z
                    strain[3, column] = grad_y
                    strain[3, column + 1] = grad_x
                    strain[4, column + 1] = grad_z
                    strain[4, column + 2] = grad_y
                    strain[5, column] = grad_z
                    strain[5, column + 2] = grad_x
                matrix = matrix + strain.T @ elastic @ strain / 8.0
    return jnp.asarray(matrix, dtype=jnp.float32)

def filter_stencil(padded, size_x, size_y, size_z):
    total = jnp.zeros((size_x, size_y, size_z), jnp.float32)
    for offset_x in range(5):
        for offset_y in range(5):
            for offset_z in range(5):
                distance = math.sqrt((offset_x - 2) ** 2 + (offset_y - 2) ** 2 + (offset_z - 2) ** 2)
                if distance < 3.0:
                    total = total + (3.0 - distance) * padded[offset_x:offset_x + size_x, offset_y:offset_y + size_y, offset_z:offset_z + size_z]
    return total

def gather_corners(padded, first_node, size_x, size_y, size_z):
    return jnp.concatenate([padded[:, first_node + side_x:first_node + side_x + size_x, first_node + side_y:first_node + side_y + size_y, first_node + side_z:first_node + side_z + size_z] for side_x, side_y, side_z in corner_list()], axis=0)

def element_forces(vectors, stiffness, modulus):
    flat = jnp.dot(stiffness, vectors.reshape(24, -1), precision=lax.Precision.HIGHEST)
    return flat.reshape(vectors.shape) * modulus[None]

def element_energy(vectors, stiffness):
    flat = jnp.dot(stiffness, vectors.reshape(24, -1), precision=lax.Precision.HIGHEST)
    return lax.optimization_barrier(jnp.sum(vectors * flat.reshape(vectors.shape), axis=0))

def node_apply(padded, padded_modulus, stiffness, size_x, size_y, size_z):
    vectors = gather_corners(padded, 0, size_x + 1, size_y + 1, size_z + 1)
    forces = element_forces(vectors, stiffness, padded_modulus[:size_x + 1, :size_y + 1, :size_z + 1])
    total = jnp.zeros((3, size_x, size_y, size_z), jnp.float32)
    for position, (side_x, side_y, side_z) in enumerate(corner_list()):
        total = total + forces[3 * position:3 * position + 3, 1 - side_x:1 - side_x + size_x, 1 - side_y:1 - side_y + size_y, 1 - side_z:1 - side_z + size_z]
    return total

def node_diagonal(padded_modulus, stiffness, size_x, size_y, size_z):
    diagonal = jnp.diagonal(stiffness)
    total = jnp.zeros((3, size_x, size_y, size_z), jnp.float32)
    for position, (side_x, side_y, side_z) in enumerate(corner_list()):
        total = total + diagonal[3 * position:3 * position + 3][:, None, None, None] * padded_modulus[None, 1 - side_x:1 - side_x + size_x, 1 - side_y:1 - side_y + size_y, 1 - side_z:1 - side_z + size_z]
    return total

def pad_nodes(field):
    return jnp.pad(field, ((0, 0), (1, 1), (1, 1), (1, 1)))

def blocked_apply(padded, padded_modulus, stiffness, size_x, size_y, size_z):
    block_size = math.gcd(size_x, 8)
    pieces = []
    for first_row in range(0, size_x, block_size):
        pieces.append(node_apply(padded[:, first_row:first_row + block_size + 2], padded_modulus[first_row:first_row + block_size + 2], stiffness, block_size, size_y, size_z))
    return jnp.concatenate(pieces, axis=1)

def blocked_energy(padded, stiffness, size_x, size_y, size_z):
    block_size = math.gcd(size_x, 8)
    pieces = []
    for first_row in range(0, size_x, block_size):
        vectors = gather_corners(padded[:, first_row:first_row + block_size + 2], 1, block_size, size_y, size_z)
        pieces.append(element_energy(vectors, stiffness))
    return jnp.concatenate(pieces, axis=0)

def reference(design, support_mask, load_mask, solid_mask, void_mask, loads, start_displacement):
    size_x, size_y, size_z = design.shape
    stiffness = unit_stiffness()
    weight_total = filter_stencil(jnp.pad(jnp.ones_like(design), 2), size_x, size_y, size_z)
    filtered = filter_stencil(jnp.pad(design, 2), size_x, size_y, size_z) / weight_total
    physical = jnp.where(solid_mask > 0, jnp.float32(1.0), jnp.where(void_mask > 0, jnp.float32(0.0), filtered))
    modulus = EMIN + (1.0 - EMIN) * physical * physical * physical
    padded_modulus = jnp.pad(modulus, 1)
    free_dofs = (1 - support_mask).astype(jnp.float32)[None]
    force = free_dofs * load_mask.astype(jnp.float32)[None] * loads
    inverse_diag = free_dofs / node_diagonal(padded_modulus, stiffness, size_x, size_y, size_z)

    def operator(field):
        return free_dofs * blocked_apply(pad_nodes(field), padded_modulus, stiffness, size_x, size_y, size_z)
    displacement = free_dofs * start_displacement
    residual = force - operator(displacement)
    precond = inverse_diag * residual
    direction = precond
    precond_norm = jnp.sum(residual * precond)
    for iteration in range(ITERS):
        image = operator(direction)
        step_length = precond_norm / jnp.sum(direction * image)
        displacement = displacement + step_length * direction
        residual = residual - step_length * image
        precond = inverse_diag * residual
        norm_next = jnp.sum(residual * precond)
        direction = precond + norm_next / precond_norm * direction
        precond_norm = norm_next
    energy = blocked_energy(pad_nodes(displacement), stiffness, size_x, size_y, size_z)
    compliance = jnp.sum(modulus * energy)
    passive = (solid_mask > 0) | (void_mask > 0)
    sensitivity = jnp.where(passive, jnp.float32(0.0), -PENALTY * (1.0 - EMIN) * physical * physical * energy)
    design_sensitivity = filter_stencil(jnp.pad(sensitivity / weight_total, 2), size_x, size_y, size_z)
    return (displacement, design_sensitivity, compliance)
```

```python
import functools
import math

import jax
import jax.numpy as jnp
from jax import lax
from jax.experimental import pallas as pl
from jax.experimental.pallas import tpu as pltpu
from jax.sharding import PartitionSpec as P

MESH = pl.DeviceIdType.MESH
AXES = ("gx", "gy", "gz")

EMIN = 0.001
PENALTY = 3.0
THETA = 1.5
MU16 = 1.0 / (2.6 * 16.0)
DIAG = 88.0 / 9.0

BX, BY, BZ = 4, 64, 128
GROUP = 12
XE = 2
NE = 8

f32 = jnp.float32


def iota(dim):
    return lax.broadcasted_iota(jnp.int32, (8, 128), dim)


def lane_pos():
    lane = iota(1)
    return lane - GROUP * ((lane * 43) >> 9)


def rot(value, shift, axis=1):
    size = value.shape[axis]
    return pltpu.roll(value, shift % size, axis)


def yz_modes(a, b, next_z):
    low, high = a + b, b - a
    low_next, high_next = next_z(low), next_z(high)
    return (low + low_next, low_next - low, high + high_next, high_next - high)


def x_modes(near, far):
    return [
        [None if m == 0 else n[m] + f[m] for m in range(4)] + [f[m] - n[m] for m in range(4)]
        for n, f in zip(near, far)
    ]


def mode_forces(q, g):
    u, v, w = q
    force = [[None] * 8 for _ in range(3)]
    trace = 1.5 * (u[4] + v[2] + w[1])
    force[0][4] = g * (trace + (u[4] + u[4]))
    force[1][2] = g * (trace + (v[2] + v[2]))
    force[2][1] = g * (trace + (w[1] + w[1]))
    for (ca, ma), (cb, mb) in (((0, 2), (1, 4)), ((1, 1), (2, 2)), ((0, 1), (2, 4))):
        shear = g * (q[ca][ma] + q[cb][mb])
        force[ca][ma] = shear
        force[cb][mb] = shear
    for (ca, ma), (cb, mb) in (((1, 6), (2, 5)), ((0, 6), (2, 3)), ((0, 5), (1, 3))):
        half = 0.5 * (q[ca][ma] + q[cb][mb])
        force[ca][ma] = g * (q[ca][ma] + half)
        force[cb][mb] = g * (q[cb][mb] + half)
    third = g * (1.0 / 3.0)
    total = u[3] + v[5] + w[6]
    force[0][3] = third * (u[3] + total)
    force[1][5] = third * (v[5] + total)
    force[2][6] = third * (w[6] + total)
    last = g * (5.5 / 9.0)
    for c in range(3):
        force[c][7] = last * q[c][7]
    return force


def mode_energy(q):
    u, v, w = q
    trace = u[4] + v[2] + w[1]
    total = 1.5 * (trace * trace) + 2.0 * (u[4] * u[4] + v[2] * v[2] + w[1] * w[1])
    for (ca, ma), (cb, mb) in (((0, 2), (1, 4)), ((1, 1), (2, 2)), ((0, 1), (2, 4))):
        shear = q[ca][ma] + q[cb][mb]
        total = total + shear * shear
    for (ca, ma), (cb, mb) in (((1, 6), (2, 5)), ((0, 6), (2, 3)), ((0, 5), (1, 3))):
        both = q[ca][ma] + q[cb][mb]
        total = total + (q[ca][ma] * q[ca][ma] + q[cb][mb] * q[cb][mb] + 0.5 * (both * both))
    both = u[3] + v[5] + w[6]
    total = total + (1.0 / 3.0) * (u[3] * u[3] + v[5] * v[5] + w[6] * w[6] + both * both)
    last = u[7] * u[7] + v[7] * v[7] + w[7] * w[7]
    return total + (5.5 / 9.0) * last


def node_planes(planes, moduli):
    before, kept = None, None
    for index, plane in enumerate(planes):
        if before is not None:
            force = mode_forces(x_modes(before, plane), moduli(index - 1))
            right = [
                [-f[4] if m == 0 else f[m] - f[4 + m] for m in range(4)] for f in force
            ]
            left = [[f[4] if m == 0 else f[m] + f[4 + m] for m in range(4)] for f in force]
            if kept is not None:
                yield index - 1, [[k + r for k, r in zip(ks, rs)] for ks, rs in zip(kept, right)]
            kept = left
        before = plane


def node_values(modes, shift_y, shift_z):
    ss, sd, ds, dd = modes
    low = (ss - ds) + shift_y(ss + ds, 0)
    high = (sd - dd) + shift_y(sd + dd, 1)
    return (low - high) + shift_z(low + high)


def body(
    sizes,
    design_in, support_in, load_in, solid_in, void_in, loads_in, start_in,
    disp_out, dsens_out, comp_out,
    dm, um, vm0, vm1, vm2, gm, sn, sup, lom, sol, voi, loads, res, inv, iw, co, s1, s2, dis, des,
    pa, pz, ko, kr, ed, qd, fx, fxd, cy, ar, ar_msg,
    in_sem, out_sem, ssem, rsem, ar_ssem, ar_rsem,
):
    nx, ny, nz = sizes
    count = nx * ny * nz
    me = [lax.axis_index(a) for a in AXES]
    linear = (me[0] * ny + me[1]) * nz + me[2]
    lane, row, pos = iota(1), iota(0), lane_pos()
    own_rows = pl.ds(8, BY)
    zero = jnp.zeros((8, 128), f32)

    copies = [
        pltpu.make_async_copy(src, dst, in_sem.at[i])
        for i, (src, dst) in enumerate(
            (
                (start_in, um.at[:, pl.ds(1, BX), own_rows]),
                (support_in, sup),
                (design_in, dm.at[0, pl.ds(2, BX), own_rows]),
                (solid_in, sol),
                (void_in, voi),
                (load_in, lom),
                (loads_in, loads),
            )
        )
    ]
    for copy in copies:
        copy.start()

    def clear_main(ref, xo, slots):
        comps = ref.shape[0]
        for c in range(comps):
            for s in range(slots):
                own = xo <= s < xo + BX
                for t in (0, 9) if own else range(10):
                    ref[c, s, 8 * t : 8 * t + 8] = zero

    def clear_edges(i, carry):
        for dz in range(2):
            for c in range(4):
                for s in range(NE):
                    pz[i, dz, c, s] = zero
        for a in range(3):
            for b in range(2):
                for d in range(2):
                    kr[i, a, b, d] = zero
        return carry

    clear_main(dm, 2, 8)
    clear_main(um, 1, 7)
    clear_edges(0, 0)

    barrier = pltpu.get_barrier_semaphore()

    def place(other):
        return (other // (ny * nz), (other // nz) % ny, other % nz)

    def greet(i, carry):
        pl.semaphore_signal(
            barrier, inc=1, device_id=place(lax.rem(linear + i, count)), device_id_type=MESH
        )
        return carry

    lax.fori_loop(1, count, greet, 0)

    clear_main(sn, 2, 8)
    clear_main(gm, 1, 6)
    for ref in (vm0, vm1, vm2):
        clear_main(ref, 1, 7)
    lax.fori_loop(1, pz.shape[0], clear_edges, 0)

    def group_mask(t, first, last):
        return (lane >= GROUP * (t + 1) + first) & (lane < GROUP * (t + 1) + last)

    def pack_tiles(tiles, base):
        for t, tile in tiles:
            base = jnp.where(group_mask(t, 0, 6), rot(tile, GROUP * (t + 1) + 3), base)
        return base

    def pack(k, fields):
        comp = 0
        total = sum(ref.shape[0] for ref, _ in fields)
        corner = [zero, zero]
        for ref, xo in fields:
            for c in range(ref.shape[0]):
                for x in range(BX):
                    packed = pack_tiles(
                        [(t, ref[c, x + xo, 8 * t + 8 : 8 * t + 16]) for t in range(8)], zero
                    )
                    pa[k, comp, x + XE] = packed
                    i = 6 * (x * total + comp)
                    for side, t in ((0, 0), (1, 7)):
                        corner[side] = jnp.where(
                            (lane >= i) & (lane < i + 6),
                            rot(packed, i - GROUP * (t + 1)),
                            corner[side],
                        )
                comp += 1
        for side in range(2):
            ko[k, side] = corner[side]

    def messages(k, fields):
        comps = sum(f[0].shape[0] for f in fields)
        low, high = max(f[2] for f in fields), max(f[3] for f in fields)
        out = []
        for dx in (0, 1, -1):
            for dy in (0, 1, -1):
                for dz in (0, 1, -1):
                    d = (dx, dy, dz)
                    if d == (0, 0, 0) or (1 in d and low == 0) or (-1 in d and high == 0):
                        continue
                    parts = []
                    if dz == 0:
                        for ref, xo, lo, hi in fields:
                            if dx == 1:
                                xs, xd = pl.ds(xo + BX - lo, lo), pl.ds(xo - lo, lo)
                            elif dx == -1:
                                xs, xd = pl.ds(xo, hi), pl.ds(xo + BX, hi)
                            else:
                                xs = xd = pl.ds(xo, BX)
                            if dy == 1:
                                ys, yd = pl.ds(BY, 8), pl.ds(0, 8)
                            elif dy == -1:
                                ys, yd = pl.ds(8, 8), pl.ds(BY + 8, 8)
                            else:
                                ys = yd = own_rows
                            parts.append((ref.at[:, xs, ys], ref.at[:, xd, yd]))
                    elif dy == 0:
                        if dx == 1:
                            xs, xd = pl.ds(XE + BX - low, low), pl.ds(XE - low, low)
                        elif dx == -1:
                            xs, xd = pl.ds(XE, high), pl.ds(XE + BX, high)
                        else:
                            xs = xd = pl.ds(XE, BX)
                        side = 0 if dz == 1 else 1
                        cs = pl.ds(0, comps)
                        parts.append((pa.at[k, cs, xs], pz.at[k, side, cs, xd]))
                    else:
                        parts.append(
                            (
                                ko.at[k, 0 if dy == -1 else 1],
                                kr.at[k, 1 - dx, 0 if dy == 1 else 1, 0 if dz == 1 else 1],
                            )
                        )
                    out.append((d, parts))
        result, slot = [], 0
        for d, parts in out:
            group = []
            for src, dst in parts:
                group.append(
                    pltpu.make_async_remote_copy(
                        src_ref=src,
                        dst_ref=dst,
                        send_sem=ssem.at[k, slot],
                        recv_sem=rsem.at[k, slot],
                        device_id=tuple(m + step for m, step in zip(me, d)),
                        device_id_type=MESH,
                    )
                )
                slot += 1
            result.append((d, group))
        return result

    def exists(d, sign):
        ok = None
        for m, step, size in zip(me, d, sizes):
            if step * sign == 1:
                here = m < size - 1
            elif step * sign == -1:
                here = m > 0
            else:
                continue
            ok = here if ok is None else ok & here
        return ok

    def send(msgs):
        for d, group in msgs:
            @pl.when(exists(d, 1))
            def _(group=group):
                for copy in group:
                    copy.start()

    def receive(msgs):
        for d, group in msgs:
            @pl.when(exists(d, -1))
            def _(group=group):
                for copy in group:
                    copy.wait_recv()

    def sent(msgs):
        for d, group in msgs:
            @pl.when(exists(d, 1))
            def _(group=group):
                for copy in group:
                    copy.wait_send()

    def assemble(k, ref, xo, first_comp, comps, planes, edge=None, halo=None):
        for c in range(ref.shape[0]):
            comp = first_comp + c
            for x in planes:
                source = x % BX
                side_x = 0 if x < 0 else 2 if x >= BX else 1
                i = 6 * (source * comps + comp)
                ends = []
                for side in range(2):
                    value = pz[k, side, comp, x + XE]
                    value = jnp.where(lane < 6, rot(kr[k, side_x, 0, side], -i), value)
                    value = jnp.where(
                        group_mask(8, 0, 6), rot(kr[k, side_x, 1, side], 9 * GROUP - i), value
                    )
                    ends.append(value)
                left, right = ends
                if halo is not None:
                    halo[c, x + XE] = jnp.where(pos < 3, left, right)
                if edge is not None:
                    if side_x == 1:
                        own = pack_tiles(
                            [(t, ref[c, x + xo, 8 * t + 8 : 8 * t + 16]) for t in (-1, 8)],
                            pa[k, comp, x + XE],
                        )
                    else:
                        own = pack_tiles(
                            [(t, ref[c, x + xo, 8 * t + 8 : 8 * t + 16]) for t in range(-1, 9)],
                            zero,
                        )
                    low = jnp.where(pos < 3, own, right)
                    high = jnp.where(pos < 3, left, own)
                    edge[c, x + XE] = jnp.where(pos < 6, low, rot(high, 6))

    def next_z(value):
        return rot(value, -1)

    def last_z(value):
        return rot(value, 1)

    def main_plane(ref, s, t):
        start = 8 * t + 8
        return [
            yz_modes(
                ref[c, s, pl.ds(pl.multiple_of(start, 8), 8)], ref[c, s, pl.ds(start + 1, 8)], next_z
            )
            for c in range(3)
        ]

    def edge_plane(edge, x):
        out = []
        for c in range(3):
            a = edge[c, x + XE]
            b = rot(jnp.where(row == 0, rot(a, -GROUP), a), -1, 0)
            out.append(yz_modes(a, b, next_z))
        return out

    def edge_down(value, _):
        down = rot(value, 1, 0)
        return jnp.where(row == 0, rot(down, GROUP), down)

    def tile(t):
        return pl.ds(pl.multiple_of(8 * t + 8, 8), 8)

    def brick(t):
        return pl.ds(pl.multiple_of(8 * t, 8), 8)

    outer = (lane == 0) | (lane == 127)

    def apply(ref, edge, planes, use):
        nodes = [planes[0] - 1, *planes, planes[-1] + 1]
        for index, modes in node_planes(
            (edge_plane(edge, x) for x in nodes), lambda e: ed[4, 0, nodes[e] + XE]
        ):
            x = nodes[index]
            for c in range(3):
                value = node_values(modes[c], edge_down, last_z)
                fx[c, x + XE] = jnp.where(pos == 3, rot(value, -6), value)

        def one(t, first):
            for index, modes in node_planes(
                (main_plane(ref, x + 1, t) for x in nodes),
                lambda e: gm[0, nodes[e] + 1, tile(t)],
            ):
                x = nodes[index]
                for c in range(3):
                    def shift_y(value, which):
                        down = rot(value, 1, 0)
                        before = None if first else cy[c, x + 1, which]
                        cy[c, x + 1, which] = down
                        return down if first else jnp.where(row == 0, before, down)

                    if first:
                        ss, sd, ds, dd = modes[c]
                        shift_y(ss + ds, 0)
                        shift_y(sd + dd, 1)
                    else:
                        value = node_values(modes[c], shift_y, last_z)
                        fixed = rot(fx[c, x + XE], lax.rem(254 - GROUP * (t + 1) - 1, 128))
                        use(x, c, t, jnp.where(outer, fixed, value))

        one(-1, True)
        lax.fori_loop(0, 8, lambda t, carry: (one(t, False), carry)[1], 0)

    weights = {}
    for a in range(3):
        for b in range(3):
            for c in range(3):
                weights[a, b, c] = max(0.0, 3.0 - math.sqrt(a * a + b * b + c * c))

    def filter_z(ref, halo):
        for s in range(8):
            def step(t, carry):
                here = ref[0, s, brick(t)]
                side = rot(halo[0, s], lax.rem(256 - GROUP * t - 3, 128))
                one = rot(jnp.where(lane < 1, side, here), -1) + rot(
                    jnp.where(lane >= 127, side, here), 1
                )
                two = rot(jnp.where(lane < 2, side, here), -2) + rot(
                    jnp.where(lane >= 126, side, here), 2
                )
                s1[s, brick(t)] = one
                s2[s, brick(t)] = two
                return carry

            lax.fori_loop(0, 10, step, 0)

    def filter_xy(ref, use):
        def step(t, carry):
            total = [None] * BX
            for s in range(8):
                def rows(source, off):
                    return source[pl.ds(8 * t + 8 + off, 8)]

                parts = []
                for source in (ref.at[0, s], s1.at[s], s2.at[s]):
                    parts.append(
                        [
                            rows(source, 0),
                            rows(source, 1) + rows(source, -1),
                            rows(source, 2) + rows(source, -2),
                        ]
                    )
                pair = {
                    (0, 0): parts[0][0],
                    (0, 1): parts[0][1] + parts[1][0],
                    (1, 1): parts[1][1],
                    (0, 2): parts[0][2] + parts[2][0],
                    (1, 2): parts[1][2] + parts[2][1],
                    (2, 2): parts[2][2],
                }
                sums = {}
                for x in range(BX):
                    away = abs(x + 2 - s)
                    if away > 2:
                        continue
                    if away not in sums:
                        value = None
                        for (b, c), term in pair.items():
                            if weights[away, b, c] > 0.0:
                                term = weights[away, b, c] * term
                                value = term if value is None else value + term
                        sums[away] = value
                    total[x] = sums[away] if total[x] is None else total[x] + sums[away]
            for x in range(BX):
                use(x, t, total[x])
            return carry

        lax.fori_loop(0, 8, step, 0)

    def reduce_start(k, value):
        ar_msg[k] = value
        ar[k, linear] = value

        def one(i, carry):
            pltpu.make_async_remote_copy(
                src_ref=ar_msg.at[k],
                dst_ref=ar.at[k, linear],
                send_sem=ar_ssem.at[k],
                recv_sem=ar_rsem.at[k],
                device_id=place(lax.rem(linear + i, count)),
                device_id_type=MESH,
            ).start()
            return carry

        lax.fori_loop(1, count, one, 0)

    def reduce_wait(k, sem):
        part = ar.at[k, pl.ds(0, count - 1)]
        pltpu.make_async_copy(part, part, sem.at[k]).wait()

    def reduce_total(k):
        reduce_wait(k, ar_rsem)
        return jnp.sum(ar[k], axis=0)


    copies[0].wait()
    copies[1].wait()
    for c in range(3):
        um[c, 1 : 1 + BX, 8 : 8 + BY] = um[c, 1 : 1 + BX, 8 : 8 + BY] * (1 - sup[...]).astype(f32)
    copies[2].wait()
    first_fields = [(um, 1), (dm, 2)]
    pack(0, first_fields)
    pl.semaphore_wait(barrier, count - 1)
    first = messages(0, [(um, 1, 1, 1), (dm, 2, 2, 2)])
    send(first)

    def inside(coord, size):
        return ((coord >= 0) & (coord < size)).astype(f32)

    z_at = me[2] * BZ + lane
    z_terms = [
        jnp.ones((8, 128), f32),
        inside(z_at - 1, nz * BZ) + inside(z_at + 1, nz * BZ),
        inside(z_at - 2, nz * BZ) + inside(z_at + 2, nz * BZ),
    ]
    x_rows = []
    for x in range(BX):
        x_at = me[0] * BX + x
        x_terms = [
            f32(1.0),
            inside(x_at - 1, nx * BX) + inside(x_at + 1, nx * BX),
            inside(x_at - 2, nx * BX) + inside(x_at + 2, nx * BX),
        ]
        per_b = []
        for b in range(3):
            value = zero
            for c in range(3):
                value = value + z_terms[c] * sum(x_terms[a] * weights[a, b, c] for a in range(3))
            per_b.append(value)
        x_rows.append(per_b)

    def weigh(t, carry):
        y_at = me[1] * BY + 8 * t + row
        one = inside(y_at - 1, ny * BY) + inside(y_at + 1, ny * BY)
        two = inside(y_at - 2, ny * BY) + inside(y_at + 2, ny * BY)
        for x in range(BX):
            iw[x, brick(t)] = 1.0 / (x_rows[x][0] + one * x_rows[x][1] + two * x_rows[x][2])
        return carry

    lax.fori_loop(0, 8, weigh, 0)
    for copy in copies[3:]:
        copy.wait()

    receive(first)
    assemble(0, dm, 2, 3, 4, range(-2, 6), halo=qd)
    assemble(0, um, 1, 0, 4, range(-1, 5), edge=ed.at[0])

    filter_z(dm, qd)

    def to_modulus(x, t, total):
        at = brick(t)
        scale = iw[x, at]
        solid, void = sol[x, at] > 0, voi[x, at] > 0
        physical = jnp.where(solid, 1.0, jnp.where(void, 0.0, total * scale))
        square = physical * physical
        gm[0, 1 + x, tile(t)] = MU16 * EMIN + (MU16 * (1.0 - EMIN)) * (square * physical)
        co[x, at] = jnp.where(
            solid | void, 0.0, (-PENALTY * (1.0 - EMIN) * MU16) * (square * scale)
        )

    filter_xy(dm, to_modulus)
    pack(1, [(gm, 1)])
    second = messages(1, [(gm, 1, 1, 0)])
    send(second)
    receive(second)
    assemble(1, gm, 1, 0, 1, range(-1, 4), edge=ed.at[4])

    for x in range(BX):
        value = ed[4, 0, x + XE] + ed[4, 0, x + XE - 1]
        value = value + edge_down(value, 0)
        fxd[x] = value + last_z(value)

    def diagonal(t, carry):
        for x in range(BX):
            value = None
            for s in (x, x + 1):
                term = gm[0, s, tile(t)] + gm[0, s, pl.ds(8 * t + 7, 8)]
                value = term if value is None else value + term
            value = value + last_z(value)
            fixed = rot(fxd[x], lax.rem(256 - GROUP * (t + 1) - 9, 128))
            value = jnp.where(lane == 0, fixed, value)
            free = (1 - sup[x, brick(t)]).astype(f32)
            inv[x, brick(t)] = free / (DIAG * value)
        return carry

    lax.fori_loop(0, 8, diagonal, 0)

    sums = {}
    acc_names = ("b0", "a00", "a01", "a11", "a12", "a22", "energy")
    for n, name in enumerate(acc_names):
        s1[n, 0:8] = zero
        sums[name] = s1.at[n, pl.ds(0, 8)]

    def add(name, value):
        sums[name][...] = sums[name][...] + value

    def from_start(x, c, t, image):
        at = brick(t)
        free = (1 - sup[x, at]).astype(f32)
        load = lom[x, at].astype(f32)
        left = free * (load * loads[c, x, at] - image)
        value = inv[x, at] * left
        vm0[c, 1 + x, tile(t)] = value
        add("b0", left * value)

    def from_vector(source, target, diag_name, next_name):
        def use(x, c, t, image):
            here = source[c, 1 + x, tile(t)]
            value = inv[x, brick(t)] * image - THETA * here
            target[c, 1 + x, tile(t)] = value
            add(diag_name, here * image)
            add(next_name, value * image)

        return use

    own = list(range(BX))
    apply(um, ed.at[0], own, from_start)
    pack(2, [(vm0, 1)])
    third = messages(2, [(vm0, 1, 1, 1)])
    send(third)
    receive(third)
    assemble(2, vm0, 1, 0, 3, range(-1, 5), edge=ed.at[1])
    apply(vm0, ed.at[1], own, from_vector(vm0, vm1, "a00", "a01"))
    pack(3, [(vm1, 1)])
    fourth = messages(3, [(vm1, 1, 1, 1)])
    send(fourth)
    receive(fourth)
    assemble(3, vm1, 1, 0, 3, range(-1, 5), edge=ed.at[2])
    apply(vm1, ed.at[2], own, from_vector(vm1, vm2, "a11", "a12"))
    pack(4, [(vm2, 1)])
    fifth = messages(4, [(vm2, 1, 0, 1)])
    send(fifth)
    receive(fifth)
    assemble(4, vm2, 1, 0, 3, range(0, 5), edge=ed.at[3])

    def energies(planes):
        before = None
        for index, plane in enumerate(planes):
            if before is not None:
                yield index - 1, mode_energy(x_modes(before, plane))
            before = plane

    column = (pos == 2) & (lane >= GROUP) & (lane < 9 * GROUP)

    edge_sum = zero
    for x, value in energies(edge_plane(ed.at[3], x) for x in range(BX + 1)):
        edge_sum = edge_sum + jnp.where(column, ed[4, 0, x + XE] * value, 0.0)

    def last_moment(t, carry):
        total = zero
        for x, value in energies(main_plane(vm2, x + 1, t) for x in range(BX + 1)):
            total = total + gm[0, 1 + x, tile(t)] * value
        add("a22", jnp.where(lane < 127, total, 0.0))
        return carry

    add("a22", edge_sum)
    lax.fori_loop(0, 8, last_moment, 0)

    message = jnp.zeros((1, 128), f32)
    lane1 = lax.broadcasted_iota(jnp.int32, (1, 128), 1)
    for n, name in enumerate(acc_names[:6]):
        part = jnp.sum(jnp.sum(sums[name][...], axis=0, keepdims=True), axis=1, keepdims=True)
        message = jnp.where(lane1 == n, part, message)
    reduce_start(0, message)
    for msgs in (first, second, third, fourth, fifth):
        sent(msgs)
    totals = reduce_total(0)
    b0, a00, a01, a11, a12, a22 = (
        jnp.broadcast_to(totals[:, n : n + 1], (1, 128)) for n in range(6)
    )
    tiny = 1e-6
    b1 = a00 - THETA * b0
    b2 = a01 - THETA * b1
    l10, l20 = a01 / a00, a11 / a00
    d1 = a11 - l10 * a01
    ok1 = d1 > tiny * a11
    safe1 = jnp.where(ok1, d1, 1.0)
    cross = a12 - l20 * a01
    l21 = jnp.where(ok1, cross / safe1, 0.0)
    d2 = a22 - l20 * a11 - l21 * cross
    ok2 = ok1 & (d2 > tiny * a22)
    y1 = b1 - l10 * b0
    y2 = b2 - l20 * b0 - l21 * y1
    c2 = jnp.where(ok2, y2 / jnp.where(ok2, d2, 1.0), 0.0)
    c1 = jnp.where(ok1, y1 / safe1, 0.0) - l21 * c2
    c0 = b0 / a00 - l10 * c1 - l20 * c2
    c0, c1, c2 = (jnp.broadcast_to(c, (8, 128)) for c in (c0, c1, c2))

    for c in range(3):
        for x in range(BX + 1):
            s = x + XE
            ed[0, c, s] = ed[0, c, s] + (
                c0 * ed[1, c, s] + c1 * ed[2, c, s] + c2 * ed[3, c, s]
            )

    def combine(t, carry):
        for c in range(3):
            for s in range(1, BX + 2):
                at = brick(t + 1)
                um[c, s, at] = um[c, s, at] + (
                    c0 * vm0[c, s, at] + c1 * vm1[c, s, at] + c2 * vm2[c, s, at]
                )
        return carry

    lax.fori_loop(0, 9, combine, 0)
    disp = pltpu.make_async_copy(um.at[:, pl.ds(1, BX), own_rows], disp_out, out_sem.at[0])
    disp.start()

    for x, value in energies(edge_plane(ed.at[0], x) for x in range(BX + 1)):
        fxd[x] = value

    def sensitivity(t, carry):
        total = zero
        for x, value in energies(main_plane(um, x + 1, t) for x in range(BX + 1)):
            fixed = rot(fxd[x], lax.rem(253 - GROUP * (t + 1), 128))
            value = jnp.where(lane == 127, fixed, value)
            total = total + gm[0, 1 + x, tile(t)] * value
            sn[0, 2 + x, tile(t)] = co[x, brick(t)] * value
        add("energy", total)
        return carry

    lax.fori_loop(0, 8, sensitivity, 0)
    pack(5, [(sn, 2)])
    sixth = messages(5, [(sn, 2, 2, 2)])
    send(sixth)
    part = jnp.sum(jnp.sum(sums["energy"][...], axis=0, keepdims=True), axis=1, keepdims=True)
    reduce_start(1, jnp.broadcast_to(part, (1, 128)))
    receive(sixth)
    assemble(5, sn, 2, 0, 1, range(-2, 6), halo=qd)
    filter_z(sn, qd)

    def finish(x, t, total):
        des[x, brick(t)] = total

    filter_xy(sn, finish)
    out = pltpu.make_async_copy(des, dsens_out, out_sem.at[1])
    out.start()
    comp_out[...] = reduce_total(1)
    sent(sixth)
    for k in range(2):
        reduce_wait(k, ar_ssem)
    disp.wait()
    out.wait()


def call(sizes, *args):
    count = sizes[0] * sizes[1] * sizes[2]
    main3 = pltpu.VMEM((3, 7, 80, 128), f32)
    wide = pltpu.VMEM((1, 8, 80, 128), f32)
    brick = pltpu.VMEM((BX, BY, BZ), f32)
    mask = pltpu.VMEM((BX, BY, BZ), jnp.int32)
    any_spec = pl.BlockSpec(memory_space=pl.ANY)
    displacement, sensitivity, compliance = pl.pallas_call(
        functools.partial(body, sizes),
        out_shape=(
            jax.ShapeDtypeStruct((3, BX, BY, BZ), f32),
            jax.ShapeDtypeStruct((BX, BY, BZ), f32),
            jax.ShapeDtypeStruct((1, 128), f32),
        ),
        in_specs=[any_spec] * 7,
        out_specs=(any_spec, any_spec, pl.BlockSpec(memory_space=pltpu.VMEM)),
        scratch_shapes=[
            wide, main3, main3, main3, main3, pltpu.VMEM((1, 6, 80, 128), f32), wide,
            mask, mask, mask, mask, pltpu.VMEM((3, BX, BY, BZ), f32),
            brick, brick, brick, brick,
            pltpu.VMEM((8, 80, 128), f32), pltpu.VMEM((8, 80, 128), f32), brick, brick,
            pltpu.VMEM((6, 4, NE, 8, 128), f32),
            pltpu.VMEM((6, 2, 4, NE, 8, 128), f32),
            pltpu.VMEM((6, 2, 8, 128), f32),
            pltpu.VMEM((6, 3, 2, 2, 8, 128), f32),
            pltpu.VMEM((5, 3, NE, 8, 128), f32),
            pltpu.VMEM((1, NE, 8, 128), f32),
            pltpu.VMEM((3, NE, 8, 128), f32),
            pltpu.VMEM((BX, 8, 128), f32),
            pltpu.VMEM((3, 7, 2, 8, 128), f32),
            pltpu.VMEM((2, count, 1, 128), f32),
            pltpu.VMEM((2, 1, 128), f32),
            pltpu.SemaphoreType.DMA((7,)),
            pltpu.SemaphoreType.DMA((2,)),
            pltpu.SemaphoreType.DMA((6, 34)),
            pltpu.SemaphoreType.DMA((6, 34)),
            pltpu.SemaphoreType.DMA((2,)),
            pltpu.SemaphoreType.DMA((2,)),
        ],
        compiler_params=pltpu.CompilerParams(
            collective_id=0, has_side_effects=True, vmem_limit_bytes=32 * 2**20
        ),
    )(*args)
    return displacement, sensitivity, compliance[0, 0]


def solution(mesh):
    sizes = tuple(mesh.shape[axis] for axis in AXES)
    block, field = P("gx", "gy", "gz"), P(None, "gx", "gy", "gz")
    return jax.shard_map(
        functools.partial(call, sizes),
        mesh=mesh,
        in_specs=(block,) * 5 + (field,) * 2,
        out_specs=(field, block, P()),
        check_vma=False,
    )
```

```python
import functools
import math

import jax
import jax.numpy as jnp
from jax import lax
from jax.experimental import pallas as pl
from jax.experimental.pallas import tpu as pltpu
from jax.sharding import PartitionSpec as P

MESH = pl.DeviceIdType.MESH
AXES = ("gx", "gy", "gz")

EMIN = 0.001
PENALTY = 3.0
THETA = 1.5
MU16 = 1.0 / (2.6 * 16.0)
DIAG = 88.0 / 9.0

BX, BY, BZ = 4, 64, 128
GROUP = 12
XE = 2
NE = 8

f32 = jnp.float32

DIRECTIONS = sorted(
    [
        (dx, dy, dz)
        for dx in (0, 1, -1)
        for dy in (0, 1, -1)
        for dz in (0, 1, -1)
        if (dx, dy, dz) != (0, 0, 0)
    ],
    key=lambda d: (d[1:] != (0, 0), -sum(abs(step) for step in d)),
)


def iota(dim):
    return lax.broadcasted_iota(jnp.int32, (8, 128), dim)


def lane_pos():
    lane = iota(1)
    return lane - GROUP * ((lane * 43) >> 9)


def rot(value, shift, axis=1):
    size = value.shape[axis]
    return pltpu.roll(value, shift % size, axis)


def yz_modes(a, b, next_z):
    low, high = a + b, b - a
    low_next, high_next = next_z(low), next_z(high)
    return (low + low_next, low_next - low, high + high_next, high_next - high)


def x_modes(near, far):
    return [
        [None if m == 0 else n[m] + f[m] for m in range(4)] + [f[m] - n[m] for m in range(4)]
        for n, f in zip(near, far)
    ]


def mode_forces(q, g):
    u, v, w = q
    force = [[None] * 8 for _ in range(3)]
    trace = 1.5 * (u[4] + v[2] + w[1])
    force[0][4] = g * (trace + (u[4] + u[4]))
    force[1][2] = g * (trace + (v[2] + v[2]))
    force[2][1] = g * (trace + (w[1] + w[1]))
    for (ca, ma), (cb, mb) in (((0, 2), (1, 4)), ((1, 1), (2, 2)), ((0, 1), (2, 4))):
        shear = g * (q[ca][ma] + q[cb][mb])
        force[ca][ma] = shear
        force[cb][mb] = shear
    for (ca, ma), (cb, mb) in (((1, 6), (2, 5)), ((0, 6), (2, 3)), ((0, 5), (1, 3))):
        half = 0.5 * (q[ca][ma] + q[cb][mb])
        force[ca][ma] = g * (q[ca][ma] + half)
        force[cb][mb] = g * (q[cb][mb] + half)
    third = g * (1.0 / 3.0)
    total = u[3] + v[5] + w[6]
    force[0][3] = third * (u[3] + total)
    force[1][5] = third * (v[5] + total)
    force[2][6] = third * (w[6] + total)
    last = g * (5.5 / 9.0)
    for c in range(3):
        force[c][7] = last * q[c][7]
    return force


def mode_energy(q):
    u, v, w = q
    trace = u[4] + v[2] + w[1]
    total = 1.5 * (trace * trace) + 2.0 * (u[4] * u[4] + v[2] * v[2] + w[1] * w[1])
    for (ca, ma), (cb, mb) in (((0, 2), (1, 4)), ((1, 1), (2, 2)), ((0, 1), (2, 4))):
        shear = q[ca][ma] + q[cb][mb]
        total = total + shear * shear
    for (ca, ma), (cb, mb) in (((1, 6), (2, 5)), ((0, 6), (2, 3)), ((0, 5), (1, 3))):
        both = q[ca][ma] + q[cb][mb]
        total = total + (q[ca][ma] * q[ca][ma] + q[cb][mb] * q[cb][mb] + 0.5 * (both * both))
    both = u[3] + v[5] + w[6]
    total = total + (1.0 / 3.0) * (u[3] * u[3] + v[5] * v[5] + w[6] * w[6] + both * both)
    last = u[7] * u[7] + v[7] * v[7] + w[7] * w[7]
    return total + (5.5 / 9.0) * last


def node_planes(planes, moduli):
    before, kept = None, None
    for index, plane in enumerate(planes):
        if before is not None:
            force = mode_forces(x_modes(before, plane), moduli(index - 1))
            right = [
                [-f[4] if m == 0 else f[m] - f[4 + m] for m in range(4)] for f in force
            ]
            left = [[f[4] if m == 0 else f[m] + f[4 + m] for m in range(4)] for f in force]
            if kept is not None:
                yield index - 1, [[k + r for k, r in zip(ks, rs)] for ks, rs in zip(kept, right)]
            kept = left
        before = plane


def node_values(modes, shift_y, shift_z):
    ss, sd, ds, dd = modes
    low = (ss - ds) + shift_y(ss + ds, 0)
    high = (sd - dd) + shift_y(sd + dd, 1)
    return (low - high) + shift_z(low + high)


def body(
    sizes,
    design_in, support_in, load_in, solid_in, void_in, loads_in, start_in,
    disp_out, dsens_out, comp_out,
    dm, um, vm0, vm1, vm2, gm, im, sn, sup, lom, sol, voi, loads, iw, co, s1, s2, des,
    pa, pz, ko, kr, ed, qd, fx, fxd, cy, ar, ar_msg,
    in_sem, out_sem, ssem, rsem, ar_ssem, ar_rsem,
):
    nx, ny, nz = sizes
    count = nx * ny * nz
    me = [lax.axis_index(a) for a in AXES]
    linear = (me[0] * ny + me[1]) * nz + me[2]
    lane, row, pos = iota(1), iota(0), lane_pos()
    own_rows = pl.ds(8, BY)
    zero = jnp.zeros((8, 128), f32)

    copies = [
        pltpu.make_async_copy(src, dst, in_sem.at[i])
        for i, (src, dst) in enumerate(
            (
                (start_in, um.at[:, pl.ds(1, BX), own_rows]),
                (support_in, sup),
                (design_in, dm.at[0, pl.ds(2, BX), own_rows]),
                (solid_in, sol),
                (void_in, voi),
                (load_in, lom),
                (loads_in, loads),
            )
        )
    ]
    for copy in copies:
        copy.start()

    def clear_main(ref, xo, slots):
        comps = ref.shape[0]
        for c in range(comps):
            for s in range(slots):
                own = xo <= s < xo + BX
                for t in (0, 9) if own else range(10):
                    ref[c, s, 8 * t : 8 * t + 8] = zero

    def clear_edges(i, carry):
        for dz in range(2):
            for c in range(4):
                for s in range(NE):
                    pz[i, dz, c, s] = zero
        for a in range(3):
            for b in range(2):
                for d in range(2):
                    kr[i, a, b, d] = zero
        return carry

    clear_main(dm, 2, 8)
    clear_main(um, 1, 7)
    clear_edges(0, 0)

    def exists(d, sign):
        ok = None
        for m, step, size in zip(me, d, sizes):
            if step * sign > 0:
                here = m < size - abs(step)
            elif step * sign < 0:
                here = m >= abs(step)
            else:
                continue
            ok = here if ok is None else ok & here
        return ok

    barrier = pltpu.get_barrier_semaphore()

    greeted = 0
    for d in DIRECTIONS + [(0, 0, 4), (0, 0, -4)]:
        there = exists(d, 1)

        @pl.when(there)
        def _(d=d):
            pl.semaphore_signal(
                barrier,
                inc=1,
                device_id=tuple(m + step for m, step in zip(me, d)),
                device_id_type=MESH,
            )

        greeted = greeted + jnp.where(there, 1, 0)

    clear_main(sn, 2, 8)
    clear_main(gm, 1, 6)
    for ref in (vm0, vm1, im):
        clear_main(ref, 1, 7)
    for c in range(3):
        for s in range(7):
            vm1[c, s, 80:88] = zero
    lax.fori_loop(1, pz.shape[0], clear_edges, 0)

    def group_mask(t, first, last):
        return (lane >= GROUP * (t + 1) + first) & (lane < GROUP * (t + 1) + last)

    def pack_tiles(tiles, base):
        for t, tile in tiles:
            base = jnp.where(group_mask(t, 0, 6), rot(tile, GROUP * (t + 1) + 3), base)
        return base

    def pack(k, fields):
        comp = 0
        total = sum(ref.shape[0] for ref, _ in fields)
        corner = [zero, zero]
        for ref, xo in fields:
            for c in range(ref.shape[0]):
                for x in range(BX):
                    packed = pack_tiles(
                        [(t, ref[c, x + xo, 8 * t + 8 : 8 * t + 16]) for t in range(8)], zero
                    )
                    pa[k, comp, x + XE] = packed
                    i = 6 * (x * total + comp)
                    for side, t in ((0, 0), (1, 7)):
                        corner[side] = jnp.where(
                            (lane >= i) & (lane < i + 6),
                            rot(packed, i - GROUP * (t + 1)),
                            corner[side],
                        )
                comp += 1
        for side in range(2):
            ko[k, side] = corner[side]

    def messages(k, fields):
        comps = sum(f[0].shape[0] for f in fields)
        low, high = max(f[2] for f in fields), max(f[3] for f in fields)
        result, slot = [], 0
        for d in DIRECTIONS:
            dx, dy, dz = d
            if (1 in d and low == 0) or (-1 in d and high == 0):
                continue
            parts = []
            if dz == 0:
                for n, (ref, xo, lo, hi) in enumerate(fields):
                    if (1 in d and lo == 0) or (-1 in d and hi == 0):
                        continue
                    if dx == 1:
                        xs, xd = pl.ds(xo + BX - lo, lo), pl.ds(xo - lo, lo)
                    elif dx == -1:
                        xs, xd = pl.ds(xo, hi), pl.ds(xo + BX, hi)
                    else:
                        xs = xd = pl.ds(xo, BX)
                    if dy == 1:
                        ys, yd = pl.ds(BY, 8), pl.ds(0, 8)
                    elif dy == -1:
                        ys, yd = pl.ds(8, 8), pl.ds(BY + 8, 8)
                    else:
                        ys = yd = own_rows
                    parts.append((n, ref.at[:, xs, ys], ref.at[:, xd, yd]))
            elif dy == 0:
                if dx == 1:
                    xs, xd = pl.ds(XE + BX - low, low), pl.ds(XE - low, low)
                elif dx == -1:
                    xs, xd = pl.ds(XE, high), pl.ds(XE + BX, high)
                else:
                    xs = xd = pl.ds(XE, BX)
                side, cs = 0 if dz == 1 else 1, pl.ds(0, comps)
                parts.append((-1, pa.at[k, cs, xs], pz.at[k, side, cs, xd]))
            else:
                own = ko.at[k, 0 if dy == -1 else 1]
                there = kr.at[k, 1 - dx, 0 if dy == 1 else 1, 0 if dz == 1 else 1]
                parts.append((-1, own, there))
            for n, src, dst in parts:
                copy = pltpu.make_async_remote_copy(
                    src_ref=src,
                    dst_ref=dst,
                    send_sem=ssem.at[k, slot],
                    recv_sem=rsem.at[k, slot],
                    device_id=tuple(m + step for m, step in zip(me, d)),
                    device_id_type=MESH,
                )
                slot += 1
                result.append((d, n, copy))
        return result

    def each(msgs, sign, act):
        for d in DIRECTIONS:
            group = [copy for way, _, copy in msgs if way == d]
            if group:
                @pl.when(exists(d, sign))
                def _(group=group):
                    for copy in group:
                        act(copy)

    def send(msgs):
        each(msgs, 1, lambda copy: copy.start())

    def receive(msgs):
        each(msgs, -1, lambda copy: copy.wait_recv())

    def sent(msgs):
        each(msgs, 1, lambda copy: copy.wait_send())

    def plain(msgs, n=None):
        return [m for m in msgs if m[1] >= 0 and n in (None, m[1])]

    def packed(msgs):
        return [m for m in msgs if m[1] < 0]

    def assemble(k, ref, xo, first_comp, comps, planes, edge=None, halo=None):
        for c in range(ref.shape[0]):
            comp = first_comp + c
            for x in planes:
                source = x % BX
                side_x = 0 if x < 0 else 2 if x >= BX else 1
                i = 6 * (source * comps + comp)
                ends = []
                for side in range(2):
                    value = pz[k, side, comp, x + XE]
                    value = jnp.where(lane < 6, rot(kr[k, side_x, 0, side], -i), value)
                    value = jnp.where(
                        group_mask(8, 0, 6), rot(kr[k, side_x, 1, side], 9 * GROUP - i), value
                    )
                    ends.append(value)
                left, right = ends
                if halo is not None:
                    halo[c, x + XE] = jnp.where(pos < 3, left, right)
                if edge is not None:
                    if side_x == 1:
                        own = pack_tiles(
                            [(t, ref[c, x + xo, 8 * t + 8 : 8 * t + 16]) for t in (-1, 8)],
                            pa[k, comp, x + XE],
                        )
                    else:
                        own = pack_tiles(
                            [(t, ref[c, x + xo, 8 * t + 8 : 8 * t + 16]) for t in range(-1, 9)],
                            zero,
                        )
                    low = jnp.where(pos < 3, own, right)
                    high = jnp.where(pos < 3, left, own)
                    edge[c, x + XE] = jnp.where(pos < 6, low, rot(high, 6))

    def next_z(value):
        return rot(value, -1)

    def last_z(value):
        return rot(value, 1)

    def main_plane(ref, s, t):
        start = 8 * t + 8
        return [
            yz_modes(
                ref[c, s, pl.ds(pl.multiple_of(start, 8), 8)], ref[c, s, pl.ds(start + 1, 8)], next_z
            )
            for c in range(3)
        ]

    def edge_plane(edge, x):
        out = []
        for c in range(3):
            a = edge[c, x + XE]
            b = rot(jnp.where(row == 0, rot(a, -GROUP), a), -1, 0)
            out.append(yz_modes(a, b, next_z))
        return out

    def edge_down(value, _):
        down = rot(value, 1, 0)
        return jnp.where(row == 0, rot(down, GROUP), down)

    def tile(t):
        return pl.ds(pl.multiple_of(8 * t + 8, 8), 8)

    def brick(t):
        return pl.ds(pl.multiple_of(8 * t, 8), 8)

    outer = (lane == 0) | (lane == 127)

    def apply(ref, edge, planes, tiles, use, use_edge=None):
        nodes = [planes[0] - 1, *planes, planes[-1] + 1]
        for index, modes in node_planes(
            (edge_plane(edge, x) for x in nodes), lambda e: ed[4, 0, nodes[e] + XE]
        ):
            x = nodes[index]
            for c in range(3):
                value = node_values(modes[c], edge_down, last_z)
                fx[c, x + XE] = jnp.where(pos == 3, rot(value, -6), value)
                if use_edge is not None:
                    use_edge(x, c, value)

        def one(t, first):
            for index, modes in node_planes(
                (main_plane(ref, x + 1, t) for x in nodes),
                lambda e: gm[0, nodes[e] + 1, tile(t)],
            ):
                x = nodes[index]
                for c in range(3):
                    def shift_y(value, which):
                        down = rot(value, 1, 0)
                        before = None if first else cy[c, x + 1, which]
                        cy[c, x + 1, which] = down
                        return down if first else jnp.where(row == 0, before, down)

                    if first:
                        ss, sd, ds, dd = modes[c]
                        shift_y(ss + ds, 0)
                        shift_y(sd + dd, 1)
                    else:
                        value = node_values(modes[c], shift_y, last_z)
                        fixed = rot(fx[c, x + XE], lax.rem(254 - GROUP * (t + 1) - 1, 128))
                        use(x, c, t, jnp.where(outer, fixed, value))

        one(-1, True)
        lax.fori_loop(0, 8, lambda t, carry: (one(t, False), carry)[1], 0)
        for t in range(8, tiles):
            one(t, False)

    weights = {}
    for a in range(3):
        for b in range(3):
            for c in range(3):
                weights[a, b, c] = max(0.0, 3.0 - math.sqrt(a * a + b * b + c * c))

    def filter_z(ref, halo):
        def step(t, carry):
            for s in range(8):
                here = ref[0, s, brick(t)]
                side = rot(halo[0, s], lax.rem(256 - GROUP * t - 3, 128))
                one = rot(jnp.where(lane < 1, side, here), -1) + rot(
                    jnp.where(lane >= 127, side, here), 1
                )
                two = rot(jnp.where(lane < 2, side, here), -2) + rot(
                    jnp.where(lane >= 126, side, here), 2
                )
                s1[s, brick(t)] = one
                s2[s, brick(t)] = two
            return carry

        lax.fori_loop(0, 10, step, 0)

    def filter_xy(ref, use):
        def step(t, carry):
            total = [None] * BX
            for s in range(8):
                def rows(source, off):
                    return source[pl.ds(8 * t + 8 + off, 8)]

                parts = []
                for source in (ref.at[0, s], s1.at[s], s2.at[s]):
                    parts.append(
                        [
                            rows(source, 0),
                            rows(source, 1) + rows(source, -1),
                            rows(source, 2) + rows(source, -2),
                        ]
                    )
                pair = {
                    (0, 0): parts[0][0],
                    (0, 1): parts[0][1] + parts[1][0],
                    (1, 1): parts[1][1],
                    (0, 2): parts[0][2] + parts[2][0],
                    (1, 2): parts[1][2] + parts[2][1],
                    (2, 2): parts[2][2],
                }
                sums = {}
                for x in range(BX):
                    away = abs(x + 2 - s)
                    if away > 2:
                        continue
                    if away not in sums:
                        value = None
                        for (b, c), term in pair.items():
                            if weights[away, b, c] > 0.0:
                                term = weights[away, b, c] * term
                                value = term if value is None else value + term
                        sums[away] = value
                    total[x] = sums[away] if total[x] is None else total[x] + sums[away]
            for x in range(BX):
                use(x, t, total[x])
            return carry

        lax.fori_loop(0, 8, step, 0)

    def reduce_start(k, value):
        ar_msg[k] = value
        ar[k, linear] = value

        steps = [
            (ox, oy, oz)
            for ox in range(nx)
            for oy in range(ny)
            for oz in range(nz)
            if (ox, oy, oz) != (0, 0, 0)
        ]
        steps.sort(key=lambda o: -sum(min(step, size - step) for step, size in zip(o, sizes)))
        for o in steps:
            pltpu.make_async_remote_copy(
                src_ref=ar_msg.at[k],
                dst_ref=ar.at[k, linear],
                send_sem=ar_ssem.at[k],
                recv_sem=ar_rsem.at[k],
                device_id=tuple(
                    lax.rem(m + step, size) if step else m for m, step, size in zip(me, o, sizes)
                ),
                device_id_type=MESH,
            ).start()

    def reduce_wait(k, sem):
        part = ar.at[k, pl.ds(0, count - 1)]
        pltpu.make_async_copy(part, part, sem.at[k]).wait()

    def reduce_total(k):
        reduce_wait(k, ar_rsem)
        return jnp.sum(ar[k], axis=0)


    copies[0].wait()
    copies[1].wait()
    for c in range(3):
        um[c, 1 : 1 + BX, 8 : 8 + BY] = um[c, 1 : 1 + BX, 8 : 8 + BY] * (1 - sup[...]).astype(f32)
    copies[2].wait()
    pack(0, [(dm, 2), (um, 1)])
    pl.semaphore_wait(barrier, greeted)
    first = messages(0, [(dm, 2, 2, 2), (um, 1, 1, 1)])
    send(packed(first))
    send(plain(first, 0))
    send(plain(first, 1))

    def inside(coord, size):
        return ((coord >= 0) & (coord < size)).astype(f32)

    z_at = me[2] * BZ + lane
    z_terms = [
        jnp.ones((8, 128), f32),
        inside(z_at - 1, nz * BZ) + inside(z_at + 1, nz * BZ),
        inside(z_at - 2, nz * BZ) + inside(z_at + 2, nz * BZ),
    ]
    x_rows = []
    for x in range(BX):
        x_at = me[0] * BX + x
        x_terms = [
            f32(1.0),
            inside(x_at - 1, nx * BX) + inside(x_at + 1, nx * BX),
            inside(x_at - 2, nx * BX) + inside(x_at + 2, nx * BX),
        ]
        per_b = []
        for b in range(3):
            value = zero
            for c in range(3):
                value = value + z_terms[c] * sum(x_terms[a] * weights[a, b, c] for a in range(3))
            per_b.append(value)
        x_rows.append(per_b)

    def weigh(t, carry):
        y_at = me[1] * BY + 8 * t + row
        one = inside(y_at - 1, ny * BY) + inside(y_at + 1, ny * BY)
        two = inside(y_at - 2, ny * BY) + inside(y_at + 2, ny * BY)
        for x in range(BX):
            iw[x, brick(t)] = 1.0 / (x_rows[x][0] + one * x_rows[x][1] + two * x_rows[x][2])
        return carry

    lax.fori_loop(0, 8, weigh, 0)
    for copy in copies[3:]:
        copy.wait()

    receive(packed(first))
    receive(plain(first, 0))
    assemble(0, dm, 2, 0, 4, range(-2, 6), halo=qd)

    filter_z(dm, qd)

    def to_modulus(x, t, total):
        at = brick(t)
        scale = iw[x, at]
        solid, void = sol[x, at] > 0, voi[x, at] > 0
        physical = jnp.where(solid, 1.0, jnp.where(void, 0.0, total * scale))
        square = physical * physical
        gm[0, 1 + x, tile(t)] = MU16 * EMIN + (MU16 * (1.0 - EMIN)) * (square * physical)
        co[x, at] = jnp.where(
            solid | void, 0.0, (-PENALTY * (1.0 - EMIN) * MU16) * (square * scale)
        )

    filter_xy(dm, to_modulus)
    second = messages(1, [(gm, 1, 1, 1)])
    send(plain(second))
    pack(1, [(gm, 1)])
    send(packed(second))
    receive(plain(first, 1))
    assemble(0, um, 1, 1, 4, range(-1, 5), edge=ed.at[0])
    receive(second)
    assemble(1, gm, 1, 0, 1, range(-1, 5), edge=ed.at[4])

    for x in range(BX):
        value = ed[4, 0, x + XE] + ed[4, 0, x + XE - 1]
        value = value + edge_down(value, 0)
        fxd[x] = value + last_z(value)

    def diagonal(t, carry):
        for x in range(BX):
            value = None
            for s in (x, x + 1):
                term = gm[0, s, tile(t)] + gm[0, s, pl.ds(8 * t + 7, 8)]
                value = term if value is None else value + term
            value = value + last_z(value)
            fixed = rot(fxd[x], lax.rem(256 - GROUP * (t + 1) - 9, 128))
            value = jnp.where(lane == 0, fixed, value)
            free = (1 - sup[x, brick(t)]).astype(f32)
            im[0, 1 + x, tile(t)] = free / (DIAG * value)
        return carry

    lax.fori_loop(0, 8, diagonal, 0)

    sums = {}
    acc_names = ("b0", "a00", "a01", "a11", "a12", "a22", "energy")
    for n, name in enumerate(acc_names):
        s1[n, 0:8] = zero
        sums[name] = s1.at[n, pl.ds(0, 8)]

    def add(name, value):
        sums[name][...] = sums[name][...] + value

    def from_start(x, c, t, image):
        at = brick(t)
        free = (1 - sup[x, at]).astype(f32)
        load = lom[x, at].astype(f32)
        left = free * (load * loads[c, x, at] - image)
        value = im[0, 1 + x, tile(t)] * left
        vm0[c, 1 + x, tile(t)] = value
        add("b0", left * value)

    def from_vector(source, target, diag_name, next_name):
        def use(x, c, t, image):
            here = source[c, 1 + x, tile(t)]
            value = im[0, 1 + x, tile(t)] * image - THETA * here
            target[c, 1 + x, tile(t)] = value
            if x < BX and not (isinstance(t, int) and t >= 8):
                add(diag_name, here * image)
                add(next_name, value * image)

        return use

    own = list(range(BX))
    third = messages(2, [(vm0, 1, 1, 1), (im, 1, 0, 1)])
    send(plain(third, 1))
    apply(um, ed.at[0], own, 8, from_start)
    send(plain(third, 0))
    pack(2, [(vm0, 1), (im, 1)])
    send(packed(third))
    receive(third)
    assemble(2, vm0, 1, 0, 4, range(-1, 5), edge=ed.at[1])
    assemble(2, im, 1, 3, 4, range(0, 5), edge=ed.at[5])
    apply(vm0, ed.at[1], own, 8, from_vector(vm0, vm1, "a00", "a01"))
    fourth = messages(3, [(vm1, 1, 1, 2)])
    send(plain(fourth))
    pack(3, [(vm1, 1)])
    send(packed(fourth))
    receive(fourth)
    assemble(3, vm1, 1, 0, 3, range(-1, 6), edge=ed.at[2])

    def edge_vector(x, c, image):
        ed[3, c, x + XE] = ed[5, 0, x + XE] * image - THETA * ed[2, c, x + XE]

    apply(
        vm1, ed.at[2], own + [BX], 9, from_vector(vm1, vm2, "a11", "a12"), edge_vector
    )

    def energies(planes):
        before = None
        for index, plane in enumerate(planes):
            if before is not None:
                yield index - 1, mode_energy(x_modes(before, plane))
            before = plane

    column = (pos == 2) & (lane >= GROUP) & (lane < 9 * GROUP)

    edge_sum = zero
    for x, value in energies(edge_plane(ed.at[3], x) for x in range(BX + 1)):
        edge_sum = edge_sum + jnp.where(column, ed[4, 0, x + XE] * value, 0.0)

    def last_moment(t, carry):
        total = zero
        for x, value in energies(main_plane(vm2, x + 1, t) for x in range(BX + 1)):
            total = total + gm[0, 1 + x, tile(t)] * value
        add("a22", jnp.where(lane < 127, total, 0.0))
        return carry

    add("a22", edge_sum)
    lax.fori_loop(0, 8, last_moment, 0)

    message = jnp.zeros((1, 128), f32)
    lane1 = lax.broadcasted_iota(jnp.int32, (1, 128), 1)
    for n, name in enumerate(acc_names[:6]):
        part = jnp.sum(jnp.sum(sums[name][...], axis=0, keepdims=True), axis=1, keepdims=True)
        message = jnp.where(lane1 == n, part, message)
    reduce_start(0, message)
    for msgs in (first, second, third, fourth):
        sent(msgs)
    totals = reduce_total(0)
    b0, a00, a01, a11, a12, a22 = (
        jnp.broadcast_to(totals[:, n : n + 1], (1, 128)) for n in range(6)
    )
    tiny = 1e-6
    b1 = a00 - THETA * b0
    b2 = a01 - THETA * b1
    l10, l20 = a01 / a00, a11 / a00
    d1 = a11 - l10 * a01
    ok1 = d1 > tiny * a11
    safe1 = jnp.where(ok1, d1, 1.0)
    cross = a12 - l20 * a01
    l21 = jnp.where(ok1, cross / safe1, 0.0)
    d2 = a22 - l20 * a11 - l21 * cross
    ok2 = ok1 & (d2 > tiny * a22)
    y1 = b1 - l10 * b0
    y2 = b2 - l20 * b0 - l21 * y1
    c2 = jnp.where(ok2, y2 / jnp.where(ok2, d2, 1.0), 0.0)
    c1 = jnp.where(ok1, y1 / safe1, 0.0) - l21 * c2
    c0 = b0 / a00 - l10 * c1 - l20 * c2
    c0, c1, c2 = (jnp.broadcast_to(c, (8, 128)) for c in (c0, c1, c2))

    for c in range(3):
        for x in range(BX + 1):
            s = x + XE
            ed[0, c, s] = ed[0, c, s] + (
                c0 * ed[1, c, s] + c1 * ed[2, c, s] + c2 * ed[3, c, s]
            )

    def combine(t, carry):
        for c in range(3):
            for s in range(1, BX + 2):
                at = brick(t + 1)
                um[c, s, at] = um[c, s, at] + (
                    c0 * vm0[c, s, at] + c1 * vm1[c, s, at] + c2 * vm2[c, s, at]
                )
        return carry

    lax.fori_loop(0, 9, combine, 0)
    disp = pltpu.make_async_copy(um.at[:, pl.ds(1, BX), own_rows], disp_out, out_sem.at[0])
    disp.start()

    for x, value in energies(edge_plane(ed.at[0], x) for x in range(BX + 1)):
        fxd[x] = value

    def sensitivity(t, carry):
        total = zero
        for x, value in energies(main_plane(um, x + 1, t) for x in range(BX + 1)):
            fixed = rot(fxd[x], lax.rem(253 - GROUP * (t + 1), 128))
            value = jnp.where(lane == 127, fixed, value)
            total = total + gm[0, 1 + x, tile(t)] * value
            sn[0, 2 + x, tile(t)] = co[x, brick(t)] * value
        add("energy", total)
        return carry

    lax.fori_loop(0, 8, sensitivity, 0)
    fifth = messages(4, [(sn, 2, 2, 2)])
    send(plain(fifth))
    pack(4, [(sn, 2)])
    send(packed(fifth))
    part = jnp.sum(jnp.sum(sums["energy"][...], axis=0, keepdims=True), axis=1, keepdims=True)
    reduce_start(1, jnp.broadcast_to(part, (1, 128)))
    receive(fifth)
    assemble(4, sn, 2, 0, 1, range(-2, 6), halo=qd)
    filter_z(sn, qd)

    def finish(x, t, total):
        des[x, brick(t)] = total

    filter_xy(sn, finish)
    out = pltpu.make_async_copy(des, dsens_out, out_sem.at[1])
    out.start()
    comp_out[...] = reduce_total(1)
    sent(fifth)
    for k in range(2):
        reduce_wait(k, ar_ssem)
    disp.wait()
    out.wait()


def call(sizes, *args):
    count = sizes[0] * sizes[1] * sizes[2]
    main3 = pltpu.VMEM((3, 7, 88, 128), f32)
    wide = pltpu.VMEM((1, 8, 80, 128), f32)
    brick = pltpu.VMEM((BX, BY, BZ), f32)
    mask = pltpu.VMEM((BX, BY, BZ), jnp.int32)
    any_spec = pl.BlockSpec(memory_space=pl.ANY)
    displacement, sensitivity, compliance = pl.pallas_call(
        functools.partial(body, sizes),
        out_shape=(
            jax.ShapeDtypeStruct((3, BX, BY, BZ), f32),
            jax.ShapeDtypeStruct((BX, BY, BZ), f32),
            jax.ShapeDtypeStruct((1, 128), f32),
        ),
        in_specs=[any_spec] * 7,
        out_specs=(any_spec, any_spec, pl.BlockSpec(memory_space=pltpu.VMEM)),
        scratch_shapes=[
            wide, main3, main3, main3, main3, pltpu.VMEM((1, 6, 80, 128), f32),
            pltpu.VMEM((1, 7, 80, 128), f32), wide,
            mask, mask, mask, mask, pltpu.VMEM((3, BX, BY, BZ), f32),
            brick, brick, pltpu.VMEM((8, 80, 128), f32), pltpu.VMEM((8, 80, 128), f32), brick,
            pltpu.VMEM((5, 4, NE, 8, 128), f32),
            pltpu.VMEM((5, 2, 4, NE, 8, 128), f32),
            pltpu.VMEM((5, 2, 8, 128), f32),
            pltpu.VMEM((5, 3, 2, 2, 8, 128), f32),
            pltpu.VMEM((6, 3, NE, 8, 128), f32),
            pltpu.VMEM((1, NE, 8, 128), f32),
            pltpu.VMEM((3, NE, 8, 128), f32),
            pltpu.VMEM((BX, 8, 128), f32),
            pltpu.VMEM((3, 7, 2, 8, 128), f32),
            pltpu.VMEM((2, count, 1, 128), f32),
            pltpu.VMEM((2, 1, 128), f32),
            pltpu.SemaphoreType.DMA((7,)),
            pltpu.SemaphoreType.DMA((2,)),
            pltpu.SemaphoreType.DMA((5, 34)),
            pltpu.SemaphoreType.DMA((5, 34)),
            pltpu.SemaphoreType.DMA((2,)),
            pltpu.SemaphoreType.DMA((2,)),
        ],
        compiler_params=pltpu.CompilerParams(
            collective_id=0, has_side_effects=True, vmem_limit_bytes=60 * 2**20
        ),
    )(*args)
    return displacement, sensitivity, compliance[0, 0]


def solution(mesh):
    sizes = tuple(mesh.shape[axis] for axis in AXES)
    block, field = P("gx", "gy", "gz"), P(None, "gx", "gy", "gz")
    return jax.shard_map(
        functools.partial(call, sizes),
        mesh=mesh,
        in_specs=(block,) * 5 + (field,) * 2,
        out_specs=(field, block, P()),
        check_vma=False,
    )
```

```python
import functools
import math

import jax
import jax.numpy as jnp
from jax import lax
from jax.experimental import pallas as pl
from jax.experimental.pallas import tpu as pltpu
from jax.sharding import PartitionSpec as P

MESH = pl.DeviceIdType.MESH
AXES = ("gx", "gy", "gz")

EMIN = 0.001
PENALTY = 3.0
THETA = 1.5
MU16 = 1.0 / (2.6 * 16.0)
DIAG = 88.0 / 9.0

BX, BY, BZ = 4, 64, 128
GROUP = 12
XE = 2
NE = 8

f32 = jnp.float32

DIRECTIONS = sorted(
    [
        (dx, dy, dz)
        for dx in (0, 1, -1)
        for dy in (0, 1, -1)
        for dz in (0, 1, -1)
        if (dx, dy, dz) != (0, 0, 0)
    ],
    key=lambda d: (d[1:] != (0, 0), -sum(abs(step) for step in d)),
)


def iota(dim):
    return lax.broadcasted_iota(jnp.int32, (8, 128), dim)


def lane_pos():
    lane = iota(1)
    return lane - GROUP * ((lane * 43) >> 9)


def rot(value, shift, axis=1):
    size = value.shape[axis]
    return pltpu.roll(value, shift % size, axis)


def yz_modes(a, b, next_z):
    low, high = a + b, b - a
    low_next, high_next = next_z(low), next_z(high)
    return (low + low_next, low_next - low, high + high_next, high_next - high)


def x_modes(near, far):
    return [
        [None if m == 0 else n[m] + f[m] for m in range(4)] + [f[m] - n[m] for m in range(4)]
        for n, f in zip(near, far)
    ]


def mode_forces(q, g):
    u, v, w = q
    force = [[None] * 8 for _ in range(3)]
    trace = 1.5 * (u[4] + v[2] + w[1])
    force[0][4] = g * (trace + (u[4] + u[4]))
    force[1][2] = g * (trace + (v[2] + v[2]))
    force[2][1] = g * (trace + (w[1] + w[1]))
    for (ca, ma), (cb, mb) in (((0, 2), (1, 4)), ((1, 1), (2, 2)), ((0, 1), (2, 4))):
        shear = g * (q[ca][ma] + q[cb][mb])
        force[ca][ma] = shear
        force[cb][mb] = shear
    for (ca, ma), (cb, mb) in (((1, 6), (2, 5)), ((0, 6), (2, 3)), ((0, 5), (1, 3))):
        half = 0.5 * (q[ca][ma] + q[cb][mb])
        force[ca][ma] = g * (q[ca][ma] + half)
        force[cb][mb] = g * (q[cb][mb] + half)
    third = g * (1.0 / 3.0)
    total = u[3] + v[5] + w[6]
    force[0][3] = third * (u[3] + total)
    force[1][5] = third * (v[5] + total)
    force[2][6] = third * (w[6] + total)
    last = g * (5.5 / 9.0)
    for c in range(3):
        force[c][7] = last * q[c][7]
    return force


def mode_energy(q):
    u, v, w = q
    trace = u[4] + v[2] + w[1]
    total = 1.5 * (trace * trace) + 2.0 * (u[4] * u[4] + v[2] * v[2] + w[1] * w[1])
    for (ca, ma), (cb, mb) in (((0, 2), (1, 4)), ((1, 1), (2, 2)), ((0, 1), (2, 4))):
        shear = q[ca][ma] + q[cb][mb]
        total = total + shear * shear
    for (ca, ma), (cb, mb) in (((1, 6), (2, 5)), ((0, 6), (2, 3)), ((0, 5), (1, 3))):
        both = q[ca][ma] + q[cb][mb]
        total = total + (q[ca][ma] * q[ca][ma] + q[cb][mb] * q[cb][mb] + 0.5 * (both * both))
    both = u[3] + v[5] + w[6]
    total = total + (1.0 / 3.0) * (u[3] * u[3] + v[5] * v[5] + w[6] * w[6] + both * both)
    last = u[7] * u[7] + v[7] * v[7] + w[7] * w[7]
    return total + (5.5 / 9.0) * last


def node_parts(planes, xs, moduli):
    before, kept = None, None
    for index, plane in enumerate(planes):
        if before is not None:
            force = mode_forces(x_modes(before, plane), moduli(xs[index - 1]))
            right = [[-f[4] if m == 0 else f[m] - f[4 + m] for m in range(4)] for f in force]
            left = [[f[4] if m == 0 else f[m] + f[4 + m] for m in range(4)] for f in force]
            if kept is not None:
                right = [[k + r for k, r in zip(ks, rs)] for ks, rs in zip(kept, right)]
            yield xs[index - 1], right
            kept = left
        before = plane
    yield xs[-1], kept


def node_values(modes, shift_y, shift_z):
    ss, sd, ds, dd = modes
    low = (ss - ds) + shift_y(ss + ds, 0)
    high = (sd - dd) + shift_y(sd + dd, 1)
    return (low - high) + shift_z(low + high)


def body(
    sizes,
    design_in, support_in, load_in, solid_in, void_in, loads_in, start_in,
    disp_out, dsens_out, comp_out,
    dm, um, vm0, vm1, vm2, gm, im, sn, sup, lom, sol, voi, loads, iw, co, fz, img, acc,
    pa, pz, po, ko, kr, ed, qd, fx, fxd, cy, ar, ar_msg,
    in_sem, out_sem, ssem, rsem, ar_ssem, ar_rsem,
):
    nx, ny, nz = sizes
    count = nx * ny * nz
    me = [lax.axis_index(a) for a in AXES]
    linear = (me[0] * ny + me[1]) * nz + me[2]
    lane, row, pos = iota(1), iota(0), lane_pos()
    pos6 = jnp.where(pos < 6, pos, pos - 6)
    own_rows = pl.ds(8, BY)
    zero = jnp.zeros((8, 128), f32)

    copies = [
        pltpu.make_async_copy(src, dst, in_sem.at[i])
        for i, (src, dst) in enumerate(
            (
                (start_in, um.at[:, pl.ds(1, BX), own_rows]),
                (support_in, sup),
                (design_in, dm.at[0, pl.ds(2, BX), own_rows]),
                (solid_in, sol),
                (void_in, voi),
                (load_in, lom),
                (loads_in, loads),
            )
        )
    ]
    for copy in copies:
        copy.start()

    def clear_main(ref, xo, slots):
        comps = ref.shape[0]
        for c in range(comps):
            for s in range(slots):
                own = xo <= s < xo + BX
                for t in (0, 9) if own else range(10):
                    ref[c, s, 8 * t : 8 * t + 8] = zero

    def clear_edges(i, carry):
        for dz in range(2):
            for c in range(4):
                for s in range(NE):
                    pz[i, dz, c, s] = zero
        for a in range(3):
            for b in range(2):
                for d in range(2):
                    kr[i, a, b, d] = zero
        return carry

    clear_main(dm, 2, 8)
    clear_main(um, 1, 7)
    clear_edges(0, 0)

    def exists(d, sign):
        ok = None
        for m, step, size in zip(me, d, sizes):
            if step * sign > 0:
                here = m < size - abs(step)
            elif step * sign < 0:
                here = m >= abs(step)
            else:
                continue
            ok = here if ok is None else ok & here
        return ok

    barrier = pltpu.get_barrier_semaphore()

    greeted = 0
    for d in DIRECTIONS + [(0, 0, 4), (0, 0, -4)]:
        there = exists(d, 1)

        @pl.when(there)
        def _(d=d):
            pl.semaphore_signal(
                barrier,
                inc=1,
                device_id=tuple(m + step for m, step in zip(me, d)),
                device_id_type=MESH,
            )

        greeted = greeted + jnp.where(there, 1, 0)

    clear_main(sn, 2, 8)
    clear_main(gm, 1, 6)
    for ref in (vm0, vm1, im):
        clear_main(ref, 1, 7)
    for c in range(3):
        for s in range(7):
            vm1[c, s, 80:88] = zero
    lax.fori_loop(1, pz.shape[0], clear_edges, 0)

    def group_mask(t, first, last):
        return (lane >= GROUP * (t + 1) + first) & (lane < GROUP * (t + 1) + last)

    def pack_tiles(tiles, base):
        for t, tile in tiles:
            base = jnp.where(group_mask(t, 0, 6), rot(tile, GROUP * (t + 1) + 3), base)
        return base

    def pack(k, fields):
        comp = 0
        total = sum(ref.shape[0] for ref, _ in fields)
        corner = [zero, zero]
        for ref, xo in fields:
            for c in range(ref.shape[0]):
                for x in range(BX):
                    packed = pack_tiles(
                        [(t, ref[c, x + xo, 8 * t + 8 : 8 * t + 16]) for t in range(8)], zero
                    )
                    pa[k, comp, x + XE] = packed
                    i = 6 * (x * total + comp)
                    for side, t in ((0, 0), (1, 7)):
                        corner[side] = jnp.where(
                            (lane >= i) & (lane < i + 6),
                            rot(packed, i - GROUP * (t + 1)),
                            corner[side],
                        )
                comp += 1
        for side in range(2):
            ko[k, side] = corner[side]

    def messages(k, fields):
        comps = sum(f[0].shape[0] for f in fields)
        low, high = max(f[2] for f in fields), max(f[3] for f in fields)
        result, slot = [], 0
        for d in DIRECTIONS:
            dx, dy, dz = d
            if (1 in d and low == 0) or (-1 in d and high == 0):
                continue
            parts = []
            if dz == 0:
                for n, (ref, xo, lo, hi) in enumerate(fields):
                    if (1 in d and lo == 0) or (-1 in d and hi == 0):
                        continue
                    if dx == 1:
                        xs, xd = pl.ds(xo + BX - lo, lo), pl.ds(xo - lo, lo)
                    elif dx == -1:
                        xs, xd = pl.ds(xo, hi), pl.ds(xo + BX, hi)
                    else:
                        xs = xd = pl.ds(xo, BX)
                    if dy == 1:
                        ys, yd = pl.ds(BY, 8), pl.ds(0, 8)
                    elif dy == -1:
                        ys, yd = pl.ds(8, 8), pl.ds(BY + 8, 8)
                    else:
                        ys = yd = own_rows
                    parts.append((n, ref.at[:, xs, ys], ref.at[:, xd, yd]))
            elif dy == 0:
                if dx == 1:
                    xs, xd = pl.ds(XE + BX - low, low), pl.ds(XE - low, low)
                elif dx == -1:
                    xs, xd = pl.ds(XE, high), pl.ds(XE + BX, high)
                else:
                    xs = xd = pl.ds(XE, BX)
                side, cs = 0 if dz == 1 else 1, pl.ds(0, comps)
                parts.append((-1, pa.at[k, cs, xs], pz.at[k, side, cs, xd]))
            else:
                own = ko.at[k, 0 if dy == -1 else 1]
                there = kr.at[k, 1 - dx, 0 if dy == 1 else 1, 0 if dz == 1 else 1]
                parts.append((-1, own, there))
            for n, src, dst in parts:
                copy = pltpu.make_async_remote_copy(
                    src_ref=src,
                    dst_ref=dst,
                    send_sem=ssem.at[k, slot],
                    recv_sem=rsem.at[k, slot],
                    device_id=tuple(m + step for m, step in zip(me, d)),
                    device_id_type=MESH,
                )
                slot += 1
                result.append((d, n, copy))
        return result

    def each(msgs, sign, act):
        for d in DIRECTIONS:
            group = [copy for way, _, copy in msgs if way == d]
            if group:
                @pl.when(exists(d, sign))
                def _(group=group):
                    for copy in group:
                        act(copy)

    def send(msgs):
        each(msgs, 1, lambda copy: copy.start())

    def receive(msgs):
        each(msgs, -1, lambda copy: copy.wait_recv())

    def sent(msgs):
        each(msgs, 1, lambda copy: copy.wait_send())

    def plain(msgs, n=None):
        return [m for m in msgs if m[1] >= 0 and n in (None, m[1])]

    def packed(msgs):
        return [m for m in msgs if m[1] < 0]

    def pack_around(ref, xo, first_comp, planes):
        for x in planes:
            for c in range(ref.shape[0]):
                outside = x < 0 or x >= BX
                po[first_comp + c, x + XE] = pack_tiles(
                    [
                        (t, ref[c, x + xo, 8 * t + 8 : 8 * t + 16])
                        for t in (range(-1, 9) if outside else (-1, 8))
                    ],
                    zero,
                )

    def assemble(k, count, first_comp, comps, planes, halo, edge=None):
        items = [(c, x) for x in planes for c in range(count)]
        around = {}
        for _, x in items:
            side = 0 if x < 0 else 2 if x >= BX else 1
            for end in range(2):
                if (side, end) not in around:
                    around[side, end] = jnp.where(pos6 < 3, kr[k, side, end, 0], kr[k, side, end, 1])
        inner = (lane >= GROUP) & (lane < 9 * GROUP)
        for c, x in items:
            comp = first_comp + c
            side = 0 if x < 0 else 2 if x >= BX else 1
            i = 6 * (x % BX * comps + comp)
            value = jnp.where(pos < 3, pz[k, 0, comp, x + XE], pz[k, 1, comp, x + XE])
            value = jnp.where(lane < 6, rot(around[side, 0], -i), value)
            value = jnp.where(group_mask(8, 0, 6), rot(around[side, 1], 9 * GROUP - i), value)
            if halo is not None:
                halo[c, x + XE] = value
            if edge is not None:
                own = po[comp, x + XE]
                if side == 1:
                    own = jnp.where(inner, pa[k, comp, x + XE], own)
                high = rot(jnp.where(pos < 3, value, own), 6)
                low = jnp.where(pos < 3, own, value)
                edge[c, x + XE] = jnp.where(pos < 6, low, high)

    def next_z(value):
        return rot(value, -1)

    def last_z(value):
        return rot(value, 1)

    def main_plane(ref, s, t, shifted=None):
        start = 8 * t + 8
        out = []
        for c in range(3):
            a, b = ref[c, s, tile(t)], ref[c, s, pl.ds(start + 1, 8)]
            if shifted is None:
                out.append(yz_modes(a, b, next_z))
            else:
                an, bn = shifted[c, s, tile(t)], shifted[c, s, pl.ds(start + 1, 8)]
                low, high, low_next, high_next = a + b, b - a, an + bn, bn - an
                out.append((low + low_next, low_next - low, high + high_next, high_next - high))
        return out

    def shift_own(ref):
        def step(t, carry):
            for c in range(3):
                for s in range(1, 1 + BX):
                    fz[c, s, tile(t)] = next_z(ref[c, s, tile(t)])
            return carry

        lax.fori_loop(0, 8, step, 0, unroll=4)

    def shift_halo(ref, high):
        for c in range(3):
            for s in range(BX + 1 + high):
                for t in (-1, 8) if 1 <= s <= BX else range(-1, 9):
                    fz[c, s, tile(t)] = next_z(ref[c, s, tile(t)])

    def edge_plane(edge, x):
        out = []
        for c in range(3):
            a = edge[c, x + XE]
            b = rot(jnp.where(row == 0, rot(a, -GROUP), a), -1, 0)
            out.append(yz_modes(a, b, next_z))
        return out

    def edge_down(value, _):
        down = rot(value, 1, 0)
        return jnp.where(row == 0, rot(down, GROUP), down)

    def tile(t):
        return pl.ds(pl.multiple_of(8 * t + 8, 8), 8)

    def brick(t):
        return pl.ds(pl.multiple_of(8 * t, 8), 8)

    outer = (lane == 0) | (lane == 127)

    def split(modes):
        ss, sd, ds, dd = modes
        return (ss - ds, sd - dd), (ss + ds, sd + dd)

    def parts_of(ref, t, first, last):
        xs = list(range(first, last + 2))
        return node_parts(
            (main_plane(ref, x + 1, t, fz) for x in xs), xs, lambda e: gm[0, e + 1, tile(t)]
        )

    def apply_inside(ref):
        for c in range(3):
            for x in range(BX):
                for which in range(2):
                    cy[0, c, x + 1, which] = zero

        def step(t, carry):
            for x, modes in parts_of(ref, t, 0, BX - 2):
                for c in range(3):
                    here, after = split(modes[c])
                    both = []
                    for which in range(2):
                        down = rot(after[which], 1, 0)
                        both.append(
                            here[which] + jnp.where(row == 0, cy[0, c, x + 1, which], down)
                        )
                        cy[0, c, x + 1, which] = down
                    img[c, x, brick(t)] = (both[0] - both[1]) + last_z(both[0] + both[1])
            return carry

        lax.fori_loop(0, 7, step, 0)

    def apply_rest(ref, edge, planes, tiles, use, use_edge=None):
        last = planes[-1]
        nodes = list(range(-1, last + 2))
        for x, modes in node_parts(
            (edge_plane(edge, x) for x in nodes), nodes, lambda e: ed[4, 0, e + XE]
        ):
            if x not in planes:
                continue
            for c in range(3):
                value = node_values(modes[c], edge_down, last_z)
                fx[c, x + XE] = jnp.where(pos == 3, rot(value, -6), value)
                if use_edge is not None:
                    use_edge(x, c, value)

        def emit(x, t, modes, inside, before):
            for c in range(3):
                both = []
                for which in range(2):
                    value, down = None, None
                    if modes is not None:
                        here, after = split(modes[c])
                        value, down = here[which], rot(after[which], 1, 0)
                    below = before(c, x, which)
                    if below is not None:
                        enter = jnp.where(row == 0, below, zero if down is None else down)
                    else:
                        enter = down
                    if enter is not None:
                        value = enter if value is None else value + enter
                    if down is not None:
                        cy[1, c, x + 1, which] = down
                    both.append(value)
                total = None
                if both[0] is not None:
                    total = (both[0] - both[1]) + last_z(both[0] + both[1])
                if inside:
                    partial = img[c, x, brick(t)]
                    total = partial if total is None else total + partial
                fixed = rot(fx[c, x + XE], lax.rem(254 - GROUP * (t + 1) - 1, 128))
                use(x, c, t, jnp.where(outer, fixed, total))

        groups = [(-1, -1), (BX - 1, last)]
        bound = [0] + list(range(BX - 1, last + 1))

        def edge_step(t, before):
            done = []
            for group in groups:
                for x, modes in parts_of(ref, t, *group):
                    if x in planes:
                        emit(x, t, modes, x < BX, before)
                        done.append(x)
            for x in planes:
                if x not in done:
                    emit(x, t, None, True, before)
            use(None, None, t, None)

        def full_step(t, before):
            for x, modes in parts_of(ref, t, -1, last):
                if x in planes:
                    emit(x, t, modes, False, before)
            use(None, None, t, None)

        for x, modes in parts_of(ref, -1, -1, last):
            if x in planes:
                for c in range(3):
                    after = split(modes[c])[1]
                    for which in range(2):
                        cy[1, c, x + 1, which] = rot(after[which], 1, 0)
        edge_step(0, lambda c, x, which: cy[1, c, x + 1, which])

        def chain(c, x, which):
            return cy[1, c, x + 1, which] if x in bound else None

        lax.fori_loop(1, 7, lambda t, carry: (edge_step(t, chain), carry)[1], 0, unroll=3)

        def join(c, x, which):
            value = cy[1, c, x + 1, which] if x in bound else None
            if x < BX:
                own = cy[0, c, x + 1, which]
                value = own if value is None else value + own
            return value

        full_step(7, join)
        for t in range(8, tiles):
            full_step(t, lambda c, x, which: cy[1, c, x + 1, which])

    weights = {}
    for a in range(3):
        for b in range(3):
            for c in range(3):
                weights[a, b, c] = max(0.0, 3.0 - math.sqrt(a * a + b * b + c * c))

    def combine_xy(planes, x):
        far = []
        for b in range(3):
            far.append(
                [
                    planes[x + 2][b],
                    planes[x + 1][b] + planes[x + 3][b],
                    planes[x][b] + planes[x + 4][b],
                ]
            )
        pair = {
            (0, 0): far[0][0],
            (0, 1): far[0][1] + far[1][0],
            (1, 1): far[1][1],
            (0, 2): far[0][2] + far[2][0],
            (1, 2): far[1][2] + far[2][1],
            (2, 2): far[2][2],
        }
        out = []
        for c in range(3):
            value = None
            for (a, b), term in pair.items():
                if weights[a, b, c] > 0.0:
                    term = weights[a, b, c] * term
                    value = term if value is None else value + term
            out.append(value)
        return out

    def filter_field(ref, halo, use):
        planes = []
        for s in range(8):
            value = halo[0, s]
            up, down = rot(value, -GROUP), rot(value, GROUP)
            one = rot(jnp.where(row == 0, up, value), -1, 0) + rot(
                jnp.where(row == 7, down, value), 1, 0
            )
            two = rot(jnp.where(row <= 1, up, value), -2, 0) + rot(
                jnp.where(row >= 6, down, value), 2, 0
            )
            planes.append((value, one, two))
        for x in range(BX):
            _, fx[1, x], fx[2, x] = combine_xy(planes, x)

        def step(t, carry):
            planes = []
            for s in range(8):
                rows = [ref[0, s, pl.ds(8 * t + 8 + off, 8)] for off in (-2, -1, 1, 2)]
                planes.append((ref[0, s, tile(t)], rows[1] + rows[2], rows[0] + rows[3]))
            shift = lax.rem(256 - GROUP * (t + 1) - 3, 128)
            for x in range(BX):
                value, one, two = combine_xy(planes, x)
                side = rot(fx[1, x], shift)
                value = value + rot(jnp.where(lane < 1, side, one), -1)
                value = value + rot(jnp.where(lane >= 127, side, one), 1)
                side = rot(fx[2, x], shift)
                value = value + rot(jnp.where(lane < 2, side, two), -2)
                value = value + rot(jnp.where(lane >= 126, side, two), 2)
                use(x, t, value)
            return carry

        lax.fori_loop(0, 8, step, 0, unroll=2)

    def reduce_start(k, value):
        ar_msg[k] = value
        ar[k, linear] = value

        steps = [
            (ox, oy, oz)
            for ox in range(nx)
            for oy in range(ny)
            for oz in range(nz)
            if (ox, oy, oz) != (0, 0, 0)
        ]
        steps.sort(key=lambda o: -sum(min(step, size - step) for step, size in zip(o, sizes)))
        for o in steps:
            pltpu.make_async_remote_copy(
                src_ref=ar_msg.at[k],
                dst_ref=ar.at[k, linear],
                send_sem=ar_ssem.at[k],
                recv_sem=ar_rsem.at[k],
                device_id=tuple(
                    lax.rem(m + step, size) if step else m for m, step, size in zip(me, o, sizes)
                ),
                device_id_type=MESH,
            ).start()

    def reduce_wait(k, sem):
        part = ar.at[k, pl.ds(0, count - 1)]
        pltpu.make_async_copy(part, part, sem.at[k]).wait()

    def reduce_total(k):
        reduce_wait(k, ar_rsem)
        return jnp.sum(ar[k], axis=0)


    copies[0].wait()
    copies[1].wait()
    for c in range(3):
        um[c, 1 : 1 + BX, 8 : 8 + BY] = um[c, 1 : 1 + BX, 8 : 8 + BY] * (1 - sup[...]).astype(f32)
    copies[2].wait()
    pack(0, [(dm, 2), (um, 1)])
    pl.semaphore_wait(barrier, greeted)
    first = messages(0, [(dm, 2, 2, 2), (um, 1, 1, 1)])
    send(packed(first))
    send(plain(first, 0))
    send(plain(first, 1))
    shift_own(um)

    def inside(coord, size):
        return ((coord >= 0) & (coord < size)).astype(f32)

    z_at = me[2] * BZ + lane
    z_terms = [
        jnp.ones((8, 128), f32),
        inside(z_at - 1, nz * BZ) + inside(z_at + 1, nz * BZ),
        inside(z_at - 2, nz * BZ) + inside(z_at + 2, nz * BZ),
    ]
    x_rows = []
    for x in range(BX):
        x_at = me[0] * BX + x
        x_terms = [
            f32(1.0),
            inside(x_at - 1, nx * BX) + inside(x_at + 1, nx * BX),
            inside(x_at - 2, nx * BX) + inside(x_at + 2, nx * BX),
        ]
        per_b = []
        for b in range(3):
            value = zero
            for c in range(3):
                value = value + z_terms[c] * sum(x_terms[a] * weights[a, b, c] for a in range(3))
            per_b.append(value)
        x_rows.append(per_b)

    def weigh(t, carry):
        y_at = me[1] * BY + 8 * t + row
        one = inside(y_at - 1, ny * BY) + inside(y_at + 1, ny * BY)
        two = inside(y_at - 2, ny * BY) + inside(y_at + 2, ny * BY)
        for x in range(BX):
            iw[x, brick(t)] = 1.0 / (x_rows[x][0] + one * x_rows[x][1] + two * x_rows[x][2])
        return carry

    lax.fori_loop(0, 8, weigh, 0, unroll=4)
    for copy in copies[3:]:
        copy.wait()

    receive(packed(first))
    receive(plain(first, 0))
    assemble(0, 1, 0, 4, range(-2, 6), qd)

    def to_modulus(x, t, total):
        at = brick(t)
        scale = iw[x, at]
        solid, void = sol[x, at] > 0, voi[x, at] > 0
        physical = jnp.where(solid, 1.0, jnp.where(void, 0.0, total * scale))
        square = physical * physical
        gm[0, 1 + x, tile(t)] = MU16 * EMIN + (MU16 * (1.0 - EMIN)) * (square * physical)
        co[x, at] = jnp.where(
            solid | void, 0.0, (-PENALTY * (1.0 - EMIN) * MU16) * (square * scale)
        )

    filter_field(dm, qd, to_modulus)
    second = messages(1, [(gm, 1, 1, 1)])
    send(plain(second))
    pack(1, [(gm, 1)])
    send(packed(second))
    apply_inside(um)
    receive(plain(first, 1))
    pack_around(um, 1, 1, range(-1, 5))
    assemble(0, 3, 1, 4, range(-1, 5), None, ed.at[0])
    shift_halo(um, 1)
    receive(plain(second))
    pack_around(gm, 1, 0, range(-1, 5))
    receive(packed(second))
    assemble(1, 1, 0, 1, range(-1, 5), None, ed.at[4])

    for x in range(BX):
        value = ed[4, 0, x + XE] + ed[4, 0, x + XE - 1]
        value = value + edge_down(value, 0)
        fxd[x] = value + last_z(value)

    def diagonal(t, carry):
        for x in range(BX):
            value = None
            for s in (x, x + 1):
                term = gm[0, s, tile(t)] + gm[0, s, pl.ds(8 * t + 7, 8)]
                value = term if value is None else value + term
            value = value + last_z(value)
            fixed = rot(fxd[x], lax.rem(256 - GROUP * (t + 1) - 9, 128))
            value = jnp.where(lane == 0, fixed, value)
            free = (1 - sup[x, brick(t)]).astype(f32)
            im[0, 1 + x, tile(t)] = free / (DIAG * value)
        return carry

    lax.fori_loop(0, 8, diagonal, 0, unroll=4)

    sums = {}
    acc_names = ("b0", "a00", "a01", "a11", "a12", "a22", "energy")
    for n, name in enumerate(acc_names):
        acc[n] = zero
        sums[name] = acc.at[n]

    def add(name, value):
        sums[name][...] = sums[name][...] + value

    kept = []

    def keep(name, value):
        kept.append((name, value))

    def flush():
        totals = {}
        for name, value in kept:
            totals[name] = value if name not in totals else totals[name] + value
        for name, value in totals.items():
            add(name, value)
        kept.clear()

    def from_start(x, c, t, image):
        if x is None:
            return flush()
        at = brick(t)
        free = (1 - sup[x, at]).astype(f32)
        load = lom[x, at].astype(f32)
        left = free * (load * loads[c, x, at] - image)
        value = im[0, 1 + x, tile(t)] * left
        vm0[c, 1 + x, tile(t)] = value
        keep("b0", left * value)

    def from_vector(source, target, diag_name, next_name):
        def use(x, c, t, image):
            if x is None:
                return flush()
            here = source[c, 1 + x, tile(t)]
            value = im[0, 1 + x, tile(t)] * image - THETA * here
            target[c, 1 + x, tile(t)] = value
            if x < BX and not (isinstance(t, int) and t >= 8):
                keep(diag_name, here * image)
                keep(next_name, value * image)

        return use

    own = list(range(BX))
    third = messages(2, [(vm0, 1, 1, 1), (im, 1, 0, 1)])
    send(plain(third, 1))
    apply_rest(um, ed.at[0], own, 8, from_start)
    send(plain(third, 0))
    pack(2, [(vm0, 1), (im, 1)])
    send(packed(third))
    shift_own(vm0)
    apply_inside(vm0)
    receive(plain(third))
    pack_around(vm0, 1, 0, range(-1, 5))
    pack_around(im, 1, 3, range(0, 5))
    shift_halo(vm0, 1)
    receive(packed(third))
    assemble(2, 3, 0, 4, range(-1, 5), None, ed.at[1])
    assemble(2, 1, 3, 4, range(0, 5), None, ed.at[5])
    apply_rest(vm0, ed.at[1], own, 8, from_vector(vm0, vm1, "a00", "a01"))
    fourth = messages(3, [(vm1, 1, 1, 2)])
    send(plain(fourth))
    pack(3, [(vm1, 1)])
    send(packed(fourth))
    shift_own(vm1)
    apply_inside(vm1)
    receive(plain(fourth))
    pack_around(vm1, 1, 0, range(-1, 6))
    shift_halo(vm1, 2)
    receive(packed(fourth))
    assemble(3, 3, 0, 3, range(-1, 6), None, ed.at[2])

    def edge_vector(x, c, image):
        ed[3, c, x + XE] = ed[5, 0, x + XE] * image - THETA * ed[2, c, x + XE]

    apply_rest(
        vm1, ed.at[2], own + [BX], 9, from_vector(vm1, vm2, "a11", "a12"), edge_vector
    )

    def energies(planes):
        before = None
        for index, plane in enumerate(planes):
            if before is not None:
                yield index - 1, mode_energy(x_modes(before, plane))
            before = plane

    column = (pos == 2) & (lane >= GROUP) & (lane < 9 * GROUP)

    edge_sum = zero
    for x, value in energies(edge_plane(ed.at[3], x) for x in range(BX + 1)):
        edge_sum = edge_sum + jnp.where(column, ed[4, 0, x + XE] * value, 0.0)

    def last_moment(t, carry):
        total = zero
        for x, value in energies(main_plane(vm2, x + 1, t) for x in range(BX + 1)):
            total = total + gm[0, 1 + x, tile(t)] * value
        add("a22", jnp.where(lane < 127, total, 0.0))
        return carry

    add("a22", edge_sum)
    lax.fori_loop(0, 8, last_moment, 0, unroll=4)

    message = jnp.zeros((1, 128), f32)
    lane1 = lax.broadcasted_iota(jnp.int32, (1, 128), 1)
    for n, name in enumerate(acc_names[:6]):
        part = jnp.sum(jnp.sum(sums[name][...], axis=0, keepdims=True), axis=1, keepdims=True)
        message = jnp.where(lane1 == n, part, message)
    reduce_start(0, message)
    for msgs in (first, second, third, fourth):
        sent(msgs)
    totals = reduce_total(0)
    b0, a00, a01, a11, a12, a22 = (
        jnp.broadcast_to(totals[:, n : n + 1], (1, 128)) for n in range(6)
    )
    tiny = 1e-6
    b1 = a00 - THETA * b0
    b2 = a01 - THETA * b1
    l10, l20 = a01 / a00, a11 / a00
    d1 = a11 - l10 * a01
    ok1 = d1 > tiny * a11
    safe1 = jnp.where(ok1, d1, 1.0)
    cross = a12 - l20 * a01
    l21 = jnp.where(ok1, cross / safe1, 0.0)
    d2 = a22 - l20 * a11 - l21 * cross
    ok2 = ok1 & (d2 > tiny * a22)
    y1 = b1 - l10 * b0
    y2 = b2 - l20 * b0 - l21 * y1
    c2 = jnp.where(ok2, y2 / jnp.where(ok2, d2, 1.0), 0.0)
    c1 = jnp.where(ok1, y1 / safe1, 0.0) - l21 * c2
    c0 = b0 / a00 - l10 * c1 - l20 * c2
    c0, c1, c2 = (jnp.broadcast_to(c, (8, 128)) for c in (c0, c1, c2))

    for c in range(3):
        for x in range(BX + 1):
            s = x + XE
            ed[0, c, s] = ed[0, c, s] + (
                c0 * ed[1, c, s] + c1 * ed[2, c, s] + c2 * ed[3, c, s]
            )

    def combine(t, carry):
        for c in range(3):
            for s in range(1, BX + 2):
                at = brick(t + 1)
                um[c, s, at] = um[c, s, at] + (
                    c0 * vm0[c, s, at] + c1 * vm1[c, s, at] + c2 * vm2[c, s, at]
                )
        return carry

    lax.fori_loop(0, 9, combine, 0)
    disp = pltpu.make_async_copy(um.at[:, pl.ds(1, BX), own_rows], disp_out, out_sem.at[0])
    disp.start()

    for x, value in energies(edge_plane(ed.at[0], x) for x in range(BX + 1)):
        fxd[x] = value

    def sensitivity(t, carry):
        total = zero
        for x, value in energies(main_plane(um, x + 1, t) for x in range(BX + 1)):
            fixed = rot(fxd[x], lax.rem(253 - GROUP * (t + 1), 128))
            value = jnp.where(lane == 127, fixed, value)
            total = total + gm[0, 1 + x, tile(t)] * value
            sn[0, 2 + x, tile(t)] = co[x, brick(t)] * value
        add("energy", total)
        return carry

    lax.fori_loop(0, 8, sensitivity, 0, unroll=4)
    fifth = messages(4, [(sn, 2, 2, 2)])
    send(plain(fifth))
    pack(4, [(sn, 2)])
    send(packed(fifth))
    part = jnp.sum(jnp.sum(sums["energy"][...], axis=0, keepdims=True), axis=1, keepdims=True)
    reduce_start(1, jnp.broadcast_to(part, (1, 128)))
    receive(fifth)
    assemble(4, 1, 0, 1, range(-2, 6), qd)

    def finish(x, t, total):
        dsens_out[x, brick(t)] = total

    filter_field(sn, qd, finish)
    comp_out[...] = reduce_total(1)
    sent(fifth)
    for k in range(2):
        reduce_wait(k, ar_ssem)
    disp.wait()


def call(sizes, *args):
    count = sizes[0] * sizes[1] * sizes[2]
    main3 = pltpu.VMEM((3, 7, 88, 128), f32)
    wide = pltpu.VMEM((1, 8, 80, 128), f32)
    brick = pltpu.VMEM((BX, BY, BZ), f32)
    mask = pltpu.VMEM((BX, BY, BZ), jnp.int32)
    any_spec = pl.BlockSpec(memory_space=pl.ANY)
    displacement, sensitivity, compliance = pl.pallas_call(
        functools.partial(body, sizes),
        out_shape=(
            pltpu.VMEM((3, BX, BY, BZ), f32),
            pltpu.VMEM((BX, BY, BZ), f32),
            jax.ShapeDtypeStruct((1, 128), f32),
        ),
        in_specs=[any_spec] * 7,
        out_specs=(pl.BlockSpec(memory_space=pltpu.VMEM),) * 3,
        scratch_shapes=[
            wide, main3, main3, main3, main3, pltpu.VMEM((1, 6, 80, 128), f32),
            pltpu.VMEM((1, 7, 80, 128), f32), wide,
            mask, mask, mask, mask, pltpu.VMEM((3, BX, BY, BZ), f32),
            brick, brick, main3, pltpu.VMEM((3, BX, BY, BZ), f32), pltpu.VMEM((8, 8, 128), f32),
            pltpu.VMEM((5, 4, NE, 8, 128), f32),
            pltpu.VMEM((5, 2, 4, NE, 8, 128), f32),
            pltpu.VMEM((4, NE, 8, 128), f32),
            pltpu.VMEM((5, 2, 8, 128), f32),
            pltpu.VMEM((5, 3, 2, 2, 8, 128), f32),
            pltpu.VMEM((6, 3, NE, 8, 128), f32),
            pltpu.VMEM((1, NE, 8, 128), f32),
            pltpu.VMEM((3, NE, 8, 128), f32),
            pltpu.VMEM((BX, 8, 128), f32),
            pltpu.VMEM((2, 3, 7, 2, 8, 128), f32),
            pltpu.VMEM((2, count, 1, 128), f32),
            pltpu.VMEM((2, 1, 128), f32),
            pltpu.SemaphoreType.DMA((7,)),
            pltpu.SemaphoreType.DMA((1,)),
            pltpu.SemaphoreType.DMA((5, 34)),
            pltpu.SemaphoreType.DMA((5, 34)),
            pltpu.SemaphoreType.DMA((2,)),
            pltpu.SemaphoreType.DMA((2,)),
        ],
        compiler_params=pltpu.CompilerParams(
            collective_id=0, has_side_effects=True, vmem_limit_bytes=60 * 2**20
        ),
    )(*args)
    return displacement, sensitivity, compliance[0, 0]


def solution(mesh):
    sizes = tuple(mesh.shape[axis] for axis in AXES)
    block, field = P("gx", "gy", "gz"), P(None, "gx", "gy", "gz")
    return jax.shard_map(
        functools.partial(call, sizes),
        mesh=mesh,
        in_specs=(block,) * 5 + (field,) * 2,
        out_specs=(field, block, P()),
        check_vma=False,
    )
```

```python
import functools
import itertools
import math

import jax
import jax.numpy as jnp
from jax import lax
from jax.experimental import pallas as pl
from jax.experimental.pallas import tpu as pltpu
from jax.sharding import PartitionSpec as P

MESH = pl.DeviceIdType.MESH
AXES = ("gx", "gy", "gz")

EMIN = 0.001
PENALTY = 3.0
THETA = 1.5
MU16 = 1.0 / (2.6 * 16.0)
DIAG = 88.0 / 9.0

BX, BY, BZ = 4, 64, 128
GROUP = 12
FACES, CORNERS = 2, 3
XE = 2
NE = 8

f32 = jnp.float32

DIRECTIONS = sorted(
    [
        (dx, dy, dz)
        for dx in (0, 1, -1)
        for dy in (0, 1, -1)
        for dz in (0, 1, -1)
        if (dx, dy, dz) != (0, 0, 0)
    ],
    key=lambda d: (d[1:] != (0, 0), -sum(abs(step) for step in d)),
)


def iota(dim):
    return lax.broadcasted_iota(jnp.int32, (8, 128), dim)


def lane_pos():
    lane = iota(1)
    return lane - GROUP * ((lane * 43) >> 9)


def rot(value, shift, axis=1):
    size = value.shape[axis]
    return pltpu.roll(value, shift % size, axis)


def yz_modes(a, b, next_z):
    low, high = a + b, b - a
    low_next, high_next = next_z(low), next_z(high)
    return (low + low_next, low_next - low, high + high_next, high_next - high)


def x_modes(near, far):
    return [
        [None if m == 0 else n[m] + f[m] for m in range(4)] + [f[m] - n[m] for m in range(4)]
        for n, f in zip(near, far)
    ]


def mode_forces(q, g):
    u, v, w = q
    force = [[None] * 8 for _ in range(3)]
    trace = 1.5 * (u[4] + v[2] + w[1])
    force[0][4] = g * (trace + (u[4] + u[4]))
    force[1][2] = g * (trace + (v[2] + v[2]))
    force[2][1] = g * (trace + (w[1] + w[1]))
    for (ca, ma), (cb, mb) in (((0, 2), (1, 4)), ((1, 1), (2, 2)), ((0, 1), (2, 4))):
        shear = g * (q[ca][ma] + q[cb][mb])
        force[ca][ma] = shear
        force[cb][mb] = shear
    for (ca, ma), (cb, mb) in (((1, 6), (2, 5)), ((0, 6), (2, 3)), ((0, 5), (1, 3))):
        half = 0.5 * (q[ca][ma] + q[cb][mb])
        force[ca][ma] = g * (q[ca][ma] + half)
        force[cb][mb] = g * (q[cb][mb] + half)
    third = g * (1.0 / 3.0)
    total = u[3] + v[5] + w[6]
    force[0][3] = third * (u[3] + total)
    force[1][5] = third * (v[5] + total)
    force[2][6] = third * (w[6] + total)
    last = g * (5.5 / 9.0)
    for c in range(3):
        force[c][7] = last * q[c][7]
    return force


def mode_energy(q):
    u, v, w = q
    trace = u[4] + v[2] + w[1]
    total = 1.5 * (trace * trace) + 2.0 * (u[4] * u[4] + v[2] * v[2] + w[1] * w[1])
    for (ca, ma), (cb, mb) in (((0, 2), (1, 4)), ((1, 1), (2, 2)), ((0, 1), (2, 4))):
        shear = q[ca][ma] + q[cb][mb]
        total = total + shear * shear
    for (ca, ma), (cb, mb) in (((1, 6), (2, 5)), ((0, 6), (2, 3)), ((0, 5), (1, 3))):
        both = q[ca][ma] + q[cb][mb]
        total = total + (q[ca][ma] * q[ca][ma] + q[cb][mb] * q[cb][mb] + 0.5 * (both * both))
    both = u[3] + v[5] + w[6]
    total = total + (1.0 / 3.0) * (u[3] * u[3] + v[5] * v[5] + w[6] * w[6] + both * both)
    last = u[7] * u[7] + v[7] * v[7] + w[7] * w[7]
    return total + (5.5 / 9.0) * last


def node_parts(planes, xs, moduli):
    before, kept = None, None
    for index, plane in enumerate(planes):
        if before is not None:
            force = mode_forces(x_modes(before, plane), moduli(xs[index - 1]))
            right = [[-f[4] if m == 0 else f[m] - f[4 + m] for m in range(4)] for f in force]
            left = [[f[4] if m == 0 else f[m] + f[4 + m] for m in range(4)] for f in force]
            if kept is not None:
                right = [[k + r for k, r in zip(ks, rs)] for ks, rs in zip(kept, right)]
            yield xs[index - 1], right
            kept = left
        before = plane
    yield xs[-1], kept


def node_values(modes, shift_y, shift_z):
    ss, sd, ds, dd = modes
    low = (ss - ds) + shift_y(ss + ds, 0)
    high = (sd - dd) + shift_y(sd + dd, 1)
    return (low - high) + shift_z(low + high)


def body(
    sizes,
    design_in, support_in, load_in, solid_in, void_in, loads_in, start_in,
    disp_out, dsens_out, comp_out,
    dm, um, vm0, vm1, vm2, gm, im, sn, sup, lom, sol, voi, loads, iw, co, fz, img, acc,
    dummy, pa, pz, po, ko, kr, ed, qd, fx, fxd, cy, ar, ar_msg,
    in_sem, out_sem, ssem, rsem, ar_ssem, ar_rsem,
):
    nx, ny, nz = sizes
    count = nx * ny * nz
    me = [lax.axis_index(a) for a in AXES]
    linear = (me[0] * ny + me[1]) * nz + me[2]
    lane, row, pos = iota(1), iota(0), lane_pos()
    pos6 = jnp.where(pos < 6, pos, pos - 6)
    own_rows = pl.ds(8, BY)
    zero = jnp.zeros((8, 128), f32)

    def tile(t):
        return pl.ds(pl.multiple_of(8 * t + 8, 8), 8)

    def brick(t):
        return pl.ds(pl.multiple_of(8 * t, 8), 8)

    copies = [
        pltpu.make_async_copy(src, dst, in_sem.at[i])
        for i, (src, dst) in enumerate(
            (
                (start_in, um.at[:, pl.ds(1, BX), own_rows]),
                (support_in, sup),
                (design_in, dm.at[0, pl.ds(2, BX), own_rows]),
                (solid_in, sol),
                (void_in, voi),
                (load_in, lom),
                (loads_in, loads),
            )
        )
    ]
    for copy in copies:
        copy.start()

    def clear_main(*refs):
        def sides(t, carry):
            for ref, xo, slots in refs:
                for c in range(ref.shape[0]):
                    for s in [*range(xo), *range(xo + BX, slots)]:
                        ref[c, s, brick(t)] = zero
            return carry

        def ends(s, carry):
            for ref, xo, _ in refs:
                for c in range(ref.shape[0]):
                    for t in (0, 9):
                        ref[c, xo + s, 8 * t : 8 * t + 8] = zero
            return carry

        lax.fori_loop(0, 10, sides, 0)
        lax.fori_loop(0, BX, ends, 0)

    def clear_edges(k):
        def planes(s, carry):
            for side in range(2):
                for c in range(4):
                    pz[k, side, c, s] = zero
            return carry

        def corners(a, carry):
            for b in range(2):
                for d in range(2):
                    kr[k, a, b, d] = zero
            return carry

        lax.fori_loop(0, NE, planes, 0)
        lax.fori_loop(0, 3, corners, 0)

    clear_main((dm, 2, 8), (um, 1, 7))
    clear_edges(0)

    def exists(d, sign):
        ok = None
        for m, step, size in zip(me, d, sizes):
            if step * sign > 0:
                here = m < size - abs(step)
            elif step * sign < 0:
                here = m >= abs(step)
            else:
                continue
            ok = here if ok is None else ok & here
        return ok

    barrier = pltpu.get_barrier_semaphore()

    greeted = 0
    for d in DIRECTIONS + [(0, 0, 4), (0, 0, -4)]:
        there = exists(d, 1)

        @pl.when(there)
        def _(d=d):
            pl.semaphore_signal(
                barrier,
                inc=1,
                device_id=tuple(m + step for m, step in zip(me, d)),
                device_id_type=MESH,
            )

        greeted = greeted + jnp.where(there, 1, 0)

    clear_main((sn, 2, 8), (gm, 1, 6), (vm0, 1, 7), (vm1, 1, 7), (im, 1, 7))
    lax.fori_loop(1, pz.shape[0], lambda k, carry: (clear_edges(k), carry)[1], 0)

    def clear_last(s, carry):
        for c in range(3):
            vm1[c, s, 80:88] = zero
        return carry

    lax.fori_loop(0, 7, clear_last, 0)

    def group_mask(t, first, last):
        return (lane >= GROUP * (t + 1) + first) & (lane < GROUP * (t + 1) + last)

    def pack_tiles(tiles, base):
        for t, tile in tiles:
            base = jnp.where(group_mask(t, 0, 6), rot(tile, GROUP * (t + 1) + 3), base)
        return base

    def pack_corners(k, fields):
        comp, total = 0, sum(ref.shape[0] for ref, _ in fields)
        corner = [zero, zero]
        for ref, xo in fields:
            for c in range(ref.shape[0]):
                for x in range(BX):
                    i = 6 * (x * total + comp)
                    for side, t in ((0, 0), (1, 7)):
                        corner[side] = jnp.where(
                            (lane >= i) & (lane < i + 6),
                            rot(ref[c, x + xo, 8 * t + 8 : 8 * t + 16], i + 3),
                            corner[side],
                        )
                comp += 1
        for side in range(2):
            ko[k, side] = corner[side]

    def pack(k, fields):
        comp = 0
        for ref, xo in fields:
            for c in range(ref.shape[0]):
                for x in range(BX):
                    pa[k, comp, x + XE] = pack_tiles(
                        [(t, ref[c, x + xo, 8 * t + 8 : 8 * t + 16]) for t in range(8)], zero
                    )
                comp += 1

    def messages(k, fields):
        comps = sum(f[0].shape[0] for f in fields)
        low, high = max(f[2] for f in fields), max(f[3] for f in fields)
        result = []
        for d in DIRECTIONS:
            dx, dy, dz = d
            if (1 in d and low == 0) or (-1 in d and high == 0):
                continue
            parts = []
            if dz == 0:
                for n, (ref, xo, lo, hi) in enumerate(fields):
                    if (1 in d and lo == 0) or (-1 in d and hi == 0):
                        continue
                    if dx == 1:
                        xs, xd = pl.ds(xo + BX - lo, lo), pl.ds(xo - lo, lo)
                    elif dx == -1:
                        xs, xd = pl.ds(xo, hi), pl.ds(xo + BX, hi)
                    else:
                        xs = xd = pl.ds(xo, BX)
                    if dy == 1:
                        ys, yd = pl.ds(BY, 8), pl.ds(0, 8)
                    elif dy == -1:
                        ys, yd = pl.ds(8, 8), pl.ds(BY + 8, 8)
                    else:
                        ys = yd = own_rows
                    parts.append((n, ref.at[:, xs, ys], ref.at[:, xd, yd]))
            elif dy == 0:
                if dx == 1:
                    xs, xd = pl.ds(XE + BX - low, low), pl.ds(XE - low, low)
                elif dx == -1:
                    xs, xd = pl.ds(XE, high), pl.ds(XE + BX, high)
                else:
                    xs = xd = pl.ds(XE, BX)
                side, cs = 0 if dz == 1 else 1, pl.ds(0, comps)
                parts.append((FACES, pa.at[k, cs, xs], pz.at[k, side, cs, xd]))
            else:
                own = ko.at[k, 0 if dy == -1 else 1]
                there = kr.at[k, 1 - dx, 0 if dy == 1 else 1, 0 if dz == 1 else 1]
                parts.append((CORNERS, own, there))
            for n, src, dst in parts:
                copy = pltpu.make_async_remote_copy(
                    src_ref=src,
                    dst_ref=dst,
                    send_sem=ssem.at[k],
                    recv_sem=rsem.at[k, n],
                    device_id=tuple(m + step for m, step in zip(me, d)),
                    device_id_type=MESH,
                )
                result.append((d, n, copy, math.prod(src.shape) // 128))
        return result

    def send(msgs):
        for d in DIRECTIONS:
            group = [m[2] for m in msgs if m[0] == d]
            if group:
                @pl.when(exists(d, 1))
                def _(group=group):
                    for copy in group:
                        copy.start()

    def wait_rows(msgs, sign, sem):
        kinds = [
            [(False, False)] if size == 1
            else [(False, True), (True, False)] + [(True, True)] * (size > 2)
            for size in sizes
        ]
        totals = set()
        for pattern in itertools.product(*kinds):
            rows = 0
            for d, _, _, n in msgs:
                if all(step == 0 or has[step * sign > 0] for step, has in zip(d, pattern)):
                    rows += n
            totals.add(rows)
        rows = 0
        for d in DIRECTIONS:
            n = sum(m[3] for m in msgs if m[0] == d)
            if n:
                rows = rows + jnp.where(exists(d, sign), n, 0)
        for total in sorted(totals - {0}):
            @pl.when(rows == total)
            def _(total=total):
                part = dummy.at[pl.ds(0, total)]
                pltpu.make_async_copy(part, part, sem).wait()

    def receive(msgs, k):
        for n in sorted({m[1] for m in msgs}):
            wait_rows([m for m in msgs if m[1] == n], -1, rsem.at[k, n])

    def sent(msgs, k):
        wait_rows(msgs, 1, ssem.at[k])

    def plain(msgs, n=None):
        return [m for m in msgs if m[1] < FACES and n in (None, m[1])]

    def packed(msgs, n=None):
        return [m for m in msgs if m[1] >= FACES and n in (None, m[1])]

    def send_all(msgs, k, fields, first=()):
        send(first)
        pack_corners(k, fields)
        send(packed(msgs, CORNERS))
        pack(k, fields)
        send(packed(msgs, FACES))

    def pack_around(ref, xo, first_comp, planes):
        for x in planes:
            for c in range(ref.shape[0]):
                outside = x < 0 or x >= BX
                po[first_comp + c, x + XE] = pack_tiles(
                    [
                        (t, ref[c, x + xo, 8 * t + 8 : 8 * t + 16])
                        for t in (range(-1, 9) if outside else (-1, 8))
                    ],
                    zero,
                )

    def assemble(k, count, first_comp, comps, planes, halo, edge=None):
        items = [(c, x) for x in planes for c in range(count)]
        around = {}
        for _, x in items:
            side = 0 if x < 0 else 2 if x >= BX else 1
            for end in range(2):
                if (side, end) not in around:
                    around[side, end] = jnp.where(pos6 < 3, kr[k, side, end, 0], kr[k, side, end, 1])
        inner = (lane >= GROUP) & (lane < 9 * GROUP)
        for c, x in items:
            comp = first_comp + c
            side = 0 if x < 0 else 2 if x >= BX else 1
            i = 6 * (x % BX * comps + comp)
            value = jnp.where(pos < 3, pz[k, 0, comp, x + XE], pz[k, 1, comp, x + XE])
            value = jnp.where(lane < 6, rot(around[side, 0], -i), value)
            value = jnp.where(group_mask(8, 0, 6), rot(around[side, 1], 9 * GROUP - i), value)
            if halo is not None:
                halo[c, x + XE] = value
            if edge is not None:
                own = po[comp, x + XE]
                if side == 1:
                    own = jnp.where(inner, pa[k, comp, x + XE], own)
                high = rot(jnp.where(pos < 3, value, own), 6)
                low = jnp.where(pos < 3, own, value)
                edge[c, x + XE] = jnp.where(pos < 6, low, high)

    def next_z(value):
        return rot(value, -1)

    def last_z(value):
        return rot(value, 1)

    def main_plane(ref, s, t, shifted=None):
        start = 8 * t + 8
        out = []
        for c in range(3):
            a, b = ref[c, s, tile(t)], ref[c, s, pl.ds(start + 1, 8)]
            if shifted is None:
                out.append(yz_modes(a, b, next_z))
            else:
                an, bn = shifted[c, s, tile(t)], shifted[c, s, pl.ds(start + 1, 8)]
                low, high, low_next, high_next = a + b, b - a, an + bn, bn - an
                out.append((low + low_next, low_next - low, high + high_next, high_next - high))
        return out

    def shift_own(ref):
        def step(t, carry):
            for c in range(3):
                for s in range(1, 1 + BX):
                    fz[c, s, tile(t)] = next_z(ref[c, s, tile(t)])
            return carry

        lax.fori_loop(0, 8, step, 0, unroll=4)

    def shift_halo(ref, high):
        for c in range(3):
            for s in range(BX + 1 + high):
                for t in (-1, 8) if 1 <= s <= BX else range(-1, 9):
                    fz[c, s, tile(t)] = next_z(ref[c, s, tile(t)])

    def edge_plane(edge, x):
        out = []
        for c in range(3):
            a = edge[c, x + XE]
            b = rot(jnp.where(row == 0, rot(a, -GROUP), a), -1, 0)
            out.append(yz_modes(a, b, next_z))
        return out

    def edge_down(value, _):
        down = rot(value, 1, 0)
        return jnp.where(row == 0, rot(down, GROUP), down)

    outer = (lane == 0) | (lane == 127)

    def split(modes):
        ss, sd, ds, dd = modes
        return (ss - ds, sd - dd), (ss + ds, sd + dd)

    def parts_of(ref, t, first, last):
        xs = list(range(first, last + 2))
        return node_parts(
            (main_plane(ref, x + 1, t, fz) for x in xs), xs, lambda e: gm[0, e + 1, tile(t)]
        )

    def apply_inside(ref):
        for c in range(3):
            for x in range(BX):
                for which in range(2):
                    cy[0, c, x + 1, which] = zero

        def step(t, carry):
            for x, modes in parts_of(ref, t, 0, BX - 2):
                for c in range(3):
                    here, after = split(modes[c])
                    both = []
                    for which in range(2):
                        down = rot(after[which], 1, 0)
                        both.append(
                            here[which] + jnp.where(row == 0, cy[0, c, x + 1, which], down)
                        )
                        cy[0, c, x + 1, which] = down
                    img[c, x, brick(t)] = (both[0] - both[1]) + last_z(both[0] + both[1])
            return carry

        lax.fori_loop(0, 7, step, 0)

    def apply_rest(ref, edge, planes, tiles, use, use_edge=None):
        last = planes[-1]
        nodes = list(range(-1, last + 2))
        for x, modes in node_parts(
            (edge_plane(edge, x) for x in nodes), nodes, lambda e: ed[4, 0, e + XE]
        ):
            if x not in planes:
                continue
            for c in range(3):
                value = node_values(modes[c], edge_down, last_z)
                fx[c, x + XE] = jnp.where(pos == 3, rot(value, -6), value)
                if use_edge is not None:
                    use_edge(x, c, value)

        def emit(x, t, modes, inside, before):
            for c in range(3):
                both = []
                for which in range(2):
                    value, down = None, None
                    if modes is not None:
                        here, after = split(modes[c])
                        value, down = here[which], rot(after[which], 1, 0)
                    below = before(c, x, which)
                    if below is not None:
                        enter = jnp.where(row == 0, below, zero if down is None else down)
                    else:
                        enter = down
                    if enter is not None:
                        value = enter if value is None else value + enter
                    if down is not None:
                        cy[1, c, x + 1, which] = down
                    both.append(value)
                total = None
                if both[0] is not None:
                    total = (both[0] - both[1]) + last_z(both[0] + both[1])
                if inside:
                    partial = img[c, x, brick(t)]
                    total = partial if total is None else total + partial
                fixed = rot(fx[c, x + XE], lax.rem(254 - GROUP * (t + 1) - 1, 128))
                use(x, c, t, jnp.where(outer, fixed, total))

        groups = [(-1, -1), (BX - 1, last)]
        bound = [0] + list(range(BX - 1, last + 1))

        def edge_step(t, before):
            done = []
            for group in groups:
                for x, modes in parts_of(ref, t, *group):
                    if x in planes:
                        emit(x, t, modes, x < BX, before)
                        done.append(x)
            for x in planes:
                if x not in done:
                    emit(x, t, None, True, before)
            use(None, None, t, None)

        def full_step(t, before):
            for x, modes in parts_of(ref, t, -1, last):
                if x in planes:
                    emit(x, t, modes, False, before)
            use(None, None, t, None)

        for x, modes in parts_of(ref, -1, -1, last):
            if x in planes:
                for c in range(3):
                    after = split(modes[c])[1]
                    for which in range(2):
                        cy[1, c, x + 1, which] = rot(after[which], 1, 0)
        edge_step(0, lambda c, x, which: cy[1, c, x + 1, which])

        def chain(c, x, which):
            return cy[1, c, x + 1, which] if x in bound else None

        lax.fori_loop(1, 7, lambda t, carry: (edge_step(t, chain), carry)[1], 0, unroll=3)

        def join(c, x, which):
            value = cy[1, c, x + 1, which] if x in bound else None
            if x < BX:
                own = cy[0, c, x + 1, which]
                value = own if value is None else value + own
            return value

        full_step(7, join)
        for t in range(8, tiles):
            full_step(t, lambda c, x, which: cy[1, c, x + 1, which])

    weights = {}
    for a in range(3):
        for b in range(3):
            for c in range(3):
                weights[a, b, c] = max(0.0, 3.0 - math.sqrt(a * a + b * b + c * c))

    def combine_xy(planes, x):
        far = []
        for b in range(3):
            far.append(
                [
                    planes[x + 2][b],
                    planes[x + 1][b] + planes[x + 3][b],
                    planes[x][b] + planes[x + 4][b],
                ]
            )
        pair = {
            (0, 0): far[0][0],
            (0, 1): far[0][1] + far[1][0],
            (1, 1): far[1][1],
            (0, 2): far[0][2] + far[2][0],
            (1, 2): far[1][2] + far[2][1],
            (2, 2): far[2][2],
        }
        out = []
        for c in range(3):
            value = None
            for (a, b), term in pair.items():
                if weights[a, b, c] > 0.0:
                    term = weights[a, b, c] * term
                    value = term if value is None else value + term
            out.append(value)
        return out

    def filter_field(ref, halo, use):
        planes = []
        for s in range(8):
            value = halo[0, s]
            up, down = rot(value, -GROUP), rot(value, GROUP)
            one = rot(jnp.where(row == 0, up, value), -1, 0) + rot(
                jnp.where(row == 7, down, value), 1, 0
            )
            two = rot(jnp.where(row <= 1, up, value), -2, 0) + rot(
                jnp.where(row >= 6, down, value), 2, 0
            )
            planes.append((value, one, two))
        for x in range(BX):
            _, fx[1, x], fx[2, x] = combine_xy(planes, x)

        def step(t, carry):
            planes = []
            for s in range(8):
                rows = [ref[0, s, pl.ds(8 * t + 8 + off, 8)] for off in (-2, -1, 1, 2)]
                planes.append((ref[0, s, tile(t)], rows[1] + rows[2], rows[0] + rows[3]))
            shift = lax.rem(256 - GROUP * (t + 1) - 3, 128)
            for x in range(BX):
                value, one, two = combine_xy(planes, x)
                side = rot(fx[1, x], shift)
                value = value + rot(jnp.where(lane < 1, side, one), -1)
                value = value + rot(jnp.where(lane >= 127, side, one), 1)
                side = rot(fx[2, x], shift)
                value = value + rot(jnp.where(lane < 2, side, two), -2)
                value = value + rot(jnp.where(lane >= 126, side, two), 2)
                use(x, t, value)
            return carry

        lax.fori_loop(0, 8, step, 0, unroll=2)

    def reduce_start(k, value):
        ar_msg[k] = value
        ar[k, linear] = value

        steps = [
            (ox, oy, oz)
            for ox in range(nx)
            for oy in range(ny)
            for oz in range(nz)
            if (ox, oy, oz) != (0, 0, 0)
        ]
        steps.sort(key=lambda o: -sum(min(step, size - step) for step, size in zip(o, sizes)))
        for o in steps:
            pltpu.make_async_remote_copy(
                src_ref=ar_msg.at[k],
                dst_ref=ar.at[k, linear],
                send_sem=ar_ssem.at[k],
                recv_sem=ar_rsem.at[k],
                device_id=tuple(
                    lax.rem(m + step, size) if step else m for m, step, size in zip(me, o, sizes)
                ),
                device_id_type=MESH,
            ).start()

    def reduce_wait(k, sem):
        part = ar.at[k, pl.ds(0, count - 1)]
        pltpu.make_async_copy(part, part, sem.at[k]).wait()

    def reduce_total(k):
        reduce_wait(k, ar_rsem)
        return jnp.sum(ar[k], axis=0)


    copies[0].wait()
    copies[1].wait()
    for c in range(3):
        um[c, 1 : 1 + BX, 8 : 8 + BY] = um[c, 1 : 1 + BX, 8 : 8 + BY] * (1 - sup[...]).astype(f32)
    copies[2].wait()
    pack_corners(0, [(dm, 2), (um, 1)])
    pack(0, [(dm, 2), (um, 1)])
    pl.semaphore_wait(barrier, greeted)
    first = messages(0, [(dm, 2, 2, 2), (um, 1, 1, 1)])
    send(packed(first))
    send(plain(first, 0))
    send(plain(first, 1))
    shift_own(um)

    def inside(coord, size):
        return ((coord >= 0) & (coord < size)).astype(f32)

    z_at = me[2] * BZ + lane
    z_terms = [
        jnp.ones((8, 128), f32),
        inside(z_at - 1, nz * BZ) + inside(z_at + 1, nz * BZ),
        inside(z_at - 2, nz * BZ) + inside(z_at + 2, nz * BZ),
    ]
    x_rows = []
    for x in range(BX):
        x_at = me[0] * BX + x
        x_terms = [
            f32(1.0),
            inside(x_at - 1, nx * BX) + inside(x_at + 1, nx * BX),
            inside(x_at - 2, nx * BX) + inside(x_at + 2, nx * BX),
        ]
        per_b = []
        for b in range(3):
            value = zero
            for c in range(3):
                value = value + z_terms[c] * sum(x_terms[a] * weights[a, b, c] for a in range(3))
            per_b.append(value)
        x_rows.append(per_b)

    def weigh(t, carry):
        y_at = me[1] * BY + 8 * t + row
        one = inside(y_at - 1, ny * BY) + inside(y_at + 1, ny * BY)
        two = inside(y_at - 2, ny * BY) + inside(y_at + 2, ny * BY)
        for x in range(BX):
            iw[x, brick(t)] = 1.0 / (x_rows[x][0] + one * x_rows[x][1] + two * x_rows[x][2])
        return carry

    lax.fori_loop(0, 8, weigh, 0, unroll=4)
    for copy in copies[3:]:
        copy.wait()

    receive(packed(first), 0)
    receive(plain(first, 0), 0)
    assemble(0, 1, 0, 4, range(-2, 6), qd)

    def to_modulus(x, t, total):
        at = brick(t)
        scale = iw[x, at]
        solid, void = sol[x, at] > 0, voi[x, at] > 0
        physical = jnp.where(solid, 1.0, jnp.where(void, 0.0, total * scale))
        square = physical * physical
        gm[0, 1 + x, tile(t)] = MU16 * EMIN + (MU16 * (1.0 - EMIN)) * (square * physical)
        co[x, at] = jnp.where(
            solid | void, 0.0, (-PENALTY * (1.0 - EMIN) * MU16) * (square * scale)
        )

    filter_field(dm, qd, to_modulus)
    second = messages(1, [(gm, 1, 1, 1)])
    send_all(second, 1, [(gm, 1)], plain(second))
    apply_inside(um)
    receive(plain(first, 1), 0)
    pack_around(um, 1, 1, range(-1, 5))
    assemble(0, 3, 1, 4, range(-1, 5), None, ed.at[0])
    shift_halo(um, 1)
    receive(plain(second), 1)
    pack_around(gm, 1, 0, range(-1, 5))
    receive(packed(second), 1)
    assemble(1, 1, 0, 1, range(-1, 5), None, ed.at[4])

    for x in range(BX):
        value = ed[4, 0, x + XE] + ed[4, 0, x + XE - 1]
        value = value + edge_down(value, 0)
        fxd[x] = value + last_z(value)

    def diagonal(t, carry):
        for x in range(BX):
            value = None
            for s in (x, x + 1):
                term = gm[0, s, tile(t)] + gm[0, s, pl.ds(8 * t + 7, 8)]
                value = term if value is None else value + term
            value = value + last_z(value)
            fixed = rot(fxd[x], lax.rem(256 - GROUP * (t + 1) - 9, 128))
            value = jnp.where(lane == 0, fixed, value)
            free = (1 - sup[x, brick(t)]).astype(f32)
            im[0, 1 + x, tile(t)] = free / (DIAG * value)
        return carry

    lax.fori_loop(0, 8, diagonal, 0, unroll=4)

    sums = {}
    acc_names = ("b0", "a00", "a01", "a11", "a12", "a22", "energy")
    for n, name in enumerate(acc_names):
        acc[n] = zero
        sums[name] = acc.at[n]

    def add(name, value):
        sums[name][...] = sums[name][...] + value

    kept = []

    def keep(name, value):
        kept.append((name, value))

    def flush():
        totals = {}
        for name, value in kept:
            totals[name] = value if name not in totals else totals[name] + value
        for name, value in totals.items():
            add(name, value)
        kept.clear()

    def from_start(x, c, t, image):
        if x is None:
            return flush()
        at = brick(t)
        free = (1 - sup[x, at]).astype(f32)
        load = lom[x, at].astype(f32)
        left = free * (load * loads[c, x, at] - image)
        value = im[0, 1 + x, tile(t)] * left
        vm0[c, 1 + x, tile(t)] = value
        keep("b0", left * value)

    def from_vector(source, target, diag_name, next_name):
        def use(x, c, t, image):
            if x is None:
                return flush()
            here = source[c, 1 + x, tile(t)]
            value = im[0, 1 + x, tile(t)] * image - THETA * here
            target[c, 1 + x, tile(t)] = value
            if x < BX and not (isinstance(t, int) and t >= 8):
                keep(diag_name, here * image)
                keep(next_name, value * image)

        return use

    own = list(range(BX))
    third = messages(2, [(vm0, 1, 1, 1), (im, 1, 0, 1)])
    send(plain(third, 1))
    apply_rest(um, ed.at[0], own, 8, from_start)
    send_all(third, 2, [(vm0, 1), (im, 1)], plain(third, 0))
    shift_own(vm0)
    apply_inside(vm0)
    receive(plain(third), 2)
    pack_around(vm0, 1, 0, range(-1, 5))
    pack_around(im, 1, 3, range(0, 5))
    shift_halo(vm0, 1)
    receive(packed(third), 2)
    assemble(2, 3, 0, 4, range(-1, 5), None, ed.at[1])
    assemble(2, 1, 3, 4, range(0, 5), None, ed.at[5])
    apply_rest(vm0, ed.at[1], own, 8, from_vector(vm0, vm1, "a00", "a01"))
    fourth = messages(3, [(vm1, 1, 1, 2)])
    send_all(fourth, 3, [(vm1, 1)], plain(fourth))
    shift_own(vm1)
    apply_inside(vm1)
    receive(plain(fourth), 3)
    pack_around(vm1, 1, 0, range(-1, 6))
    shift_halo(vm1, 2)
    receive(packed(fourth), 3)
    assemble(3, 3, 0, 3, range(-1, 6), None, ed.at[2])

    def edge_vector(x, c, image):
        ed[3, c, x + XE] = ed[5, 0, x + XE] * image - THETA * ed[2, c, x + XE]

    apply_rest(
        vm1, ed.at[2], own + [BX], 9, from_vector(vm1, vm2, "a11", "a12"), edge_vector
    )

    def energies(planes):
        before = None
        for index, plane in enumerate(planes):
            if before is not None:
                yield index - 1, mode_energy(x_modes(before, plane))
            before = plane

    column = (pos == 2) & (lane >= GROUP) & (lane < 9 * GROUP)

    edge_sum = zero
    for x, value in energies(edge_plane(ed.at[3], x) for x in range(BX + 1)):
        edge_sum = edge_sum + jnp.where(column, ed[4, 0, x + XE] * value, 0.0)

    def last_moment(t, carry):
        total = zero
        for x, value in energies(main_plane(vm2, x + 1, t) for x in range(BX + 1)):
            total = total + gm[0, 1 + x, tile(t)] * value
        add("a22", jnp.where(lane < 127, total, 0.0))
        return carry

    add("a22", edge_sum)
    lax.fori_loop(0, 8, last_moment, 0, unroll=4)

    message = jnp.zeros((1, 128), f32)
    lane1 = lax.broadcasted_iota(jnp.int32, (1, 128), 1)
    for n, name in enumerate(acc_names[:6]):
        part = jnp.sum(jnp.sum(sums[name][...], axis=0, keepdims=True), axis=1, keepdims=True)
        message = jnp.where(lane1 == n, part, message)
    reduce_start(0, message)
    for k, msgs in enumerate((first, second, third, fourth)):
        sent(msgs, k)
    totals = reduce_total(0)
    b0, a00, a01, a11, a12, a22 = (
        jnp.broadcast_to(totals[:, n : n + 1], (1, 128)) for n in range(6)
    )
    tiny = 1e-6
    b1 = a00 - THETA * b0
    b2 = a01 - THETA * b1
    l10, l20 = a01 / a00, a11 / a00
    d1 = a11 - l10 * a01
    ok1 = d1 > tiny * a11
    safe1 = jnp.where(ok1, d1, 1.0)
    cross = a12 - l20 * a01
    l21 = jnp.where(ok1, cross / safe1, 0.0)
    d2 = a22 - l20 * a11 - l21 * cross
    ok2 = ok1 & (d2 > tiny * a22)
    y1 = b1 - l10 * b0
    y2 = b2 - l20 * b0 - l21 * y1
    c2 = jnp.where(ok2, y2 / jnp.where(ok2, d2, 1.0), 0.0)
    c1 = jnp.where(ok1, y1 / safe1, 0.0) - l21 * c2
    c0 = b0 / a00 - l10 * c1 - l20 * c2
    c0, c1, c2 = (jnp.broadcast_to(c, (8, 128)) for c in (c0, c1, c2))

    for c in range(3):
        for x in range(BX + 1):
            s = x + XE
            ed[0, c, s] = ed[0, c, s] + (
                c0 * ed[1, c, s] + c1 * ed[2, c, s] + c2 * ed[3, c, s]
            )

    def combine(t, carry):
        for c in range(3):
            for s in range(1, BX + 2):
                at = brick(t + 1)
                um[c, s, at] = um[c, s, at] + (
                    c0 * vm0[c, s, at] + c1 * vm1[c, s, at] + c2 * vm2[c, s, at]
                )
        return carry

    lax.fori_loop(0, 9, combine, 0)
    disp = pltpu.make_async_copy(um.at[:, pl.ds(1, BX), own_rows], disp_out, out_sem.at[0])
    disp.start()

    for x, value in energies(edge_plane(ed.at[0], x) for x in range(BX + 1)):
        fxd[x] = value

    def sensitivity(t, carry):
        total = zero
        for x, value in energies(main_plane(um, x + 1, t) for x in range(BX + 1)):
            fixed = rot(fxd[x], lax.rem(253 - GROUP * (t + 1), 128))
            value = jnp.where(lane == 127, fixed, value)
            total = total + gm[0, 1 + x, tile(t)] * value
            sn[0, 2 + x, tile(t)] = co[x, brick(t)] * value
        add("energy", total)
        return carry

    lax.fori_loop(0, 8, sensitivity, 0, unroll=4)
    fifth = messages(4, [(sn, 2, 2, 2)])
    send_all(fifth, 4, [(sn, 2)], plain(fifth))
    part = jnp.sum(jnp.sum(sums["energy"][...], axis=0, keepdims=True), axis=1, keepdims=True)
    reduce_start(1, jnp.broadcast_to(part, (1, 128)))
    receive(fifth, 4)
    assemble(4, 1, 0, 1, range(-2, 6), qd)

    def finish(x, t, total):
        dsens_out[x, brick(t)] = total

    filter_field(sn, qd, finish)
    comp_out[...] = reduce_total(1)
    sent(fifth, 4)
    for k in range(2):
        reduce_wait(k, ar_ssem)
    disp.wait()


def call(sizes, *args):
    count = sizes[0] * sizes[1] * sizes[2]
    main3 = pltpu.VMEM((3, 7, 88, 128), f32)
    wide = pltpu.VMEM((1, 8, 80, 128), f32)
    brick = pltpu.VMEM((BX, BY, BZ), f32)
    mask = pltpu.VMEM((BX, BY, BZ), jnp.int32)
    any_spec = pl.BlockSpec(memory_space=pl.ANY)
    displacement, sensitivity, compliance = pl.pallas_call(
        functools.partial(body, sizes),
        out_shape=(
            pltpu.VMEM((3, BX, BY, BZ), f32),
            pltpu.VMEM((BX, BY, BZ), f32),
            jax.ShapeDtypeStruct((1, 128), f32),
        ),
        in_specs=[any_spec] * 7,
        out_specs=(pl.BlockSpec(memory_space=pltpu.VMEM),) * 3,
        scratch_shapes=[
            wide, main3, main3, main3, main3, pltpu.VMEM((1, 6, 80, 128), f32),
            pltpu.VMEM((1, 7, 80, 128), f32), wide,
            mask, mask, mask, mask, pltpu.VMEM((3, BX, BY, BZ), f32),
            brick, brick, main3, pltpu.VMEM((3, BX, BY, BZ), f32), pltpu.VMEM((8, 8, 128), f32),
            pltpu.VMEM((4096, 128), f32),
            pltpu.VMEM((5, 4, NE, 8, 128), f32),
            pltpu.VMEM((5, 2, 4, NE, 8, 128), f32),
            pltpu.VMEM((4, NE, 8, 128), f32),
            pltpu.VMEM((5, 2, 8, 128), f32),
            pltpu.VMEM((5, 3, 2, 2, 8, 128), f32),
            pltpu.VMEM((6, 3, NE, 8, 128), f32),
            pltpu.VMEM((1, NE, 8, 128), f32),
            pltpu.VMEM((3, NE, 8, 128), f32),
            pltpu.VMEM((BX, 8, 128), f32),
            pltpu.VMEM((2, 3, 7, 2, 8, 128), f32),
            pltpu.VMEM((2, count, 1, 128), f32),
            pltpu.VMEM((2, 1, 128), f32),
            pltpu.SemaphoreType.DMA((7,)),
            pltpu.SemaphoreType.DMA((1,)),
            pltpu.SemaphoreType.DMA((5,)),
            pltpu.SemaphoreType.DMA((5, 4)),
            pltpu.SemaphoreType.DMA((2,)),
            pltpu.SemaphoreType.DMA((2,)),
        ],
        compiler_params=pltpu.CompilerParams(
            collective_id=0, has_side_effects=True, vmem_limit_bytes=60 * 2**20
        ),
    )(*args)
    return displacement, sensitivity, compliance[0, 0]


def solution(mesh):
    sizes = tuple(mesh.shape[axis] for axis in AXES)
    block, field = P("gx", "gy", "gz"), P(None, "gx", "gy", "gz")
    return jax.shard_map(
        functools.partial(call, sizes),
        mesh=mesh,
        in_specs=(block,) * 5 + (field,) * 2,
        out_specs=(field, block, P()),
        check_vma=False,
    )
```

```python
import functools
import itertools
import math

import jax
import jax.numpy as jnp
from jax import lax
from jax.experimental import pallas as pl
from jax.experimental.pallas import tpu as pltpu
from jax.sharding import PartitionSpec as P

MESH = pl.DeviceIdType.MESH
AXES = ("gx", "gy", "gz")

EMIN = 0.001
PENALTY = 3.0
THETA = 1.5
MU16 = 1.0 / (2.6 * 16.0)
DIAG = 88.0 / 9.0

BX, BY, BZ = 4, 64, 128
GROUP = 12
FACES, CORNERS = 2, 3
XE = 2
NE = 8

f32 = jnp.float32

DIRECTIONS = sorted(
    [
        (dx, dy, dz)
        for dx in (0, 1, -1)
        for dy in (0, 1, -1)
        for dz in (0, 1, -1)
        if (dx, dy, dz) != (0, 0, 0)
    ],
    key=lambda d: (d[1:] != (0, 0), -sum(abs(step) for step in d)),
)


def iota(dim):
    return lax.broadcasted_iota(jnp.int32, (8, 128), dim)


def lane_pos():
    lane = iota(1)
    return lane - GROUP * ((lane * 43) >> 9)


def rot(value, shift, axis=1):
    size = value.shape[axis]
    return pltpu.roll(value, shift % size, axis)


def yz_modes(a, b, next_z):
    low, high = a + b, b - a
    low_next, high_next = next_z(low), next_z(high)
    return (low + low_next, low_next - low, high + high_next, high_next - high)


def x_modes(near, far):
    return [
        [None if m == 0 else n[m] + f[m] for m in range(4)] + [f[m] - n[m] for m in range(4)]
        for n, f in zip(near, far)
    ]


def mode_forces(q, g):
    u, v, w = q
    force = [[None] * 8 for _ in range(3)]
    trace = 1.5 * (u[4] + v[2] + w[1])
    force[0][4] = g * (trace + (u[4] + u[4]))
    force[1][2] = g * (trace + (v[2] + v[2]))
    force[2][1] = g * (trace + (w[1] + w[1]))
    for (ca, ma), (cb, mb) in (((0, 2), (1, 4)), ((1, 1), (2, 2)), ((0, 1), (2, 4))):
        shear = g * (q[ca][ma] + q[cb][mb])
        force[ca][ma] = shear
        force[cb][mb] = shear
    for (ca, ma), (cb, mb) in (((1, 6), (2, 5)), ((0, 6), (2, 3)), ((0, 5), (1, 3))):
        half = 0.5 * (q[ca][ma] + q[cb][mb])
        force[ca][ma] = g * (q[ca][ma] + half)
        force[cb][mb] = g * (q[cb][mb] + half)
    third = g * (1.0 / 3.0)
    total = u[3] + v[5] + w[6]
    force[0][3] = third * (u[3] + total)
    force[1][5] = third * (v[5] + total)
    force[2][6] = third * (w[6] + total)
    last = g * (5.5 / 9.0)
    for c in range(3):
        force[c][7] = last * q[c][7]
    return force


def mode_energy(q):
    u, v, w = q
    trace = u[4] + v[2] + w[1]
    total = 1.5 * (trace * trace) + 2.0 * (u[4] * u[4] + v[2] * v[2] + w[1] * w[1])
    for (ca, ma), (cb, mb) in (((0, 2), (1, 4)), ((1, 1), (2, 2)), ((0, 1), (2, 4))):
        shear = q[ca][ma] + q[cb][mb]
        total = total + shear * shear
    for (ca, ma), (cb, mb) in (((1, 6), (2, 5)), ((0, 6), (2, 3)), ((0, 5), (1, 3))):
        both = q[ca][ma] + q[cb][mb]
        total = total + (q[ca][ma] * q[ca][ma] + q[cb][mb] * q[cb][mb] + 0.5 * (both * both))
    both = u[3] + v[5] + w[6]
    total = total + (1.0 / 3.0) * (u[3] * u[3] + v[5] * v[5] + w[6] * w[6] + both * both)
    last = u[7] * u[7] + v[7] * v[7] + w[7] * w[7]
    return total + (5.5 / 9.0) * last


def node_parts(planes, xs, moduli):
    before, kept = None, None
    for index, plane in enumerate(planes):
        if before is not None:
            force = mode_forces(x_modes(before, plane), moduli(xs[index - 1]))
            right = [[-f[4] if m == 0 else f[m] - f[4 + m] for m in range(4)] for f in force]
            left = [[f[4] if m == 0 else f[m] + f[4 + m] for m in range(4)] for f in force]
            if kept is not None:
                right = [[k + r for k, r in zip(ks, rs)] for ks, rs in zip(kept, right)]
            yield xs[index - 1], right
            kept = left
        before = plane
    yield xs[-1], kept


def node_values(modes, shift_y, shift_z):
    ss, sd, ds, dd = modes
    low = (ss - ds) + shift_y(ss + ds, 0)
    high = (sd - dd) + shift_y(sd + dd, 1)
    return (low - high) + shift_z(low + high)


def body(
    sizes,
    design_in, support_in, load_in, solid_in, void_in, loads_in, start_in,
    disp_out, dsens_out, comp_out,
    dm, um, vm0, vm1, vm2, gm, im, sn, sup, lom, sol, voi, loads, iw, co, fz, img, acc,
    dummy, pa, pz, po, ko, kr, ed, qd, fx, fxd, cy, ar, ar_msg,
    in_sem, out_sem, ssem, rsem, ar_ssem, ar_rsem,
):
    nx, ny, nz = sizes
    count = nx * ny * nz
    me = [lax.axis_index(a) for a in AXES]
    linear = (me[0] * ny + me[1]) * nz + me[2]
    lane, row, pos = iota(1), iota(0), lane_pos()
    pos6 = jnp.where(pos < 6, pos, pos - 6)
    own_rows = pl.ds(8, BY)
    zero = jnp.zeros((8, 128), f32)

    def tile(t):
        return pl.ds(pl.multiple_of(8 * t + 8, 8), 8)

    def brick(t):
        return pl.ds(pl.multiple_of(8 * t, 8), 8)

    copies = [
        pltpu.make_async_copy(src, dst, in_sem.at[i])
        for i, (src, dst) in enumerate(
            (
                (start_in, um.at[:, pl.ds(1, BX), own_rows]),
                (support_in, sup),
                (design_in, dm.at[0, pl.ds(2, BX), own_rows]),
                (solid_in, sol),
                (void_in, voi),
                (load_in, lom),
                (loads_in, loads),
            )
        )
    ]
    for copy in copies:
        copy.start()

    def clear_main(*refs):
        def sides(t, carry):
            for ref, xo, slots in refs:
                for c in range(ref.shape[0]):
                    for s in [*range(xo), *range(xo + BX, slots)]:
                        ref[c, s, brick(t)] = zero
            return carry

        def ends(s, carry):
            for ref, xo, _ in refs:
                for c in range(ref.shape[0]):
                    for t in (0, 9):
                        ref[c, xo + s, 8 * t : 8 * t + 8] = zero
            return carry

        lax.fori_loop(0, 10, sides, 0)
        lax.fori_loop(0, BX, ends, 0)

    def clear_edges(k):
        def planes(s, carry):
            for side in range(2):
                for c in range(4):
                    pz[k, side, c, s] = zero
            return carry

        def corners(a, carry):
            for b in range(2):
                for d in range(2):
                    kr[k, a, b, d] = zero
            return carry

        lax.fori_loop(0, NE, planes, 0)
        lax.fori_loop(0, 3, corners, 0)

    clear_main((dm, 2, 8), (um, 1, 7))
    clear_edges(0)

    def exists(d, sign):
        ok = None
        for m, step, size in zip(me, d, sizes):
            if step * sign > 0:
                here = m < size - abs(step)
            elif step * sign < 0:
                here = m >= abs(step)
            else:
                continue
            ok = here if ok is None else ok & here
        return ok

    barrier = pltpu.get_barrier_semaphore()

    greeted = 0
    for d in DIRECTIONS + [(0, 0, 4), (0, 0, -4)]:
        there = exists(d, 1)

        @pl.when(there)
        def _(d=d):
            pl.semaphore_signal(
                barrier,
                inc=1,
                device_id=tuple(m + step for m, step in zip(me, d)),
                device_id_type=MESH,
            )

        greeted = greeted + jnp.where(there, 1, 0)

    clear_main((sn, 2, 8), (gm, 1, 6), (vm0, 1, 7), (vm1, 1, 7), (im, 1, 7))
    lax.fori_loop(1, pz.shape[0], lambda k, carry: (clear_edges(k), carry)[1], 0)

    def clear_last(s, carry):
        for c in range(3):
            vm1[c, s, 80:88] = zero
        return carry

    lax.fori_loop(0, 7, clear_last, 0)

    def group_mask(t, first, last):
        return (lane >= GROUP * (t + 1) + first) & (lane < GROUP * (t + 1) + last)

    def pack_tiles(tiles, base):
        for t, tile in tiles:
            base = jnp.where(group_mask(t, 0, 6), rot(tile, GROUP * (t + 1) + 3), base)
        return base

    def pack_corners(k, fields):
        comp, total = 0, sum(ref.shape[0] for ref, _ in fields)
        corner = [zero, zero]
        for ref, xo in fields:
            for c in range(ref.shape[0]):
                for x in range(BX):
                    i = 6 * (x * total + comp)
                    for side, t in ((0, 0), (1, 7)):
                        corner[side] = jnp.where(
                            (lane >= i) & (lane < i + 6),
                            rot(ref[c, x + xo, 8 * t + 8 : 8 * t + 16], i + 3),
                            corner[side],
                        )
                comp += 1
        for side in range(2):
            ko[k, side] = corner[side]

    def pack(k, fields):
        comp = 0
        for ref, xo in fields:
            for c in range(ref.shape[0]):
                for x in range(BX):
                    pa[k, comp, x + XE] = pack_tiles(
                        [(t, ref[c, x + xo, 8 * t + 8 : 8 * t + 16]) for t in range(8)], zero
                    )
                comp += 1

    def messages(k, fields):
        comps = sum(f[0].shape[0] for f in fields)
        low, high = max(f[2] for f in fields), max(f[3] for f in fields)
        result = []
        for d in DIRECTIONS:
            dx, dy, dz = d
            if (1 in d and low == 0) or (-1 in d and high == 0):
                continue
            parts = []
            if dz == 0:
                for n, (ref, xo, lo, hi) in enumerate(fields):
                    if (1 in d and lo == 0) or (-1 in d and hi == 0):
                        continue
                    if dx == 1:
                        xs, xd = pl.ds(xo + BX - lo, lo), pl.ds(xo - lo, lo)
                    elif dx == -1:
                        xs, xd = pl.ds(xo, hi), pl.ds(xo + BX, hi)
                    else:
                        xs = xd = pl.ds(xo, BX)
                    if dy == 1:
                        ys, yd = pl.ds(BY, 8), pl.ds(0, 8)
                    elif dy == -1:
                        ys, yd = pl.ds(8, 8), pl.ds(BY + 8, 8)
                    else:
                        ys = yd = own_rows
                    parts.append((n, ref.at[:, xs, ys], ref.at[:, xd, yd]))
            elif dy == 0:
                if dx == 1:
                    xs, xd = pl.ds(XE + BX - low, low), pl.ds(XE - low, low)
                elif dx == -1:
                    xs, xd = pl.ds(XE, high), pl.ds(XE + BX, high)
                else:
                    xs = xd = pl.ds(XE, BX)
                side, cs = 0 if dz == 1 else 1, pl.ds(0, comps)
                parts.append((FACES, pa.at[k, cs, xs], pz.at[k, side, cs, xd]))
            else:
                own = ko.at[k, 0 if dy == -1 else 1]
                there = kr.at[k, 1 - dx, 0 if dy == 1 else 1, 0 if dz == 1 else 1]
                parts.append((CORNERS, own, there))
            for n, src, dst in parts:
                copy = pltpu.make_async_remote_copy(
                    src_ref=src,
                    dst_ref=dst,
                    send_sem=ssem.at[k],
                    recv_sem=rsem.at[k, n],
                    device_id=tuple(m + step for m, step in zip(me, d)),
                    device_id_type=MESH,
                )
                result.append((d, n, copy, math.prod(src.shape) // 128))
        return result

    def send(msgs):
        for d in DIRECTIONS:
            group = [m[2] for m in msgs if m[0] == d]
            if group:
                @pl.when(exists(d, 1))
                def _(group=group):
                    for copy in group:
                        copy.start()

    def wait_rows(msgs, sign, sem):
        kinds = [
            [(False, False)] if size == 1
            else [(False, True), (True, False)] + [(True, True)] * (size > 2)
            for size in sizes
        ]
        totals = set()
        for pattern in itertools.product(*kinds):
            rows = 0
            for d, _, _, n in msgs:
                if all(step == 0 or has[step * sign > 0] for step, has in zip(d, pattern)):
                    rows += n
            totals.add(rows)
        rows = 0
        for d in DIRECTIONS:
            n = sum(m[3] for m in msgs if m[0] == d)
            if n:
                rows = rows + jnp.where(exists(d, sign), n, 0)
        for total in sorted(totals - {0}):
            @pl.when(rows == total)
            def _(total=total):
                part = dummy.at[pl.ds(0, total)]
                pltpu.make_async_copy(part, part, sem).wait()

    def receive(msgs, k):
        for n in sorted({m[1] for m in msgs}):
            wait_rows([m for m in msgs if m[1] == n], -1, rsem.at[k, n])

    def sent(msgs, k):
        wait_rows(msgs, 1, ssem.at[k])

    def plain(msgs, n=None):
        return [m for m in msgs if m[1] < FACES and n in (None, m[1])]

    def packed(msgs, n=None):
        return [m for m in msgs if m[1] >= FACES and n in (None, m[1])]

    def send_all(msgs, k, fields, first=()):
        send(first)
        pack_corners(k, fields)
        send(packed(msgs, CORNERS))
        pack(k, fields)
        send(packed(msgs, FACES))

    def pack_around(ref, xo, first_comp, planes):
        for x in planes:
            for c in range(ref.shape[0]):
                outside = x < 0 or x >= BX
                po[first_comp + c, x + XE] = pack_tiles(
                    [
                        (t, ref[c, x + xo, 8 * t + 8 : 8 * t + 16])
                        for t in (range(-1, 9) if outside else (-1, 8))
                    ],
                    zero,
                )

    def assemble(k, count, first_comp, comps, planes, halo, edge=None):
        items = [(c, x) for x in planes for c in range(count)]
        around = {}
        for _, x in items:
            side = 0 if x < 0 else 2 if x >= BX else 1
            for end in range(2):
                if (side, end) not in around:
                    around[side, end] = jnp.where(pos6 < 3, kr[k, side, end, 0], kr[k, side, end, 1])
        inner = (lane >= GROUP) & (lane < 9 * GROUP)
        for c, x in items:
            comp = first_comp + c
            side = 0 if x < 0 else 2 if x >= BX else 1
            i = 6 * (x % BX * comps + comp)
            value = jnp.where(pos < 3, pz[k, 0, comp, x + XE], pz[k, 1, comp, x + XE])
            value = jnp.where(lane < 6, rot(around[side, 0], -i), value)
            value = jnp.where(group_mask(8, 0, 6), rot(around[side, 1], 9 * GROUP - i), value)
            if halo is not None:
                halo[c, x + XE] = value
            if edge is not None:
                own = po[comp, x + XE]
                if side == 1:
                    own = jnp.where(inner, pa[k, comp, x + XE], own)
                high = rot(jnp.where(pos < 3, value, own), 6)
                low = jnp.where(pos < 3, own, value)
                edge[c, x + XE] = jnp.where(pos < 6, low, high)

    def next_z(value):
        return rot(value, -1)

    def last_z(value):
        return rot(value, 1)

    def main_plane(ref, s, t, shifted=None):
        start = 8 * t + 8
        out = []
        for c in range(3):
            a, b = ref[c, s, tile(t)], ref[c, s, pl.ds(start + 1, 8)]
            if shifted is None:
                out.append(yz_modes(a, b, next_z))
            else:
                an, bn = shifted[c, s, tile(t)], shifted[c, s, pl.ds(start + 1, 8)]
                low, high, low_next, high_next = a + b, b - a, an + bn, bn - an
                out.append((low + low_next, low_next - low, high + high_next, high_next - high))
        return out

    def shift_own(ref):
        def step(t, carry):
            for c in range(3):
                for s in range(1, 1 + BX):
                    fz[c, s, tile(t)] = next_z(ref[c, s, tile(t)])
            return carry

        lax.fori_loop(0, 8, step, 0, unroll=4)

    def shift_halo(ref, high):
        for c in range(3):
            for s in range(BX + 1 + high):
                for t in (-1, 8) if 1 <= s <= BX else range(-1, 9):
                    fz[c, s, tile(t)] = next_z(ref[c, s, tile(t)])

    def edge_plane(edge, x):
        out = []
        for c in range(3):
            a = edge[c, x + XE]
            b = rot(jnp.where(row == 0, rot(a, -GROUP), a), -1, 0)
            out.append(yz_modes(a, b, next_z))
        return out

    def edge_down(value, _):
        down = rot(value, 1, 0)
        return jnp.where(row == 0, rot(down, GROUP), down)

    outer = (lane == 0) | (lane == 127)

    def split(modes):
        ss, sd, ds, dd = modes
        return (ss - ds, sd - dd), (ss + ds, sd + dd)

    def parts_of(ref, t, first, last):
        xs = list(range(first, last + 2))
        return node_parts(
            (main_plane(ref, x + 1, t, fz) for x in xs), xs, lambda e: gm[0, e + 1, tile(t)]
        )

    def apply_inside(ref):
        for c in range(3):
            for x in range(BX):
                for which in range(2):
                    cy[0, c, x + 1, which] = zero

        def step(t, carry):
            for x, modes in parts_of(ref, t, 0, BX - 2):
                for c in range(3):
                    here, after = split(modes[c])
                    both = []
                    for which in range(2):
                        down = rot(after[which], 1, 0)
                        both.append(
                            here[which] + jnp.where(row == 0, cy[0, c, x + 1, which], down)
                        )
                        cy[0, c, x + 1, which] = down
                    img[c, x, brick(t)] = (both[0] - both[1]) + last_z(both[0] + both[1])
            return carry

        lax.fori_loop(0, 7, step, 0)

    def apply_rest(ref, edge, planes, tiles, use, use_edge=None):
        last = planes[-1]
        nodes = list(range(-1, last + 2))
        for x, modes in node_parts(
            (edge_plane(edge, x) for x in nodes), nodes, lambda e: ed[4, 0, e + XE]
        ):
            if x not in planes:
                continue
            for c in range(3):
                value = node_values(modes[c], edge_down, last_z)
                fx[c, x + XE] = jnp.where(pos == 3, rot(value, -6), value)
                if use_edge is not None:
                    use_edge(x, c, value)

        def emit(x, t, modes, inside, before):
            for c in range(3):
                both = []
                for which in range(2):
                    value, down = None, None
                    if modes is not None:
                        here, after = split(modes[c])
                        value, down = here[which], rot(after[which], 1, 0)
                    below = before(c, x, which)
                    if below is not None:
                        enter = jnp.where(row == 0, below, zero if down is None else down)
                    else:
                        enter = down
                    if enter is not None:
                        value = enter if value is None else value + enter
                    if down is not None:
                        cy[1, c, x + 1, which] = down
                    both.append(value)
                total = None
                if both[0] is not None:
                    total = (both[0] - both[1]) + last_z(both[0] + both[1])
                if inside:
                    partial = img[c, x, brick(t)]
                    total = partial if total is None else total + partial
                fixed = rot(fx[c, x + XE], lax.rem(254 - GROUP * (t + 1) - 1, 128))
                use(x, c, t, jnp.where(outer, fixed, total))

        groups = [(-1, -1), (BX - 1, last)]
        bound = [0] + list(range(BX - 1, last + 1))

        def edge_step(t, before):
            done = []
            for group in groups:
                for x, modes in parts_of(ref, t, *group):
                    if x in planes:
                        emit(x, t, modes, x < BX, before)
                        done.append(x)
            for x in planes:
                if x not in done:
                    emit(x, t, None, True, before)
            use(None, None, t, None)

        def full_step(t, before):
            for x, modes in parts_of(ref, t, -1, last):
                if x in planes:
                    emit(x, t, modes, False, before)
            use(None, None, t, None)

        for x, modes in parts_of(ref, -1, -1, last):
            if x in planes:
                for c in range(3):
                    after = split(modes[c])[1]
                    for which in range(2):
                        cy[1, c, x + 1, which] = rot(after[which], 1, 0)
        edge_step(0, lambda c, x, which: cy[1, c, x + 1, which])

        def chain(c, x, which):
            return cy[1, c, x + 1, which] if x in bound else None

        lax.fori_loop(1, 7, lambda t, carry: (edge_step(t, chain), carry)[1], 0, unroll=3)

        def join(c, x, which):
            value = cy[1, c, x + 1, which] if x in bound else None
            if x < BX:
                own = cy[0, c, x + 1, which]
                value = own if value is None else value + own
            return value

        full_step(7, join)
        for t in range(8, tiles):
            full_step(t, lambda c, x, which: cy[1, c, x + 1, which])

    weights = {}
    for a in range(3):
        for b in range(3):
            for c in range(3):
                weights[a, b, c] = max(0.0, 3.0 - math.sqrt(a * a + b * b + c * c))

    def combine_xy(planes, x):
        far = []
        for b in range(3):
            far.append(
                [
                    planes[x + 2][b],
                    planes[x + 1][b] + planes[x + 3][b],
                    planes[x][b] + planes[x + 4][b],
                ]
            )
        pair = {
            (0, 0): far[0][0],
            (0, 1): far[0][1] + far[1][0],
            (1, 1): far[1][1],
            (0, 2): far[0][2] + far[2][0],
            (1, 2): far[1][2] + far[2][1],
            (2, 2): far[2][2],
        }
        out = []
        for c in range(3):
            value = None
            for (a, b), term in pair.items():
                if weights[a, b, c] > 0.0:
                    term = weights[a, b, c] * term
                    value = term if value is None else value + term
            out.append(value)
        return out

    def filter_field(ref, halo, use):
        planes = []
        for s in range(8):
            value = halo[0, s]
            up, down = rot(value, -GROUP), rot(value, GROUP)
            one = rot(jnp.where(row == 0, up, value), -1, 0) + rot(
                jnp.where(row == 7, down, value), 1, 0
            )
            two = rot(jnp.where(row <= 1, up, value), -2, 0) + rot(
                jnp.where(row >= 6, down, value), 2, 0
            )
            planes.append((value, one, two))
        for x in range(BX):
            _, fx[1, x], fx[2, x] = combine_xy(planes, x)

        def step(t, carry):
            planes = []
            for s in range(8):
                rows = [ref[0, s, pl.ds(8 * t + 8 + off, 8)] for off in (-2, -1, 1, 2)]
                planes.append((ref[0, s, tile(t)], rows[1] + rows[2], rows[0] + rows[3]))
            shift = lax.rem(256 - GROUP * (t + 1) - 3, 128)
            for x in range(BX):
                value, one, two = combine_xy(planes, x)
                side = rot(fx[1, x], shift)
                value = value + rot(jnp.where(lane < 1, side, one), -1)
                value = value + rot(jnp.where(lane >= 127, side, one), 1)
                side = rot(fx[2, x], shift)
                value = value + rot(jnp.where(lane < 2, side, two), -2)
                value = value + rot(jnp.where(lane >= 126, side, two), 2)
                use(x, t, value)
            return carry

        lax.fori_loop(0, 8, step, 0, unroll=4)

    def reduce_start(k, value):
        ar_msg[k] = value
        ar[k, linear] = value

        steps = [
            (ox, oy, oz)
            for ox in range(nx)
            for oy in range(ny)
            for oz in range(nz)
            if (ox, oy, oz) != (0, 0, 0)
        ]
        steps.sort(key=lambda o: -sum(min(step, size - step) for step, size in zip(o, sizes)))
        for o in steps:
            pltpu.make_async_remote_copy(
                src_ref=ar_msg.at[k],
                dst_ref=ar.at[k, linear],
                send_sem=ar_ssem.at[k],
                recv_sem=ar_rsem.at[k],
                device_id=tuple(
                    lax.rem(m + step, size) if step else m for m, step, size in zip(me, o, sizes)
                ),
                device_id_type=MESH,
            ).start()

    def reduce_wait(k, sem):
        part = ar.at[k, pl.ds(0, count - 1)]
        pltpu.make_async_copy(part, part, sem.at[k]).wait()

    def reduce_total(k):
        reduce_wait(k, ar_rsem)
        return jnp.sum(ar[k], axis=0)


    copies[0].wait()
    copies[1].wait()
    for c in range(3):
        um[c, 1 : 1 + BX, 8 : 8 + BY] = um[c, 1 : 1 + BX, 8 : 8 + BY] * (1 - sup[...]).astype(f32)
    copies[2].wait()
    pack_corners(0, [(dm, 2), (um, 1)])
    pack(0, [(dm, 2), (um, 1)])
    pl.semaphore_wait(barrier, greeted)
    first = messages(0, [(dm, 2, 2, 2), (um, 1, 1, 1)])
    send(packed(first))
    send(plain(first, 0))
    send(plain(first, 1))
    shift_own(um)

    def inside(coord, size):
        return ((coord >= 0) & (coord < size)).astype(f32)

    z_at = me[2] * BZ + lane
    z_terms = [
        jnp.ones((8, 128), f32),
        inside(z_at - 1, nz * BZ) + inside(z_at + 1, nz * BZ),
        inside(z_at - 2, nz * BZ) + inside(z_at + 2, nz * BZ),
    ]
    x_rows = []
    for x in range(BX):
        x_at = me[0] * BX + x
        x_terms = [
            f32(1.0),
            inside(x_at - 1, nx * BX) + inside(x_at + 1, nx * BX),
            inside(x_at - 2, nx * BX) + inside(x_at + 2, nx * BX),
        ]
        per_b = []
        for b in range(3):
            value = zero
            for c in range(3):
                value = value + z_terms[c] * sum(x_terms[a] * weights[a, b, c] for a in range(3))
            per_b.append(value)
        x_rows.append(per_b)

    def weigh(t, carry):
        y_at = me[1] * BY + 8 * t + row
        one = inside(y_at - 1, ny * BY) + inside(y_at + 1, ny * BY)
        two = inside(y_at - 2, ny * BY) + inside(y_at + 2, ny * BY)
        for x in range(BX):
            iw[x, brick(t)] = 1.0 / (x_rows[x][0] + one * x_rows[x][1] + two * x_rows[x][2])
        return carry

    lax.fori_loop(0, 8, weigh, 0, unroll=4)
    for copy in copies[3:]:
        copy.wait()

    receive(packed(first), 0)
    receive(plain(first, 0), 0)
    assemble(0, 1, 0, 4, range(-2, 6), qd)

    def to_modulus(x, t, total):
        at = brick(t)
        scale = iw[x, at]
        solid, void = sol[x, at] > 0, voi[x, at] > 0
        physical = jnp.where(solid, 1.0, jnp.where(void, 0.0, total * scale))
        square = physical * physical
        gm[0, 1 + x, tile(t)] = MU16 * EMIN + (MU16 * (1.0 - EMIN)) * (square * physical)
        co[x, at] = jnp.where(
            solid | void, 0.0, (-PENALTY * (1.0 - EMIN) * MU16) * (square * scale)
        )

    filter_field(dm, qd, to_modulus)
    second = messages(1, [(gm, 1, 1, 1)])
    send_all(second, 1, [(gm, 1)], plain(second))
    apply_inside(um)
    receive(plain(first, 1), 0)
    pack_around(um, 1, 1, range(-1, 5))
    assemble(0, 3, 1, 4, range(-1, 5), None, ed.at[0])
    shift_halo(um, 1)
    receive(plain(second), 1)
    pack_around(gm, 1, 0, range(-1, 5))
    receive(packed(second), 1)
    assemble(1, 1, 0, 1, range(-1, 5), None, ed.at[4])

    for x in range(BX):
        value = ed[4, 0, x + XE] + ed[4, 0, x + XE - 1]
        value = value + edge_down(value, 0)
        fxd[x] = value + last_z(value)

    def diagonal(t, carry):
        for x in range(BX):
            value = None
            for s in (x, x + 1):
                term = gm[0, s, tile(t)] + gm[0, s, pl.ds(8 * t + 7, 8)]
                value = term if value is None else value + term
            value = value + last_z(value)
            fixed = rot(fxd[x], lax.rem(256 - GROUP * (t + 1) - 9, 128))
            value = jnp.where(lane == 0, fixed, value)
            free = (1 - sup[x, brick(t)]).astype(f32)
            im[0, 1 + x, tile(t)] = free / (DIAG * value)
        return carry

    lax.fori_loop(0, 8, diagonal, 0, unroll=4)

    sums = {}
    acc_names = ("b0", "a00", "a01", "a11", "a12", "a22", "energy")
    for n, name in enumerate(acc_names):
        acc[n] = zero
        sums[name] = acc.at[n]

    def add(name, value):
        sums[name][...] = sums[name][...] + value

    kept = []

    def keep(name, value):
        kept.append((name, value))

    def flush():
        totals = {}
        for name, value in kept:
            totals[name] = value if name not in totals else totals[name] + value
        for name, value in totals.items():
            add(name, value)
        kept.clear()

    def from_start(x, c, t, image):
        if x is None:
            return flush()
        at = brick(t)
        free = (1 - sup[x, at]).astype(f32)
        load = lom[x, at].astype(f32)
        left = free * (load * loads[c, x, at] - image)
        value = im[0, 1 + x, tile(t)] * left
        vm0[c, 1 + x, tile(t)] = value
        keep("b0", left * value)

    def from_vector(source, target, diag_name, next_name):
        def use(x, c, t, image):
            if x is None:
                return flush()
            here = source[c, 1 + x, tile(t)]
            value = im[0, 1 + x, tile(t)] * image - THETA * here
            target[c, 1 + x, tile(t)] = value
            if x < BX and not (isinstance(t, int) and t >= 8):
                keep(diag_name, here * image)
                keep(next_name, value * image)

        return use

    own = list(range(BX))
    third = messages(2, [(vm0, 1, 1, 1), (im, 1, 0, 1)])
    send(plain(third, 1))
    apply_rest(um, ed.at[0], own, 8, from_start)
    send_all(third, 2, [(vm0, 1), (im, 1)], plain(third, 0))
    shift_own(vm0)
    apply_inside(vm0)
    receive(plain(third), 2)
    pack_around(vm0, 1, 0, range(-1, 5))
    pack_around(im, 1, 3, range(0, 5))
    shift_halo(vm0, 1)
    receive(packed(third), 2)
    assemble(2, 3, 0, 4, range(-1, 5), None, ed.at[1])
    assemble(2, 1, 3, 4, range(0, 5), None, ed.at[5])
    apply_rest(vm0, ed.at[1], own, 8, from_vector(vm0, vm1, "a00", "a01"))
    fourth = messages(3, [(vm1, 1, 1, 2)])
    send_all(fourth, 3, [(vm1, 1)], plain(fourth))
    shift_own(vm1)
    apply_inside(vm1)
    receive(plain(fourth), 3)
    pack_around(vm1, 1, 0, range(-1, 6))
    shift_halo(vm1, 2)
    receive(packed(fourth), 3)
    assemble(3, 3, 0, 3, range(-1, 6), None, ed.at[2])

    def edge_vector(x, c, image):
        ed[3, c, x + XE] = ed[5, 0, x + XE] * image - THETA * ed[2, c, x + XE]

    apply_rest(
        vm1, ed.at[2], own + [BX], 9, from_vector(vm1, vm2, "a11", "a12"), edge_vector
    )

    def energies(planes):
        before = None
        for index, plane in enumerate(planes):
            if before is not None:
                yield index - 1, mode_energy(x_modes(before, plane))
            before = plane

    column = (pos == 2) & (lane >= GROUP) & (lane < 9 * GROUP)

    edge_sum = zero
    for x, value in energies(edge_plane(ed.at[3], x) for x in range(BX + 1)):
        edge_sum = edge_sum + jnp.where(column, ed[4, 0, x + XE] * value, 0.0)

    def last_moment(t, carry):
        total = zero
        for x, value in energies(main_plane(vm2, x + 1, t) for x in range(BX + 1)):
            total = total + gm[0, 1 + x, tile(t)] * value
        add("a22", jnp.where(lane < 127, total, 0.0))
        return carry

    add("a22", edge_sum)
    lax.fori_loop(0, 8, last_moment, 0, unroll=4)

    message = jnp.zeros((1, 128), f32)
    lane1 = lax.broadcasted_iota(jnp.int32, (1, 128), 1)
    for n, name in enumerate(acc_names[:6]):
        part = jnp.sum(jnp.sum(sums[name][...], axis=0, keepdims=True), axis=1, keepdims=True)
        message = jnp.where(lane1 == n, part, message)
    reduce_start(0, message)
    for k, msgs in enumerate((first, second, third, fourth)):
        sent(msgs, k)
    totals = reduce_total(0)
    b0, a00, a01, a11, a12, a22 = (
        jnp.broadcast_to(totals[:, n : n + 1], (1, 128)) for n in range(6)
    )
    tiny = 1e-6
    b1 = a00 - THETA * b0
    b2 = a01 - THETA * b1
    l10, l20 = a01 / a00, a11 / a00
    d1 = a11 - l10 * a01
    ok1 = d1 > tiny * a11
    safe1 = jnp.where(ok1, d1, 1.0)
    cross = a12 - l20 * a01
    l21 = jnp.where(ok1, cross / safe1, 0.0)
    d2 = a22 - l20 * a11 - l21 * cross
    ok2 = ok1 & (d2 > tiny * a22)
    y1 = b1 - l10 * b0
    y2 = b2 - l20 * b0 - l21 * y1
    c2 = jnp.where(ok2, y2 / jnp.where(ok2, d2, 1.0), 0.0)
    c1 = jnp.where(ok1, y1 / safe1, 0.0) - l21 * c2
    c0 = b0 / a00 - l10 * c1 - l20 * c2
    c0, c1, c2 = (jnp.broadcast_to(c, (8, 128)) for c in (c0, c1, c2))

    for c in range(3):
        for x in range(BX + 1):
            s = x + XE
            ed[0, c, s] = ed[0, c, s] + (
                c0 * ed[1, c, s] + c1 * ed[2, c, s] + c2 * ed[3, c, s]
            )

    def combine(t, carry):
        for c in range(3):
            for s in range(1, BX + 2):
                at = brick(t + 1)
                um[c, s, at] = um[c, s, at] + (
                    c0 * vm0[c, s, at] + c1 * vm1[c, s, at] + c2 * vm2[c, s, at]
                )
        return carry

    lax.fori_loop(0, 9, combine, 0)
    disp = pltpu.make_async_copy(um.at[:, pl.ds(1, BX), own_rows], disp_out, out_sem.at[0])
    disp.start()

    for x, value in energies(edge_plane(ed.at[0], x) for x in range(BX + 1)):
        fxd[x] = value

    def sensitivity(t, carry):
        total = zero
        for x, value in energies(main_plane(um, x + 1, t) for x in range(BX + 1)):
            fixed = rot(fxd[x], lax.rem(253 - GROUP * (t + 1), 128))
            value = jnp.where(lane == 127, fixed, value)
            total = total + gm[0, 1 + x, tile(t)] * value
            sn[0, 2 + x, tile(t)] = co[x, brick(t)] * value
        add("energy", total)
        return carry

    lax.fori_loop(0, 8, sensitivity, 0, unroll=4)
    fifth = messages(4, [(sn, 2, 2, 2)])
    send(plain(fifth))
    part = jnp.sum(jnp.sum(sums["energy"][...], axis=0, keepdims=True), axis=1, keepdims=True)
    reduce_start(1, jnp.broadcast_to(part, (1, 128)))
    send_all(fifth, 4, [(sn, 2)])
    receive(fifth, 4)
    assemble(4, 1, 0, 1, range(-2, 6), qd)

    def finish(x, t, total):
        dsens_out[x, brick(t)] = total

    filter_field(sn, qd, finish)
    comp_out[...] = reduce_total(1)
    sent(fifth, 4)
    for k in range(2):
        reduce_wait(k, ar_ssem)
    disp.wait()


def call(sizes, *args):
    count = sizes[0] * sizes[1] * sizes[2]
    main3 = pltpu.VMEM((3, 7, 88, 128), f32)
    wide = pltpu.VMEM((1, 8, 80, 128), f32)
    brick = pltpu.VMEM((BX, BY, BZ), f32)
    mask = pltpu.VMEM((BX, BY, BZ), jnp.int32)
    any_spec = pl.BlockSpec(memory_space=pl.ANY)
    displacement, sensitivity, compliance = pl.pallas_call(
        functools.partial(body, sizes),
        out_shape=(
            pltpu.VMEM((3, BX, BY, BZ), f32),
            pltpu.VMEM((BX, BY, BZ), f32),
            jax.ShapeDtypeStruct((1, 128), f32),
        ),
        in_specs=[any_spec] * 7,
        out_specs=(pl.BlockSpec(memory_space=pltpu.VMEM),) * 3,
        scratch_shapes=[
            wide, main3, main3, main3, main3, pltpu.VMEM((1, 6, 80, 128), f32),
            pltpu.VMEM((1, 7, 80, 128), f32), wide,
            mask, mask, mask, mask, pltpu.VMEM((3, BX, BY, BZ), f32),
            brick, brick, main3, pltpu.VMEM((3, BX, BY, BZ), f32), pltpu.VMEM((8, 8, 128), f32),
            pltpu.VMEM((4096, 128), f32),
            pltpu.VMEM((5, 4, NE, 8, 128), f32),
            pltpu.VMEM((5, 2, 4, NE, 8, 128), f32),
            pltpu.VMEM((4, NE, 8, 128), f32),
            pltpu.VMEM((5, 2, 8, 128), f32),
            pltpu.VMEM((5, 3, 2, 2, 8, 128), f32),
            pltpu.VMEM((6, 3, NE, 8, 128), f32),
            pltpu.VMEM((1, NE, 8, 128), f32),
            pltpu.VMEM((3, NE, 8, 128), f32),
            pltpu.VMEM((BX, 8, 128), f32),
            pltpu.VMEM((2, 3, 7, 2, 8, 128), f32),
            pltpu.VMEM((2, count, 1, 128), f32),
            pltpu.VMEM((2, 1, 128), f32),
            pltpu.SemaphoreType.DMA((7,)),
            pltpu.SemaphoreType.DMA((1,)),
            pltpu.SemaphoreType.DMA((5,)),
            pltpu.SemaphoreType.DMA((5, 4)),
            pltpu.SemaphoreType.DMA((2,)),
            pltpu.SemaphoreType.DMA((2,)),
        ],
        compiler_params=pltpu.CompilerParams(
            collective_id=0, has_side_effects=True, vmem_limit_bytes=60 * 2**20
        ),
    )(*args)
    return displacement, sensitivity, compliance[0, 0]


def solution(mesh):
    sizes = tuple(mesh.shape[axis] for axis in AXES)
    block, field = P("gx", "gy", "gz"), P(None, "gx", "gy", "gz")
    return jax.shard_map(
        functools.partial(call, sizes),
        mesh=mesh,
        in_specs=(block,) * 5 + (field,) * 2,
        out_specs=(field, block, P()),
        check_vma=False,
    )
```

```python
import functools
import itertools
import math

import jax
import jax.numpy as jnp
from jax import lax
from jax.experimental import pallas as pl
from jax.experimental.pallas import tpu as pltpu
from jax.sharding import PartitionSpec as P

MESH = pl.DeviceIdType.MESH
AXES = ("gx", "gy", "gz")

EMIN = 0.001
PENALTY = 3.0
THETA = 1.5
MU16 = 1.0 / (2.6 * 16.0)
DIAG = 88.0 / 9.0

BX, BY, BZ = 4, 64, 128
GROUP = 12
FACES, CORNERS = 2, 3
XE = 2
NE = 8

f32 = jnp.float32

DIRECTIONS = sorted(
    [
        (dx, dy, dz)
        for dx in (0, 1, -1)
        for dy in (0, 1, -1)
        for dz in (0, 1, -1)
        if (dx, dy, dz) != (0, 0, 0)
    ],
    key=lambda d: (d[1:] != (0, 0), -sum(abs(step) for step in d)),
)


def iota(dim):
    return lax.broadcasted_iota(jnp.int32, (8, 128), dim)


def lane_pos():
    lane = iota(1)
    return lane - GROUP * ((lane * 43) >> 9)


def rot(value, shift, axis=1):
    size = value.shape[axis]
    return pltpu.roll(value, shift % size, axis)


def yz_modes(a, b, next_z):
    low, high = a + b, b - a
    low_next, high_next = next_z(low), next_z(high)
    return (low + low_next, low_next - low, high + high_next, high_next - high)


def x_modes(near, far):
    return [
        [None if m == 0 else n[m] + f[m] for m in range(4)] + [f[m] - n[m] for m in range(4)]
        for n, f in zip(near, far)
    ]


def mode_forces(q, g):
    u, v, w = q
    force = [[None] * 8 for _ in range(3)]
    trace = 1.5 * (u[4] + v[2] + w[1])
    force[0][4] = g * (trace + (u[4] + u[4]))
    force[1][2] = g * (trace + (v[2] + v[2]))
    force[2][1] = g * (trace + (w[1] + w[1]))
    for (ca, ma), (cb, mb) in (((0, 2), (1, 4)), ((1, 1), (2, 2)), ((0, 1), (2, 4))):
        shear = g * (q[ca][ma] + q[cb][mb])
        force[ca][ma] = shear
        force[cb][mb] = shear
    for (ca, ma), (cb, mb) in (((1, 6), (2, 5)), ((0, 6), (2, 3)), ((0, 5), (1, 3))):
        half = 0.5 * (q[ca][ma] + q[cb][mb])
        force[ca][ma] = g * (q[ca][ma] + half)
        force[cb][mb] = g * (q[cb][mb] + half)
    third = g * (1.0 / 3.0)
    total = u[3] + v[5] + w[6]
    force[0][3] = third * (u[3] + total)
    force[1][5] = third * (v[5] + total)
    force[2][6] = third * (w[6] + total)
    last = g * (5.5 / 9.0)
    for c in range(3):
        force[c][7] = last * q[c][7]
    return force


def mode_energy(q):
    u, v, w = q
    trace = u[4] + v[2] + w[1]
    total = 1.5 * (trace * trace) + 2.0 * (u[4] * u[4] + v[2] * v[2] + w[1] * w[1])
    for (ca, ma), (cb, mb) in (((0, 2), (1, 4)), ((1, 1), (2, 2)), ((0, 1), (2, 4))):
        shear = q[ca][ma] + q[cb][mb]
        total = total + shear * shear
    for (ca, ma), (cb, mb) in (((1, 6), (2, 5)), ((0, 6), (2, 3)), ((0, 5), (1, 3))):
        both = q[ca][ma] + q[cb][mb]
        total = total + (q[ca][ma] * q[ca][ma] + q[cb][mb] * q[cb][mb] + 0.5 * (both * both))
    both = u[3] + v[5] + w[6]
    total = total + (1.0 / 3.0) * (u[3] * u[3] + v[5] * v[5] + w[6] * w[6] + both * both)
    last = u[7] * u[7] + v[7] * v[7] + w[7] * w[7]
    return total + (5.5 / 9.0) * last


def node_parts(planes, xs, moduli):
    before, kept = None, None
    for index, plane in enumerate(planes):
        if before is not None:
            force = mode_forces(x_modes(before, plane), moduli(xs[index - 1]))
            right = [[-f[4] if m == 0 else f[m] - f[4 + m] for m in range(4)] for f in force]
            left = [[f[4] if m == 0 else f[m] + f[4 + m] for m in range(4)] for f in force]
            if kept is not None:
                right = [[k + r for k, r in zip(ks, rs)] for ks, rs in zip(kept, right)]
            yield xs[index - 1], right
            kept = left
        before = plane
    yield xs[-1], kept


def node_values(modes, shift_y, shift_z):
    ss, sd, ds, dd = modes
    low = (ss - ds) + shift_y(ss + ds, 0)
    high = (sd - dd) + shift_y(sd + dd, 1)
    return (low - high) + shift_z(low + high)


def body(
    sizes,
    design_in, support_in, load_in, solid_in, void_in, loads_in, start_in,
    disp_out, dsens_out, comp_out,
    dm, um, vm0, vm1, vm2, gm, im, sn, sup, lom, sol, voi, loads, iw, co, fz, img, acc,
    dummy, pa, pz, po, ko, kr, ed, qd, fx, fxd, cy, ar, ar_msg,
    in_sem, out_sem, ssem, rsem, ar_ssem, ar_rsem,
):
    nx, ny, nz = sizes
    count = nx * ny * nz
    me = [lax.axis_index(a) for a in AXES]
    linear = (me[0] * ny + me[1]) * nz + me[2]
    lane, row, pos = iota(1), iota(0), lane_pos()
    pos6 = jnp.where(pos < 6, pos, pos - 6)
    own_rows = pl.ds(8, BY)
    zero = jnp.zeros((8, 128), f32)

    def tile(t):
        return pl.ds(pl.multiple_of(8 * t + 8, 8), 8)

    def brick(t):
        return pl.ds(pl.multiple_of(8 * t, 8), 8)

    copies = [
        pltpu.make_async_copy(src, dst, in_sem.at[i])
        for i, (src, dst) in enumerate(
            (
                (start_in, um.at[:, pl.ds(1, BX), own_rows]),
                (support_in, sup),
                (design_in, dm.at[0, pl.ds(2, BX), own_rows]),
                (solid_in, sol),
                (void_in, voi),
                (load_in, lom),
                (loads_in, loads),
            )
        )
    ]
    def clear_main(*refs):
        def sides(t, carry):
            for ref, xo, slots in refs:
                for c in range(ref.shape[0]):
                    for s in [*range(xo), *range(xo + BX, slots)]:
                        ref[c, s, brick(t)] = zero
            return carry

        def ends(s, carry):
            for ref, xo, _ in refs:
                for c in range(ref.shape[0]):
                    for t in (0, 9):
                        ref[c, xo + s, 8 * t : 8 * t + 8] = zero
            return carry

        lax.fori_loop(0, 10, sides, 0)
        lax.fori_loop(0, BX, ends, 0)

    def clear_edges(k):
        def planes(s, carry):
            for side in range(2):
                for c in range(4):
                    pz[k, side, c, s] = zero
            return carry

        def corners(a, carry):
            for b in range(2):
                for d in range(2):
                    kr[k, a, b, d] = zero
            return carry

        lax.fori_loop(0, NE, planes, 0)
        lax.fori_loop(0, 3, corners, 0)

    clear_main((dm, 2, 8), (um, 1, 7))
    clear_edges(0)

    def exists(d, sign):
        ok = None
        for m, step, size in zip(me, d, sizes):
            if step * sign > 0:
                here = m < size - abs(step)
            elif step * sign < 0:
                here = m >= abs(step)
            else:
                continue
            ok = here if ok is None else ok & here
        return ok

    barrier = pltpu.get_barrier_semaphore()

    greeted = 0
    for d in DIRECTIONS + [(0, 0, 4), (0, 0, -4)]:
        there = exists(d, 1)

        @pl.when(there)
        def _(d=d):
            pl.semaphore_signal(
                barrier,
                inc=1,
                device_id=tuple(m + step for m, step in zip(me, d)),
                device_id_type=MESH,
            )

        greeted = greeted + jnp.where(there, 1, 0)

    for copy in copies:
        copy.start()
    clear_main((sn, 2, 8), (gm, 1, 6), (vm0, 1, 7), (vm1, 1, 7), (im, 1, 7))
    lax.fori_loop(1, pz.shape[0], lambda k, carry: (clear_edges(k), carry)[1], 0)

    def clear_last(s, carry):
        for c in range(3):
            vm1[c, s, 80:88] = zero
        return carry

    lax.fori_loop(0, 7, clear_last, 0)

    def group_mask(t, first, last):
        return (lane >= GROUP * (t + 1) + first) & (lane < GROUP * (t + 1) + last)

    def pack_tiles(tiles, base):
        for t, tile in tiles:
            base = jnp.where(group_mask(t, 0, 6), rot(tile, GROUP * (t + 1) + 3), base)
        return base

    def pack_corners(k, fields):
        comp, total = 0, sum(ref.shape[0] for ref, _ in fields)
        corner = [zero, zero]
        for ref, xo in fields:
            for c in range(ref.shape[0]):
                for x in range(BX):
                    i = 6 * (x * total + comp)
                    for side, t in ((0, 0), (1, 7)):
                        corner[side] = jnp.where(
                            (lane >= i) & (lane < i + 6),
                            rot(ref[c, x + xo, 8 * t + 8 : 8 * t + 16], i + 3),
                            corner[side],
                        )
                comp += 1
        for side in range(2):
            ko[k, side] = corner[side]

    def pack(k, fields):
        comp = 0
        for ref, xo in fields:
            for c in range(ref.shape[0]):
                for x in range(BX):
                    pa[k, comp, x + XE] = pack_tiles(
                        [(t, ref[c, x + xo, 8 * t + 8 : 8 * t + 16]) for t in range(8)], zero
                    )
                comp += 1

    def messages(k, fields):
        comps = sum(f[0].shape[0] for f in fields)
        low, high = max(f[2] for f in fields), max(f[3] for f in fields)
        result = []
        for d in DIRECTIONS:
            dx, dy, dz = d
            if (1 in d and low == 0) or (-1 in d and high == 0):
                continue
            parts = []
            if dz == 0:
                for n, (ref, xo, lo, hi) in enumerate(fields):
                    if (1 in d and lo == 0) or (-1 in d and hi == 0):
                        continue
                    if dx == 1:
                        xs, xd = pl.ds(xo + BX - lo, lo), pl.ds(xo - lo, lo)
                    elif dx == -1:
                        xs, xd = pl.ds(xo, hi), pl.ds(xo + BX, hi)
                    else:
                        xs = xd = pl.ds(xo, BX)
                    if dy == 1:
                        ys, yd = pl.ds(BY, 8), pl.ds(0, 8)
                    elif dy == -1:
                        ys, yd = pl.ds(8, 8), pl.ds(BY + 8, 8)
                    else:
                        ys = yd = own_rows
                    parts.append((n, ref.at[:, xs, ys], ref.at[:, xd, yd]))
            elif dy == 0:
                if dx == 1:
                    xs, xd = pl.ds(XE + BX - low, low), pl.ds(XE - low, low)
                elif dx == -1:
                    xs, xd = pl.ds(XE, high), pl.ds(XE + BX, high)
                else:
                    xs = xd = pl.ds(XE, BX)
                side, cs = 0 if dz == 1 else 1, pl.ds(0, comps)
                parts.append((FACES, pa.at[k, cs, xs], pz.at[k, side, cs, xd]))
            else:
                own = ko.at[k, 0 if dy == -1 else 1]
                there = kr.at[k, 1 - dx, 0 if dy == 1 else 1, 0 if dz == 1 else 1]
                parts.append((CORNERS, own, there))
            for n, src, dst in parts:
                copy = pltpu.make_async_remote_copy(
                    src_ref=src,
                    dst_ref=dst,
                    send_sem=ssem.at[k],
                    recv_sem=rsem.at[k, n],
                    device_id=tuple(m + step for m, step in zip(me, d)),
                    device_id_type=MESH,
                )
                result.append((d, n, copy, math.prod(src.shape) // 128))
        return result

    def send(msgs):
        for d in DIRECTIONS:
            group = [m[2] for m in msgs if m[0] == d]
            if group:
                @pl.when(exists(d, 1))
                def _(group=group):
                    for copy in group:
                        copy.start()

    def wait_rows(msgs, sign, sem):
        kinds = [
            [(False, False)] if size == 1
            else [(False, True), (True, False)] + [(True, True)] * (size > 2)
            for size in sizes
        ]
        totals = set()
        for pattern in itertools.product(*kinds):
            rows = 0
            for d, _, _, n in msgs:
                if all(step == 0 or has[step * sign > 0] for step, has in zip(d, pattern)):
                    rows += n
            totals.add(rows)
        rows = 0
        for d in DIRECTIONS:
            n = sum(m[3] for m in msgs if m[0] == d)
            if n:
                rows = rows + jnp.where(exists(d, sign), n, 0)
        for total in sorted(totals - {0}):
            @pl.when(rows == total)
            def _(total=total):
                part = dummy.at[pl.ds(0, total)]
                pltpu.make_async_copy(part, part, sem).wait()

    def receive(msgs, k):
        for n in sorted({m[1] for m in msgs}):
            wait_rows([m for m in msgs if m[1] == n], -1, rsem.at[k, n])

    def sent(msgs, k):
        wait_rows(msgs, 1, ssem.at[k])

    def plain(msgs, n=None):
        return [m for m in msgs if m[1] < FACES and n in (None, m[1])]

    def packed(msgs, n=None):
        return [m for m in msgs if m[1] >= FACES and n in (None, m[1])]

    def send_all(msgs, k, fields, first=()):
        send(first)
        pack_corners(k, fields)
        send(packed(msgs, CORNERS))
        pack(k, fields)
        send(packed(msgs, FACES))

    def pack_around(ref, xo, first_comp, planes):
        for x in planes:
            for c in range(ref.shape[0]):
                outside = x < 0 or x >= BX
                po[first_comp + c, x + XE] = pack_tiles(
                    [
                        (t, ref[c, x + xo, 8 * t + 8 : 8 * t + 16])
                        for t in (range(-1, 9) if outside else (-1, 8))
                    ],
                    zero,
                )

    def assemble(k, count, first_comp, comps, planes, halo, edge=None):
        items = [(c, x) for x in planes for c in range(count)]
        around = {}
        for _, x in items:
            side = 0 if x < 0 else 2 if x >= BX else 1
            for end in range(2):
                if (side, end) not in around:
                    around[side, end] = jnp.where(pos6 < 3, kr[k, side, end, 0], kr[k, side, end, 1])
        inner = (lane >= GROUP) & (lane < 9 * GROUP)
        for c, x in items:
            comp = first_comp + c
            side = 0 if x < 0 else 2 if x >= BX else 1
            i = 6 * (x % BX * comps + comp)
            value = jnp.where(pos < 3, pz[k, 0, comp, x + XE], pz[k, 1, comp, x + XE])
            value = jnp.where(lane < 6, rot(around[side, 0], -i), value)
            value = jnp.where(group_mask(8, 0, 6), rot(around[side, 1], 9 * GROUP - i), value)
            if halo is not None:
                halo[c, x + XE] = value
            if edge is not None:
                own = po[comp, x + XE]
                if side == 1:
                    own = jnp.where(inner, pa[k, comp, x + XE], own)
                high = rot(jnp.where(pos < 3, value, own), 6)
                low = jnp.where(pos < 3, own, value)
                edge[c, x + XE] = jnp.where(pos < 6, low, high)

    def next_z(value):
        return rot(value, -1)

    def last_z(value):
        return rot(value, 1)

    def main_plane(ref, s, t, shifted=None):
        start = 8 * t + 8
        out = []
        for c in range(3):
            a, b = ref[c, s, tile(t)], ref[c, s, pl.ds(start + 1, 8)]
            if shifted is None:
                out.append(yz_modes(a, b, next_z))
            else:
                an, bn = shifted[c, s, tile(t)], shifted[c, s, pl.ds(start + 1, 8)]
                low, high, low_next, high_next = a + b, b - a, an + bn, bn - an
                out.append((low + low_next, low_next - low, high + high_next, high_next - high))
        return out

    def shift_own(ref):
        def step(t, carry):
            for c in range(3):
                for s in range(1, 1 + BX):
                    fz[c, s, tile(t)] = next_z(ref[c, s, tile(t)])
            return carry

        lax.fori_loop(0, 8, step, 0, unroll=4)

    def shift_halo(ref, high):
        for c in range(3):
            for s in range(BX + 1 + high):
                for t in (-1, 8) if 1 <= s <= BX else range(-1, 9):
                    fz[c, s, tile(t)] = next_z(ref[c, s, tile(t)])

    def edge_plane(edge, x):
        out = []
        for c in range(3):
            a = edge[c, x + XE]
            b = rot(jnp.where(row == 0, rot(a, -GROUP), a), -1, 0)
            out.append(yz_modes(a, b, next_z))
        return out

    def edge_down(value, _):
        down = rot(value, 1, 0)
        return jnp.where(row == 0, rot(down, GROUP), down)

    outer = (lane == 0) | (lane == 127)

    def split(modes):
        ss, sd, ds, dd = modes
        return (ss - ds, sd - dd), (ss + ds, sd + dd)

    def parts_of(ref, t, first, last):
        xs = list(range(first, last + 2))
        return node_parts(
            (main_plane(ref, x + 1, t, fz) for x in xs), xs, lambda e: gm[0, e + 1, tile(t)]
        )

    def apply_inside(ref):
        for c in range(3):
            for x in range(BX):
                for which in range(2):
                    cy[0, c, x + 1, which] = zero

        def step(t, carry):
            for x, modes in parts_of(ref, t, 0, BX - 2):
                for c in range(3):
                    here, after = split(modes[c])
                    both = []
                    for which in range(2):
                        down = rot(after[which], 1, 0)
                        both.append(
                            here[which] + jnp.where(row == 0, cy[0, c, x + 1, which], down)
                        )
                        cy[0, c, x + 1, which] = down
                    img[c, x, brick(t)] = (both[0] - both[1]) + last_z(both[0] + both[1])
            return carry

        lax.fori_loop(0, 7, step, 0)

    def apply_rest(ref, edge, planes, tiles, use, use_edge=None):
        last = planes[-1]
        nodes = list(range(-1, last + 2))
        for x, modes in node_parts(
            (edge_plane(edge, x) for x in nodes), nodes, lambda e: ed[4, 0, e + XE]
        ):
            if x not in planes:
                continue
            for c in range(3):
                value = node_values(modes[c], edge_down, last_z)
                fx[c, x + XE] = jnp.where(pos == 3, rot(value, -6), value)
                if use_edge is not None:
                    use_edge(x, c, value)

        def emit(x, t, modes, inside, before):
            for c in range(3):
                both = []
                for which in range(2):
                    value, down = None, None
                    if modes is not None:
                        here, after = split(modes[c])
                        value, down = here[which], rot(after[which], 1, 0)
                    below = before(c, x, which)
                    if below is not None:
                        enter = jnp.where(row == 0, below, zero if down is None else down)
                    else:
                        enter = down
                    if enter is not None:
                        value = enter if value is None else value + enter
                    if down is not None:
                        cy[1, c, x + 1, which] = down
                    both.append(value)
                total = None
                if both[0] is not None:
                    total = (both[0] - both[1]) + last_z(both[0] + both[1])
                if inside:
                    partial = img[c, x, brick(t)]
                    total = partial if total is None else total + partial
                fixed = rot(fx[c, x + XE], lax.rem(254 - GROUP * (t + 1) - 1, 128))
                use(x, c, t, jnp.where(outer, fixed, total))

        groups = [(-1, -1), (BX - 1, last)]
        bound = [0] + list(range(BX - 1, last + 1))

        def edge_step(t, before):
            done = []
            for group in groups:
                for x, modes in parts_of(ref, t, *group):
                    if x in planes:
                        emit(x, t, modes, x < BX, before)
                        done.append(x)
            for x in planes:
                if x not in done:
                    emit(x, t, None, True, before)
            use(None, None, t, None)

        def full_step(t, before):
            for x, modes in parts_of(ref, t, -1, last):
                if x in planes:
                    emit(x, t, modes, False, before)
            use(None, None, t, None)

        for x, modes in parts_of(ref, -1, -1, last):
            if x in planes:
                for c in range(3):
                    after = split(modes[c])[1]
                    for which in range(2):
                        cy[1, c, x + 1, which] = rot(after[which], 1, 0)
        edge_step(0, lambda c, x, which: cy[1, c, x + 1, which])

        def chain(c, x, which):
            return cy[1, c, x + 1, which] if x in bound else None

        lax.fori_loop(1, 7, lambda t, carry: (edge_step(t, chain), carry)[1], 0, unroll=3)

        def join(c, x, which):
            value = cy[1, c, x + 1, which] if x in bound else None
            if x < BX:
                own = cy[0, c, x + 1, which]
                value = own if value is None else value + own
            return value

        full_step(7, join)
        for t in range(8, tiles):
            full_step(t, lambda c, x, which: cy[1, c, x + 1, which])

    weights = {}
    for a in range(3):
        for b in range(3):
            for c in range(3):
                weights[a, b, c] = max(0.0, 3.0 - math.sqrt(a * a + b * b + c * c))

    def combine_xy(planes, x):
        far = []
        for b in range(3):
            far.append(
                [
                    planes[x + 2][b],
                    planes[x + 1][b] + planes[x + 3][b],
                    planes[x][b] + planes[x + 4][b],
                ]
            )
        pair = {
            (0, 0): far[0][0],
            (0, 1): far[0][1] + far[1][0],
            (1, 1): far[1][1],
            (0, 2): far[0][2] + far[2][0],
            (1, 2): far[1][2] + far[2][1],
            (2, 2): far[2][2],
        }
        out = []
        for c in range(3):
            value = None
            for (a, b), term in pair.items():
                if weights[a, b, c] > 0.0:
                    term = weights[a, b, c] * term
                    value = term if value is None else value + term
            out.append(value)
        return out

    def filter_field(ref, halo, use):
        planes = []
        for s in range(8):
            value = halo[0, s]
            up, down = rot(value, -GROUP), rot(value, GROUP)
            one = rot(jnp.where(row == 0, up, value), -1, 0) + rot(
                jnp.where(row == 7, down, value), 1, 0
            )
            two = rot(jnp.where(row <= 1, up, value), -2, 0) + rot(
                jnp.where(row >= 6, down, value), 2, 0
            )
            planes.append((value, one, two))
        for x in range(BX):
            _, fx[1, x], fx[2, x] = combine_xy(planes, x)

        def step(t, carry):
            planes = []
            for s in range(8):
                rows = [ref[0, s, pl.ds(8 * t + 8 + off, 8)] for off in (-2, -1, 1, 2)]
                planes.append((ref[0, s, tile(t)], rows[1] + rows[2], rows[0] + rows[3]))
            shift = lax.rem(256 - GROUP * (t + 1) - 3, 128)
            for x in range(BX):
                value, one, two = combine_xy(planes, x)
                side = rot(fx[1, x], shift)
                value = value + rot(jnp.where(lane < 1, side, one), -1)
                value = value + rot(jnp.where(lane >= 127, side, one), 1)
                side = rot(fx[2, x], shift)
                value = value + rot(jnp.where(lane < 2, side, two), -2)
                value = value + rot(jnp.where(lane >= 126, side, two), 2)
                use(x, t, value)
            return carry

        lax.fori_loop(0, 8, step, 0, unroll=4)

    def reduce_start(k, value):
        ar_msg[k] = value
        ar[k, linear] = value

        steps = [
            (ox, oy, oz)
            for ox in range(nx)
            for oy in range(ny)
            for oz in range(nz)
            if (ox, oy, oz) != (0, 0, 0)
        ]
        steps.sort(key=lambda o: -sum(min(step, size - step) for step, size in zip(o, sizes)))
        for o in steps:
            pltpu.make_async_remote_copy(
                src_ref=ar_msg.at[k],
                dst_ref=ar.at[k, linear],
                send_sem=ar_ssem.at[k],
                recv_sem=ar_rsem.at[k],
                device_id=tuple(
                    lax.rem(m + step, size) if step else m for m, step, size in zip(me, o, sizes)
                ),
                device_id_type=MESH,
            ).start()

    def reduce_wait(k, sem):
        part = ar.at[k, pl.ds(0, count - 1)]
        pltpu.make_async_copy(part, part, sem.at[k]).wait()

    def reduce_total(k):
        reduce_wait(k, ar_rsem)
        return jnp.sum(ar[k], axis=0)


    copies[0].wait()
    copies[1].wait()
    for c in range(3):
        um[c, 1 : 1 + BX, 8 : 8 + BY] = um[c, 1 : 1 + BX, 8 : 8 + BY] * (1 - sup[...]).astype(f32)
    copies[2].wait()
    pack_corners(0, [(dm, 2), (um, 1)])
    pack(0, [(dm, 2), (um, 1)])
    pl.semaphore_wait(barrier, greeted)
    first = messages(0, [(dm, 2, 2, 2), (um, 1, 1, 1)])
    send(packed(first))
    send(plain(first, 0))
    send(plain(first, 1))
    shift_own(um)

    def inside(coord, size):
        return ((coord >= 0) & (coord < size)).astype(f32)

    z_at = me[2] * BZ + lane
    z_terms = [
        jnp.ones((8, 128), f32),
        inside(z_at - 1, nz * BZ) + inside(z_at + 1, nz * BZ),
        inside(z_at - 2, nz * BZ) + inside(z_at + 2, nz * BZ),
    ]
    x_rows = []
    for x in range(BX):
        x_at = me[0] * BX + x
        x_terms = [
            f32(1.0),
            inside(x_at - 1, nx * BX) + inside(x_at + 1, nx * BX),
            inside(x_at - 2, nx * BX) + inside(x_at + 2, nx * BX),
        ]
        per_b = []
        for b in range(3):
            value = zero
            for c in range(3):
                value = value + z_terms[c] * sum(x_terms[a] * weights[a, b, c] for a in range(3))
            per_b.append(value)
        x_rows.append(per_b)

    def weigh(t, carry):
        y_at = me[1] * BY + 8 * t + row
        one = inside(y_at - 1, ny * BY) + inside(y_at + 1, ny * BY)
        two = inside(y_at - 2, ny * BY) + inside(y_at + 2, ny * BY)
        for x in range(BX):
            iw[x, brick(t)] = 1.0 / (x_rows[x][0] + one * x_rows[x][1] + two * x_rows[x][2])
        return carry

    lax.fori_loop(0, 8, weigh, 0, unroll=4)
    for copy in copies[3:]:
        copy.wait()

    receive(packed(first), 0)
    receive(plain(first, 0), 0)
    assemble(0, 1, 0, 4, range(-2, 6), qd)

    def to_modulus(x, t, total):
        at = brick(t)
        scale = iw[x, at]
        solid, void = sol[x, at] > 0, voi[x, at] > 0
        physical = jnp.where(solid, 1.0, jnp.where(void, 0.0, total * scale))
        square = physical * physical
        gm[0, 1 + x, tile(t)] = MU16 * EMIN + (MU16 * (1.0 - EMIN)) * (square * physical)
        co[x, at] = jnp.where(
            solid | void, 0.0, (-PENALTY * (1.0 - EMIN) * MU16) * (square * scale)
        )

    filter_field(dm, qd, to_modulus)
    second = messages(1, [(gm, 1, 1, 1)])
    send_all(second, 1, [(gm, 1)], plain(second))
    apply_inside(um)
    receive(plain(first, 1), 0)
    pack_around(um, 1, 1, range(-1, 5))
    assemble(0, 3, 1, 4, range(-1, 5), None, ed.at[0])
    shift_halo(um, 1)
    receive(plain(second), 1)
    pack_around(gm, 1, 0, range(-1, 5))
    receive(packed(second), 1)
    assemble(1, 1, 0, 1, range(-1, 5), None, ed.at[4])

    for x in range(BX):
        value = ed[4, 0, x + XE] + ed[4, 0, x + XE - 1]
        value = value + edge_down(value, 0)
        fxd[x] = value + last_z(value)

    def diagonal(t, carry):
        for x in range(BX):
            value = None
            for s in (x, x + 1):
                term = gm[0, s, tile(t)] + gm[0, s, pl.ds(8 * t + 7, 8)]
                value = term if value is None else value + term
            value = value + last_z(value)
            fixed = rot(fxd[x], lax.rem(256 - GROUP * (t + 1) - 9, 128))
            value = jnp.where(lane == 0, fixed, value)
            free = (1 - sup[x, brick(t)]).astype(f32)
            im[0, 1 + x, tile(t)] = free / (DIAG * value)
        return carry

    lax.fori_loop(0, 8, diagonal, 0, unroll=4)

    sums = {}
    acc_names = ("b0", "a00", "a01", "a11", "a12", "a22", "energy")
    for n, name in enumerate(acc_names):
        acc[n] = zero
        sums[name] = acc.at[n]

    def add(name, value):
        sums[name][...] = sums[name][...] + value

    kept = []

    def keep(name, value):
        kept.append((name, value))

    def flush():
        totals = {}
        for name, value in kept:
            totals[name] = value if name not in totals else totals[name] + value
        for name, value in totals.items():
            add(name, value)
        kept.clear()

    def from_start(x, c, t, image):
        if x is None:
            return flush()
        at = brick(t)
        free = (1 - sup[x, at]).astype(f32)
        load = lom[x, at].astype(f32)
        left = free * (load * loads[c, x, at] - image)
        value = im[0, 1 + x, tile(t)] * left
        vm0[c, 1 + x, tile(t)] = value
        keep("b0", left * value)

    def from_vector(source, target, diag_name, next_name):
        def use(x, c, t, image):
            if x is None:
                return flush()
            here = source[c, 1 + x, tile(t)]
            value = im[0, 1 + x, tile(t)] * image - THETA * here
            target[c, 1 + x, tile(t)] = value
            if x < BX and not (isinstance(t, int) and t >= 8):
                keep(diag_name, here * image)
                keep(next_name, value * image)

        return use

    own = list(range(BX))
    third = messages(2, [(vm0, 1, 1, 1), (im, 1, 0, 1)])
    send(plain(third, 1))
    apply_rest(um, ed.at[0], own, 8, from_start)
    send_all(third, 2, [(vm0, 1), (im, 1)], plain(third, 0))
    shift_own(vm0)
    apply_inside(vm0)
    receive(plain(third), 2)
    pack_around(vm0, 1, 0, range(-1, 5))
    pack_around(im, 1, 3, range(0, 5))
    shift_halo(vm0, 1)
    receive(packed(third), 2)
    assemble(2, 3, 0, 4, range(-1, 5), None, ed.at[1])
    assemble(2, 1, 3, 4, range(0, 5), None, ed.at[5])
    apply_rest(vm0, ed.at[1], own, 8, from_vector(vm0, vm1, "a00", "a01"))
    fourth = messages(3, [(vm1, 1, 1, 2)])
    send_all(fourth, 3, [(vm1, 1)], plain(fourth))
    shift_own(vm1)
    apply_inside(vm1)
    receive(plain(fourth), 3)
    pack_around(vm1, 1, 0, range(-1, 6))
    shift_halo(vm1, 2)
    receive(packed(fourth), 3)
    assemble(3, 3, 0, 3, range(-1, 6), None, ed.at[2])

    def edge_vector(x, c, image):
        ed[3, c, x + XE] = ed[5, 0, x + XE] * image - THETA * ed[2, c, x + XE]

    apply_rest(
        vm1, ed.at[2], own + [BX], 9, from_vector(vm1, vm2, "a11", "a12"), edge_vector
    )

    def energies(planes):
        before = None
        for index, plane in enumerate(planes):
            if before is not None:
                yield index - 1, mode_energy(x_modes(before, plane))
            before = plane

    column = (pos == 2) & (lane >= GROUP) & (lane < 9 * GROUP)

    edge_sum = zero
    for x, value in energies(edge_plane(ed.at[3], x) for x in range(BX + 1)):
        edge_sum = edge_sum + jnp.where(column, ed[4, 0, x + XE] * value, 0.0)

    def last_moment(t, carry):
        total = zero
        for x, value in energies(main_plane(vm2, x + 1, t) for x in range(BX + 1)):
            total = total + gm[0, 1 + x, tile(t)] * value
        add("a22", jnp.where(lane < 127, total, 0.0))
        return carry

    add("a22", edge_sum)
    lax.fori_loop(0, 8, last_moment, 0, unroll=4)

    message = jnp.zeros((1, 128), f32)
    lane1 = lax.broadcasted_iota(jnp.int32, (1, 128), 1)
    for n, name in enumerate(acc_names[:6]):
        part = jnp.sum(jnp.sum(sums[name][...], axis=0, keepdims=True), axis=1, keepdims=True)
        message = jnp.where(lane1 == n, part, message)
    reduce_start(0, message)
    for k, msgs in enumerate((first, second, third, fourth)):
        sent(msgs, k)
    totals = reduce_total(0)
    b0, a00, a01, a11, a12, a22 = (
        jnp.broadcast_to(totals[:, n : n + 1], (1, 128)) for n in range(6)
    )
    tiny = 1e-6
    b1 = a00 - THETA * b0
    b2 = a01 - THETA * b1
    l10, l20 = a01 / a00, a11 / a00
    d1 = a11 - l10 * a01
    ok1 = d1 > tiny * a11
    safe1 = jnp.where(ok1, d1, 1.0)
    cross = a12 - l20 * a01
    l21 = jnp.where(ok1, cross / safe1, 0.0)
    d2 = a22 - l20 * a11 - l21 * cross
    ok2 = ok1 & (d2 > tiny * a22)
    y1 = b1 - l10 * b0
    y2 = b2 - l20 * b0 - l21 * y1
    c2 = jnp.where(ok2, y2 / jnp.where(ok2, d2, 1.0), 0.0)
    c1 = jnp.where(ok1, y1 / safe1, 0.0) - l21 * c2
    c0 = b0 / a00 - l10 * c1 - l20 * c2
    c0, c1, c2 = (jnp.broadcast_to(c, (8, 128)) for c in (c0, c1, c2))

    for c in range(3):
        for x in range(BX + 1):
            s = x + XE
            ed[0, c, s] = ed[0, c, s] + (
                c0 * ed[1, c, s] + c1 * ed[2, c, s] + c2 * ed[3, c, s]
            )

    def combine(t, carry):
        for c in range(3):
            for s in range(1, BX + 2):
                at = brick(t + 1)
                um[c, s, at] = um[c, s, at] + (
                    c0 * vm0[c, s, at] + c1 * vm1[c, s, at] + c2 * vm2[c, s, at]
                )
        return carry

    lax.fori_loop(0, 9, combine, 0)
    disp = pltpu.make_async_copy(um.at[:, pl.ds(1, BX), own_rows], disp_out, out_sem.at[0])
    disp.start()

    for x, value in energies(edge_plane(ed.at[0], x) for x in range(BX + 1)):
        fxd[x] = value

    def sensitivity(t, carry):
        total = zero
        for x, value in energies(main_plane(um, x + 1, t) for x in range(BX + 1)):
            fixed = rot(fxd[x], lax.rem(253 - GROUP * (t + 1), 128))
            value = jnp.where(lane == 127, fixed, value)
            total = total + gm[0, 1 + x, tile(t)] * value
            sn[0, 2 + x, tile(t)] = co[x, brick(t)] * value
        add("energy", total)
        return carry

    lax.fori_loop(0, 8, sensitivity, 0, unroll=4)
    fifth = messages(4, [(sn, 2, 2, 2)])
    send(plain(fifth))
    part = jnp.sum(jnp.sum(sums["energy"][...], axis=0, keepdims=True), axis=1, keepdims=True)
    reduce_start(1, jnp.broadcast_to(part, (1, 128)))
    send_all(fifth, 4, [(sn, 2)])
    receive(fifth, 4)
    assemble(4, 1, 0, 1, range(-2, 6), qd)

    def finish(x, t, total):
        dsens_out[x, brick(t)] = total

    filter_field(sn, qd, finish)
    comp_out[...] = reduce_total(1)
    sent(fifth, 4)
    for k in range(2):
        reduce_wait(k, ar_ssem)
    disp.wait()


def call(sizes, *args):
    count = sizes[0] * sizes[1] * sizes[2]
    main3 = pltpu.VMEM((3, 7, 88, 128), f32)
    wide = pltpu.VMEM((1, 8, 80, 128), f32)
    brick = pltpu.VMEM((BX, BY, BZ), f32)
    mask = pltpu.VMEM((BX, BY, BZ), jnp.int32)
    any_spec = pl.BlockSpec(memory_space=pl.ANY)
    displacement, sensitivity, compliance = pl.pallas_call(
        functools.partial(body, sizes),
        out_shape=(
            pltpu.VMEM((3, BX, BY, BZ), f32),
            pltpu.VMEM((BX, BY, BZ), f32),
            jax.ShapeDtypeStruct((1, 128), f32),
        ),
        in_specs=[any_spec] * 7,
        out_specs=(pl.BlockSpec(memory_space=pltpu.VMEM),) * 3,
        scratch_shapes=[
            wide, main3, main3, main3, main3, pltpu.VMEM((1, 6, 80, 128), f32),
            pltpu.VMEM((1, 7, 80, 128), f32), wide,
            mask, mask, mask, mask, pltpu.VMEM((3, BX, BY, BZ), f32),
            brick, brick, main3, pltpu.VMEM((3, BX, BY, BZ), f32), pltpu.VMEM((8, 8, 128), f32),
            pltpu.VMEM((4096, 128), f32),
            pltpu.VMEM((5, 4, NE, 8, 128), f32),
            pltpu.VMEM((5, 2, 4, NE, 8, 128), f32),
            pltpu.VMEM((4, NE, 8, 128), f32),
            pltpu.VMEM((5, 2, 8, 128), f32),
            pltpu.VMEM((5, 3, 2, 2, 8, 128), f32),
            pltpu.VMEM((6, 3, NE, 8, 128), f32),
            pltpu.VMEM((1, NE, 8, 128), f32),
            pltpu.VMEM((3, NE, 8, 128), f32),
            pltpu.VMEM((BX, 8, 128), f32),
            pltpu.VMEM((2, 3, 7, 2, 8, 128), f32),
            pltpu.VMEM((2, count, 1, 128), f32),
            pltpu.VMEM((2, 1, 128), f32),
            pltpu.SemaphoreType.DMA((7,)),
            pltpu.SemaphoreType.DMA((1,)),
            pltpu.SemaphoreType.DMA((5,)),
            pltpu.SemaphoreType.DMA((5, 4)),
            pltpu.SemaphoreType.DMA((2,)),
            pltpu.SemaphoreType.DMA((2,)),
        ],
        compiler_params=pltpu.CompilerParams(
            collective_id=0, has_side_effects=True, vmem_limit_bytes=60 * 2**20
        ),
    )(*args)
    return displacement, sensitivity, compliance[0, 0]


def solution(mesh):
    sizes = tuple(mesh.shape[axis] for axis in AXES)
    block, field = P("gx", "gy", "gz"), P(None, "gx", "gy", "gz")
    return jax.shard_map(
        functools.partial(call, sizes),
        mesh=mesh,
        in_specs=(block,) * 5 + (field,) * 2,
        out_specs=(field, block, P()),
        check_vma=False,
    )
```
